32 devices in a mesh: dp: 8 (over y, x, core), ctx: 4 (over z).
Axes of the slice: x: 2, y: 2, z: 4, core: 2. Of those that a mesh axis runs over, the one named last changes fastest.
Arguments:
- tokens_in: bfloat16 [2, 8, 1024, 1024], P(None, 'dp', 'ctx'), may hold values from -6 to 6
- seq_lengths: int32 [2, 8, 4], P(None, 'dp'), may hold values from 0 to 1024, as said below
- norm_linear: bfloat16 [1024], P(('dp', 'ctx')), may hold values from 0.25 to 1.75
- proj_qk: bfloat16 [1024, 512], P(('dp', 'ctx')), may hold values from -0.1875 to 0.1875
- proj_values: bfloat16 [1024, 1024], P(('dp', 'ctx')), may hold values from -0.1875 to 0.1875
- conv_taps: bfloat16 [1024, 3], P(('dp', 'ctx')), may hold values from -3.5 to 3.5
- out_linear: bfloat16 [1024, 1024], P(('dp', 'ctx')), may hold values from -3 to 3
- norm_ffn_one: bfloat16 [1024], P(('dp', 'ctx')), may hold values from 0.25 to 1.75
- gate_up_one: bfloat16 [1024, 5632], P(('dp', 'ctx')), may hold values from -0.1875 to 0.1875
- down_one: bfloat16 [2816, 1024], P(('dp', 'ctx')), may hold values from -0.109375 to 0.109375
- norm_window: bfloat16 [1024], P(('dp', 'ctx')), may hold values from 0.25 to 1.75
- proj_qkv: bfloat16 [1024, 3072], P(('dp', 'ctx')), may hold values from -0.1875 to 0.1875
- out_window: bfloat16 [1024, 1024], P(('dp', 'ctx')), may hold values from -1 to 1
- norm_ffn_two: bfloat16 [1024], P(('dp', 'ctx')), may hold values from 0.25 to 1.75
- gate_up_two: bfloat16 [1024, 5632], P(('dp', 'ctx')), may hold values from -0.1875 to 0.1875
- down_two: bfloat16 [2816, 1024], P(('dp', 'ctx')), may hold values from -0.109375 to 0.109375
- cotangent: bfloat16 [2, 8, 1024, 1024], P(None, 'dp', 'ctx'), may hold values from -6 to 6
Outputs:
- output: bfloat16 [2, 8, 1024, 1024], P(None, 'dp', 'ctx')
- tokens_grad: bfloat16 [2, 8, 1024, 1024], P(None, 'dp', 'ctx')
- grad_norm_linear: float32 [1024], P(('dp', 'ctx'))
- grad_proj_qk: float32 [1024, 512], P(('dp', 'ctx'))
- grad_proj_values: float32 [1024, 1024], P(('dp', 'ctx'))
- grad_conv_taps: float32 [1024, 3], P(('dp', 'ctx'))
- grad_out_linear: float32 [1024, 1024], P(('dp', 'ctx'))
- grad_norm_ffn_one: float32 [1024], P(('dp', 'ctx'))
- grad_gate_up_one: float32 [1024, 5632], P(('dp', 'ctx'))
- grad_down_one: float32 [2816, 1024], P(('dp', 'ctx'))
- grad_norm_window: float32 [1024], P(('dp', 'ctx'))
- grad_proj_qkv: float32 [1024, 3072], P(('dp', 'ctx'))
- grad_out_window: float32 [1024, 1024], P(('dp', 'ctx'))
- grad_norm_ffn_two: float32 [1024], P(('dp', 'ctx'))
- grad_gate_up_two: float32 [1024, 5632], P(('dp', 'ctx'))
- grad_down_two: float32 [2816, 1024], P(('dp', 'ctx'))
The draws below stay inside these ranges and needn't reach their ends.
Inputs may be any that keep to these rules, and one draw needn't show every extreme that they name: `seq_lengths`: for each slot exactly one of the 2 micro-batches holds a single sequence of 1024 tokens there (its other entries zero); in the other micro-batches the first 3 entries lie between 128 and 307 and the last is zero. Tokens after the sum of a slot's lengths are padding.
All inputs are finite; a program needn't handle non-finite values.
Results may differ from the reference program's by a relative error of at most 0.014.
Values may be sent and summed in bfloat16 or wider, within the bound.
A program may use at most 384 MiB of HBM per device.

```python
import math
import jax
import jax.numpy as jnp
from jax import lax

D = 1024
FF = 2816
HEADS = 16
FEAT = 16
WINDOW = 64
CONV = 3
MICRO = 2
SEQS = 4
SLOT_LEN = 1024
HDIM = 64
SLOTS = 8


def draw_seq_lengths(key, part):
    key = jax.random.fold_in(key, 7)
    ragged_key = jax.random.fold_in(key, 1)
    pick_key = jax.random.fold_in(key, 2)
    ragged = jax.random.randint(ragged_key, (MICRO, SLOTS, SEQS - 1), SLOT_LEN // 8, 3 * SLOT_LEN // 10 + 1, dtype=jnp.int32)
    ragged = jnp.concatenate([ragged, jnp.zeros((MICRO, SLOTS, 1), jnp.int32)], axis=2)
    full_slot = jnp.zeros((MICRO, SLOTS, SEQS), jnp.int32).at[:, :, 0].set(SLOT_LEN)
    chosen = jax.random.randint(pick_key, (SLOTS,), 0, MICRO, dtype=jnp.int32)
    takes_full = (jnp.arange(MICRO, dtype=jnp.int32)[:, None] == chosen[None, :])[:, :, None]
    return jnp.where(takes_full, full_slot, ragged)


def shard_levels(stream_key, shape, pieces, low, largest):
    gain = 1.0
    for axis_at, shards_of in pieces:
        steps = jax.random.uniform(jax.random.fold_in(jax.random.fold_in(stream_key, 6), axis_at), (shards_of,), jnp.float32, low / len(pieces), largest / len(pieces))
        gain = gain * jnp.repeat(jnp.exp(steps), shape[axis_at] // shards_of).reshape((-1,) + (1,) * (len(shape) - 1 - axis_at))
    return gain


def noise(rng, dims, width, bound, split=(), held_as=jnp.bfloat16):
    values = jax.random.normal(rng, dims, jnp.float32) * width
    if len(split) > 0:
        values = shard_levels(rng, dims, split, -0.22, 0.18) * values
    return jnp.clip(values, min=-bound, max=bound).astype(held_as)


def setup_inputs(seed: int = 0) -> dict:
    key_of = jax.random.split(jax.random.key(seed), 18)
    tokens_in = noise(key_of[0], (MICRO, SLOTS, SLOT_LEN, D), 1.0, 6.0, ((1, 8), (2, 4)))
    seq_lengths = draw_seq_lengths(jax.random.fold_in(key_of[17], 71), 0)
    norm_linear = jnp.clip(1.0 + 0.15 * jax.random.normal(key_of[2], (D,), jnp.float32), 0.25, 1.75).astype(jnp.bfloat16)
    proj_qk = noise(key_of[3], (D, 2 * HEADS * FEAT), D ** -0.5, 0.1875, ((0, 32),))
    proj_values = noise(key_of[4], (D, D), D ** -0.5, 0.1875, ((0, 32),))
    conv_taps = noise(key_of[5], (D, CONV), CONV ** -0.5, 3.5, ((0, 32),))
    out_linear = noise(key_of[6], (D, D), (max(D // 256, 2)) ** -0.5, 3.0, ((0, 32),))
    norm_ffn_one = jnp.clip(1.0 + 0.15 * jax.random.normal(key_of[7], (D,), jnp.float32), 0.25, 1.75).astype(jnp.bfloat16)
    gate_up_one = noise(key_of[8], (D, 2 * FF), D ** -0.5, 0.1875, ((0, 32),))
    down_one = noise(key_of[9], (FF, D), FF ** -0.5, 0.109375, ((0, 32),))
    norm_window = jnp.clip(1.0 + 0.15 * jax.random.normal(key_of[10], (D,), jnp.float32), 0.25, 1.75).astype(jnp.bfloat16)
    proj_qkv = noise(key_of[11], (D, 3 * D), D ** -0.5, 0.1875, ((0, 32),))
    out_window = noise(key_of[12], (D, D), (D // 32) ** -0.5, 1.0, ((0, 32),))
    norm_ffn_two = jnp.clip(1.0 + 0.15 * jax.random.normal(key_of[13], (D,), jnp.float32), 0.25, 1.75).astype(jnp.bfloat16)
    gate_up_two = noise(key_of[14], (D, 2 * FF), D ** -0.5, 0.1875, ((0, 32),))
    down_two = noise(key_of[15], (FF, D), FF ** -0.5, 0.109375, ((0, 32),))
    cotangent = noise(key_of[16], (MICRO, SLOTS, SLOT_LEN, D), 1.0, 6.0, ((1, 8), (2, 4)))
    return {"tokens_in": tokens_in, "seq_lengths": seq_lengths, "norm_linear": norm_linear, "proj_qk": proj_qk, "proj_values": proj_values, "conv_taps": conv_taps, "out_linear": out_linear, "norm_ffn_one": norm_ffn_one, "gate_up_one": gate_up_one, "down_one": down_one, "norm_window": norm_window, "proj_qkv": proj_qkv, "out_window": out_window, "norm_ffn_two": norm_ffn_two, "gate_up_two": gate_up_two, "down_two": down_two, "cotangent": cotangent}


epsilon = 1e-05
masked_fill = -1e+30
highest = lax.Precision.HIGHEST

@jax.custom_vjp
def low(v):
    return lax.optimization_barrier(v.astype(jnp.bfloat16)).astype(jnp.float32)

@jax.custom_vjp
def low_back(v):
    return v

def low_keep(v):
    return (low(v), None)

def low_pass(kept, grad):
    return (grad,)

def back_keep(v):
    return (v, None)

def back_low(kept, grad):
    return (low(grad),)
low.defvjp(low_keep, low_pass)
low_back.defvjp(back_keep, back_low)

def product(operand, weight):
    return jnp.dot(operand, weight, precision=highest)

def normed(stream, scale_gain):
    return stream * lax.rsqrt(lax.optimization_barrier(jnp.mean(stream * stream, axis=-1, keepdims=True)) + epsilon) * scale_gain

def segments(lengths_row):
    seq_ends = jnp.cumsum(lengths_row, dtype=jnp.int32)
    places = jnp.arange(SLOT_LEN, dtype=jnp.int32)
    segment = lax.optimization_barrier(jnp.sum((places[:, None] >= seq_ends[None, :]).astype(jnp.int32), axis=1, dtype=jnp.int32))
    valid_rows = (places < seq_ends[-1]).astype(jnp.float32)
    return (segment, valid_rows)

def linear_mixer(stream, segment, norm_gain, qk_weight, value_weight, tap_weights, out_weight):
    normed_rows = low(normed(stream, norm_gain))
    qk_rows = low(low_back(product(normed_rows, qk_weight)))
    pre_values = low_back(product(normed_rows, value_weight))
    half_cols = HEADS * FEAT
    query_rows = qk_rows[:, :half_cols].reshape(SLOT_LEN, HEADS, FEAT)
    key_rows = qk_rows[:, half_cols:].reshape(SLOT_LEN, HEADS, FEAT)
    conv_sum = jnp.zeros_like(pre_values)
    for offset in range(CONV):
        shifted = jnp.concatenate([jnp.zeros((offset, D), jnp.float32), pre_values[:SLOT_LEN - offset]], axis=0)
        shifted_seg = jnp.concatenate([jnp.full((offset,), -1, jnp.int32), segment[:SLOT_LEN - offset]], axis=0)
        same_seg = (shifted_seg == segment).astype(jnp.float32)
        conv_sum = conv_sum + tap_weights[:, offset] * shifted * same_seg[:, None]
    value_rows = low(conv_sum * jax.nn.silu(pre_values)).reshape(SLOT_LEN, HEADS, HDIM)
    scores = jnp.einsum('ihf,jhf->hij', query_rows, key_rows, precision=highest) / math.sqrt(FEAT)
    places = jnp.arange(SLOT_LEN, dtype=jnp.int32)
    causal = ((places[:, None] >= places[None, :]) & (segment[:, None] == segment[None, :])).astype(jnp.float32)
    weights = (1.0 + scores + 0.5 * scores * scores) * causal[None]
    numerator = jnp.einsum('hij,jhe->ihe', weights, value_rows, precision=highest)
    denominator = jnp.transpose(lax.optimization_barrier(jnp.sum(weights, axis=-1)))
    attended = low((numerator / denominator[:, :, None]).reshape(SLOT_LEN, D))
    return low_back(product(attended, out_weight))

def window_mixer(stream, segment, norm_gain, qkv_weight, out_weight):
    normed_rows = low(normed(stream, norm_gain))
    qkv_rows = low(low_back(product(normed_rows, qkv_weight)))
    query_rows = qkv_rows[:, :D].reshape(SLOT_LEN, HEADS, HDIM)
    key_rows = qkv_rows[:, D:2 * D].reshape(SLOT_LEN, HEADS, HDIM)
    value_rows = qkv_rows[:, 2 * D:].reshape(SLOT_LEN, HEADS, HDIM)
    scores = low_back(jnp.einsum('ihe,jhe->hij', query_rows, key_rows, precision=highest) * HDIM ** (-0.5))
    places = jnp.arange(SLOT_LEN, dtype=jnp.int32)
    visible = (places[:, None] >= places[None, :]) & (places[:, None] - places[None, :] < WINDOW)
    visible = visible & (segment[:, None] == segment[None, :])
    scores = jnp.where(visible[None], scores, masked_fill)
    probabilities = low(jax.nn.softmax(scores, axis=-1))
    attended = low(low_back(jnp.einsum('hij,jhe->ihe', probabilities, value_rows, precision=highest)))
    return low_back(product(attended.reshape(SLOT_LEN, D), out_weight))

def feed_forward(stream, norm_gain, gate_up, down_weight):
    normed_rows = low(normed(stream, norm_gain))
    projected = low_back(product(normed_rows, gate_up))
    hidden = low(jax.nn.silu(projected[:, :FF]) * projected[:, FF:])
    return low_back(product(hidden, down_weight))

def two_layers(stream, segment, valid_rows, params):
    middle = stream + linear_mixer(stream, segment, params[0], params[1], params[2], params[3], params[4])
    first_out = middle + feed_forward(middle, params[5], params[6], params[7])
    second_mid = first_out + window_mixer(first_out, segment, params[8], params[9], params[10])
    closing = second_mid + feed_forward(second_mid, params[11], params[12], params[13])
    return closing * valid_rows[:, None]

def reference(tokens_in, seq_lengths, norm_linear, proj_qk, proj_values, conv_taps, out_linear, norm_ffn_one, gate_up_one, down_one, norm_window, proj_qkv, out_window, norm_ffn_two, gate_up_two, down_two, cotangent):
    params = tuple((weight.astype(jnp.float32) for weight in (norm_linear, proj_qk, proj_values, conv_taps, out_linear, norm_ffn_one, gate_up_one, down_one, norm_window, proj_qkv, out_window, norm_ffn_two, gate_up_two, down_two)))
    slot_rows = tokens_in.astype(jnp.float32).reshape(MICRO * SLOTS, SLOT_LEN, D)
    slot_lengths = seq_lengths.reshape(MICRO * SLOTS, SEQS)
    slot_cot = cotangent.astype(jnp.float32).reshape(MICRO * SLOTS, SLOT_LEN, D)

    def one_slot(totals, inputs):
        stream, lengths_row, cot_rows = inputs
        segment, valid_rows = segments(lengths_row)

        def forward(stream_in, weights):
            return two_layers(stream_in, segment, valid_rows, weights)
        result, pullback = jax.vjp(forward, stream, params)
        grad_stream, grad_params = pullback(cot_rows)
        totals = jax.tree.map(jnp.add, totals, grad_params)
        return (totals, (result.astype(jnp.bfloat16), grad_stream.astype(jnp.bfloat16)))
    initial = tuple((jnp.zeros_like(weight) for weight in params))
    totals, outputs = lax.scan(one_slot, initial, (slot_rows, slot_lengths, slot_cot))
    shape_out = (MICRO, SLOTS, SLOT_LEN, D)
    return (outputs[0].reshape(shape_out), outputs[1].reshape(shape_out), totals[0], totals[1], totals[2], totals[3], totals[4], totals[5], totals[6], totals[7], totals[8], totals[9], totals[10], totals[11], totals[12], totals[13])
```

```python
from functools import partial
import math

import jax
import jax.numpy as jnp
from jax import lax
from jax.experimental import pallas as pl
from jax.experimental.pallas import tpu as pltpu
from jax.sharding import PartitionSpec as P

HEADS = 16
FEAT = 16
WINDOW = 64
CONV = 3


epsilon = 1e-05
masked_fill = -1e30
highest = lax.Precision.HIGHEST


MESH = pl.DeviceIdType.MESH

def gather_kernel(n_dp, n_ctx, chunks, lag, n_w, *refs):
    ins, outs = refs[:n_w], refs[n_w:2 * n_w]
    local_sem, send_sem, recv_sem = refs[2 * n_w:]
    dp, ctx = lax.axis_index("dp"), lax.axis_index("ctx")
    bits = [1 << i for i in range(n_dp.bit_length() - 1)]
    low_bits, (bit_x, bit_y) = bits[:-2], bits[-2:]
    barrier = pltpu.get_barrier_semaphore()
    greeted = 0
    for bit in bits:
        pl.semaphore_signal(barrier, inc=1, device_id=(dp ^ bit, ctx), device_id_type=MESH)
        greeted += 1
    for hop in range(1, n_ctx):
        pl.semaphore_signal(barrier, inc=1, device_id=(dp, lax.rem(ctx + hop, n_ctx)), device_id_type=MESH)
        greeted += 1
    pl.semaphore_wait(barrier, greeted)
    sends = []

    def piece(c, start, shards):
        w, col, width = chunks[c]
        return outs[w].at[pl.ds(start, shards), :, pl.ds(col, width)]

    def send(c, slot, start, rows, target, src=None):
        where = piece(c, start, rows)
        copy = pltpu.make_async_remote_copy(
            src_ref=where if src is None else src, dst_ref=where,
            send_sem=send_sem.at[c, slot], recv_sem=recv_sem.at[c, slot],
            device_id=target, device_id_type=MESH)
        copy.start()
        sends.append(copy)

    def arrive(c, slot, start, rows):
        where = piece(c, start, rows)
        pltpu.make_async_remote_copy(
            src_ref=where, dst_ref=where, send_sem=send_sem.at[c, slot], recv_sem=recv_sem.at[c, slot],
            device_id=(dp ^ 1, ctx), device_id_type=MESH).wait_recv()

    def stage_ctx(c):
        w, col, width = chunks[c]
        own = ins[w].at[:, :, pl.ds(col, width)]
        start = dp * n_ctx + ctx
        for hop in range(1, n_ctx):
            send(c, hop - 1, start, 1, (dp, lax.rem(ctx + hop, n_ctx)), src=own)
        pltpu.make_async_copy(own, piece(c, start, 1), local_sem.at[c]).start()

    base = n_ctx - 1
    SX, SY, SDX, SDY, SC = base, base + 1, base + 2, base + 3, base + 4

    def stage_sides(c):
        w, col, width = chunks[c]
        for hop in range(1, n_ctx):
            arrive(c, hop - 1, dp * n_ctx + lax.rem(ctx - hop + n_ctx, n_ctx), 1)
        own = ins[w].at[:, :, pl.ds(col, width)]
        pltpu.make_async_copy(own, piece(c, dp * n_ctx + ctx, 1), local_sem.at[c]).wait()
        group = n_ctx
        send(c, SX, dp * group, group, (dp ^ bit_x, ctx))
        send(c, SY, dp * group, group, (dp ^ bit_y, ctx))

    def stage_diag(c):
        group = n_ctx
        a0, an, b0, bn = 0, n_ctx // 2, n_ctx // 2, n_ctx - n_ctx // 2
        arrive(c, SX, (dp ^ bit_x) * group, group)
        send(c, SDY, (dp ^ bit_x) * group + a0, an, (dp ^ bit_y, ctx))
        arrive(c, SY, (dp ^ bit_y) * group, group)
        send(c, SDX, (dp ^ bit_y) * group + b0, bn, (dp ^ bit_x, ctx))

    def low_slot(level, j):
        return SC + 4 * ((1 << level) - 1) + j

    def quads(base_dp, level):
        out = []
        for top in range(4):
            for low in range(1 << level):
                flip = (bit_x if top & 1 else 0) | (bit_y if top & 2 else 0)
                for i in range(level):
                    if low >> i & 1:
                        flip |= low_bits[len(low_bits) - 1 - i]
                out.append(base_dp ^ flip)
        return out

    def stage_low(c, level):
        group = n_ctx
        if level == 0:
            a0, an, b0, bn = 0, n_ctx // 2, n_ctx // 2, n_ctx - n_ctx // 2
            arrive(c, SDY, (dp ^ bit_x ^ bit_y) * group + a0, an)
            arrive(c, SDX, (dp ^ bit_x ^ bit_y) * group + b0, bn)
        else:
            bit = low_bits[len(low_bits) - level]
            for j, block in enumerate(quads(dp ^ bit, level - 1)):
                arrive(c, low_slot(level - 1, j), block * group, group)
        if level < len(low_bits):
            bit = low_bits[len(low_bits) - 1 - level]
            for j, block in enumerate(quads(dp, level)):
                send(c, low_slot(level, j), block * group, group, (dp ^ bit, ctx))

    stages = [stage_ctx, stage_sides, stage_diag] + [partial(stage_low, level=l) for l in range(len(low_bits) + 1)]
    depth = len(stages)
    for t in range(len(chunks) + (depth - 1) * lag):
        for s in range(depth):
            c = t - s * lag
            if 0 <= c < len(chunks):
                stages[s](c)
    for copy in sends:
        copy.wait_send()

def gather_all(weights, n_dp, n_ctx, chunks, lag=1, cid=0):
    n = len(weights)
    places = n_dp * n_ctx
    slots = n_ctx - 1 + 4 + 4 * (n_dp // 4 - 1)
    full = pl.pallas_call(
        partial(gather_kernel, n_dp, n_ctx, chunks, lag, n),
        out_shape=[jax.ShapeDtypeStruct((places,) + w.shape, w.dtype) for w in weights],
        in_specs=[pl.BlockSpec(memory_space=pltpu.HBM)] * n,
        out_specs=[pl.BlockSpec(memory_space=pltpu.HBM)] * n,
        scratch_shapes=[pltpu.SemaphoreType.DMA((len(chunks),)), pltpu.SemaphoreType.DMA((len(chunks), slots)), pltpu.SemaphoreType.DMA((len(chunks), slots))],
        compiler_params=pltpu.CompilerParams(collective_id=cid, has_side_effects=True),
        name="gather_weights")(*[w[None] for w in weights])
    return [f.reshape(places * f.shape[1], f.shape[2]) for f in full]


def passed_along(value, axis, steps):
    count = lax.axis_size(axis)
    leading, last = (max(0, -steps), min(count, count - steps))
    return lax.ppermute(value, axis, [(source, source + steps) for source in range(leading, last)])


def carried_in(x, flags, axis, join):
    count = lax.axis_size(axis)
    low = jax.tree.map(lambda a: a.astype(jnp.bfloat16), x)
    state = jax.tree.map(jnp.zeros_like, x) + (flags[0] * 0.0,)
    for hop in range(count - 1, 0, -1):
        pairs = [(source, source + hop) for source in range(count - hop)]
        came = jax.tree.map(lambda a, own: lax.ppermute(a, axis, pairs).astype(own.dtype), low, x)
        state = join(state, came + (flags[hop],))
    return state


def entering(x, flags, axis, join):
    count = lax.axis_size(axis)
    low = jax.tree.map(lambda a: a.astype(jnp.bfloat16), x)
    state = jax.tree.map(jnp.zeros_like, x) + (flags[0] * 0.0,)
    for hop in range(count - 1, 0, -1):
        pairs = [(source + hop, source) for source in range(count - hop)]
        came = jax.tree.map(lambda a, own: lax.ppermute(a, axis, pairs).astype(own.dtype), low, x)
        state = join(state, came + (flags[hop],))
    return state


def chunks_of(shards):
    out = []
    for place, shard in enumerate(shards):
        rows, columns = shard.shape
        unit = max(128, 1408 * 32 // rows // 128 * 128)
        width = -(-(columns // 128) // -(-columns // unit)) * 128
        for first in range(0, columns, width):
            out.append((place, first, min(width, columns - first)))
    return out


def bit_reversed(value, bits):
    return sum(1 << (bits - 1 - i) for i in range(bits) if value >> i & 1)


def swapped(value, bit):
    count = lax.axis_size("dp")
    return lax.ppermute(value, "dp", [(source, source ^ bit) for source in range(count)])


def halving_order():
    count = lax.axis_size("dp")
    bits = count.bit_length() - 1
    return sorted(range(count), key=lambda place: bit_reversed(place, bits))


def by_place(operand):
    tokens, rows = operand.shape
    count = lax.axis_size("dp")
    blocks = operand.reshape(tokens, count, rows // count)
    me = lax.axis_index("dp")
    return jnp.stack(
        [lax.dynamic_index_in_dim(blocks, me ^ place, 1, False) for place in halving_order()],
        axis=1,
    )


def token_dot(operand, gradient):
    return jnp.einsum("tpr,te->pre", operand, gradient, preferred_element_type=jnp.float32)


def summed_to_owner(operand, gradient, extra=None):
    low = jnp.bfloat16
    count, ctx_count = lax.axis_size("dp"), lax.axis_size("ctx")
    bits = count.bit_length() - 1
    operand = operand.reshape(-1, operand.shape[-1])
    gradient = gradient.reshape(-1, gradient.shape[-1])
    placed = by_place(operand)
    half = count // 2
    sent = token_dot(placed[:, half:], gradient)
    kept = token_dot(placed[:, :half], gradient)
    if extra is not None:
        extra_placed = by_place(extra.T).transpose(1, 2, 0)
        sent = jnp.concatenate([sent, extra_placed[half:]], axis=-1)
        kept = jnp.concatenate([kept, extra_placed[:half]], axis=-1)
    kept = (kept + swapped(sent.astype(low), 1).astype(jnp.float32)).astype(low)
    for level in range(1, bits - 2):
        half //= 2
        came = swapped(kept[half:], 1 << level)
        kept = (kept[:half].astype(jnp.float32) + came.astype(jnp.float32)).astype(low)
    own, over_y, over_x, across = kept[0], kept[1], kept[2], kept[3]
    bit_x, bit_y = count // 4, count // 2
    rows, columns = own.shape
    first = rows // 32 * 16
    by_y = swapped(across[:first], bit_y)
    by_x = swapped(across[first:], bit_x)
    over_x = jnp.concatenate([over_x[:first] + by_y, over_x[first:]], axis=0)
    over_y = jnp.concatenate([over_y[:first], over_y[first:] + by_x], axis=0)
    came_x = swapped(over_x, bit_x)
    came_y = swapped(over_y, bit_y)
    total = own.astype(jnp.float32) + came_x.astype(jnp.float32) + came_y.astype(jnp.float32)
    total = total.reshape(ctx_count, rows // ctx_count, columns)
    me = lax.axis_index("ctx")
    result = lax.dynamic_index_in_dim(total, me, 0, False)
    for hop in range(1, ctx_count):
        block = lax.dynamic_index_in_dim(total, lax.rem(me + hop, ctx_count), 0, False).astype(low)
        came = lax.ppermute(block, "ctx", [(i, (i + hop) % ctx_count) for i in range(ctx_count)])
        result = result + came.astype(jnp.float32)
    return result


def normed(stream, scale_gain):
    return (
        stream * lax.rsqrt(jnp.mean(stream * stream, axis=-1, keepdims=True) + epsilon) * scale_gain
    )


def matmul(operand, weight):
    return jnp.einsum("mtd,de->mte", operand, weight, preferred_element_type=jnp.float32)


def matmul_back(operand, weight):
    return jnp.einsum("mte,de->mtd", operand, weight, preferred_element_type=jnp.float32)


def weight_grad(operand, gradient):
    return jnp.einsum("mtd,mte->de", operand, gradient, preferred_element_type=jnp.float32)


def feature_map(source):
    feat_width = source.shape[-1]
    outer_prod = (source[..., :, None] * source[..., None, :]).reshape(
        source.shape[:-1] + (feat_width * feat_width,)
    )
    ones_col = jnp.ones(source.shape[:-1] + (1,), source.dtype)
    return jnp.concatenate(
        [ones_col, source * feat_width ** (-0.25), outer_prod / math.sqrt(2.0 * feat_width)],
        axis=-1,
    )


def chain_states(earlier, later):
    keep_part = 1.0 - later[2]
    return (
        later[0] + keep_part[:, None, None, None] * earlier[0],
        later[1] + keep_part[:, None, None] * earlier[1],
        jnp.maximum(earlier[2], later[2]),
    )


def layout(seq_lengths, tok_count):
    seq_ends = jnp.cumsum(seq_lengths[:, 0, :], axis=-1, dtype=jnp.int32)
    first_pos = lax.axis_index("ctx") * tok_count

    def segment_of(positions):
        return jnp.sum(
            (positions[None, :, None] >= seq_ends[:, None, :]).astype(jnp.int32),
            axis=-1,
            dtype=jnp.int32,
        )

    own_pos = first_pos + jnp.arange(tok_count, dtype=jnp.int32)
    own_seg = segment_of(own_pos)
    before_seg = segment_of(own_pos - 1)

    def flags(direction):
        out = []
        for hop in range(lax.axis_size("ctx")):
            first = first_pos + direction * hop * tok_count
            held = (seq_ends >= first) & (seq_ends < first + tok_count) & (seq_ends < total_len)
            out.append(jnp.any(held | (first == 0), axis=1).astype(jnp.float32))
        return out

    total_len = tok_count * lax.axis_size("ctx")
    tap_masks = []
    for offset in range(CONV):
        source = own_pos - offset
        tap_masks.append(
            ((segment_of(source) == own_seg) & (source >= 0)[None, :]).astype(jnp.float32)
        )
    key_pos = first_pos - (WINDOW - 1) + jnp.arange(tok_count + WINDOW - 1, dtype=jnp.int32)
    visible = (key_pos[None, :] <= own_pos[:, None]) & (
        key_pos[None, :] > own_pos[:, None] - WINDOW
    )
    visible = visible & (key_pos >= 0)[None, :]
    window_mask = visible[None] & (segment_of(key_pos)[:, None, :] == own_seg[:, :, None])
    causal = (own_pos[:, None] >= own_pos[None, :])[None] & (
        own_seg[:, :, None] == own_seg[:, None, :]
    )
    return {
        "valid": (own_pos[None, :] < seq_ends[:, -1:]).astype(jnp.float32),
        "flags_before": flags(-1),
        "flags_after": flags(1),
        "carried": ((own_seg == before_seg[:, :1]) & (first_pos > 0)).astype(jnp.float32),
        "last": (own_seg == own_seg[:, -1:]).astype(jnp.float32),
        "causal": causal,
        "taps": jnp.stack(tap_masks),
        "window": window_mask,
    }


def conv_gate(pre_values, rim_rows, tap_weights, tap_masks):
    tok_count = pre_values.shape[1]
    rim_width = rim_rows.shape[1]
    extended = jnp.concatenate([rim_rows, pre_values], axis=1)
    conv_sum = jnp.zeros_like(pre_values)
    for offset in range(rim_width + 1):
        shifted = extended[:, rim_width - offset : rim_width - offset + tok_count, :]
        conv_sum = conv_sum + tap_weights[:, offset] * shifted * tap_masks[offset][:, :, None]
    return conv_sum * jax.nn.silu(pre_values)


def end_state(key_rows, head_values, last_mask):
    features = feature_map(key_rows) * last_mask[:, :, None, None]
    return (
        jnp.einsum("mthr,mthe->mhre", features, head_values, precision=highest),
        jnp.sum(features, axis=1),
    )


def attend_linear(query_rows, key_rows, head_values, state_in, totals_in, causal, carried):
    micro_count, tok_count = (query_rows.shape[0], query_rows.shape[1])
    scores = jnp.einsum("mihf,mjhf->mhij", query_rows, key_rows, precision=highest) / math.sqrt(
        query_rows.shape[-1]
    )
    weights = (1.0 + scores + 0.5 * scores * scores) * causal[:, None].astype(jnp.float32)
    numerator = jnp.einsum("mhij,mjhe->mihe", weights, head_values, precision=highest)
    denominator = jnp.transpose(jnp.sum(weights, axis=-1), (0, 2, 1))
    features = feature_map(query_rows) * carried[:, :, None, None]
    numerator = numerator + jnp.einsum("mihr,mhre->mihe", features, state_in, precision=highest)
    denominator = denominator + jnp.einsum("mihr,mhr->mih", features, totals_in, precision=highest)
    return (numerator / denominator[..., None]).reshape(micro_count, tok_count, -1)


def linear_forward(stream, weights, layout_info):
    norm_gain, qk_weight, value_weight, tap_weights, out_weight = weights
    micro_count, tok_count, model_width = stream.shape
    normed_rows, norm_back = jax.vjp(normed, stream, norm_gain.astype(jnp.float32))
    normed_low = normed_rows.astype(jnp.bfloat16)
    qk_rows = matmul(normed_low, qk_weight).astype(jnp.bfloat16)
    pre_values = matmul(normed_low, value_weight)
    rim_rows = passed_along(pre_values[:, tok_count - CONV + 1 :, :], "ctx", 1)
    value_rows, conv_back = jax.vjp(
        partial(conv_gate, tap_masks=layout_info["taps"]),
        pre_values,
        rim_rows,
        tap_weights.astype(jnp.float32),
    )
    head_values = (
        value_rows.astype(jnp.bfloat16)
        .astype(jnp.float32)
        .reshape(micro_count, tok_count, HEADS, model_width // HEADS)
    )
    half_cols = qk_rows.shape[-1] // 2
    query_rows = (
        qk_rows[..., :half_cols].astype(jnp.float32).reshape(micro_count, tok_count, HEADS, FEAT)
    )
    key_rows = (
        qk_rows[..., half_cols:].astype(jnp.float32).reshape(micro_count, tok_count, HEADS, FEAT)
    )
    state_out, state_back = jax.vjp(
        partial(end_state, last_mask=layout_info["last"]), key_rows, head_values
    )
    incoming = carried_in(state_out, layout_info["flags_before"], "ctx", chain_states)
    attended, attend_back = jax.vjp(
        partial(attend_linear, causal=layout_info["causal"], carried=layout_info["carried"]),
        query_rows,
        key_rows,
        head_values,
        incoming[0],
        incoming[1],
    )
    attended_low = attended.astype(jnp.bfloat16)
    branch = matmul(attended_low, out_weight)
    return (
        stream + branch,
        (norm_back, normed_low, conv_back, state_back, attend_back, attended_low),
    )


def linear_backward(grad_stream, residuals, weights, layout_info, other_gains):
    norm_back, normed_low, conv_back, state_back, attend_back, attended_low = residuals
    qk_weight, value_weight, out_weight = (weights[1], weights[2], weights[4])
    micro_count, tok_count, model_width = grad_stream.shape
    grad_branch = grad_stream.astype(jnp.bfloat16)
    grad_out = summed_to_owner(attended_low, grad_branch)
    grad_attended = matmul_back(grad_branch, out_weight)
    grad_query, grad_key, grad_value, grad_state, grad_totals = attend_back(grad_attended)
    later_grads = entering((grad_state, grad_totals), layout_info["flags_after"], "ctx", chain_states)
    key_more, value_more = state_back((later_grads[0], later_grads[1]))
    grad_key = grad_key + key_more
    grad_value = grad_value + value_more
    grad_qk = jnp.concatenate(
        [
            grad_query.reshape(micro_count, tok_count, -1),
            grad_key.reshape(micro_count, tok_count, -1),
        ],
        axis=-1,
    ).astype(jnp.bfloat16)
    grad_pre, grad_rim, grad_taps = conv_back(
        grad_value.reshape(micro_count, tok_count, model_width)
    )
    returned = passed_along(grad_rim, "ctx", -1)
    grad_pre = grad_pre.at[:, tok_count - CONV + 1 :, :].add(returned)
    grad_pre_low = grad_pre.astype(jnp.bfloat16)
    grad_normed = matmul_back(grad_qk, qk_weight) + matmul_back(grad_pre_low, value_weight)
    grad_input, grad_gain = norm_back(grad_normed)
    small = jnp.concatenate(
        [other_gains, grad_gain[:, None], grad_taps, jnp.zeros((model_width, 121), jnp.float32)], axis=1
    )
    grad_both = summed_to_owner(normed_low, jnp.concatenate([grad_qk, grad_pre_low], axis=-1), small)
    return (grad_stream + grad_input, grad_both, grad_out)


def window_scores(heads_query, key_ext, window_mask, head_size):
    raw_scores = jnp.einsum(
        "mihe,mjhe->mhij", heads_query, key_ext, preferred_element_type=jnp.float32
    ) * head_size ** (-0.5)
    return jnp.where(window_mask[:, None], raw_scores, masked_fill)


def window_forward(stream, weights, layout_info):
    norm_gain, qkv_weight, out_weight = weights
    micro_count, tok_count, model_width = stream.shape
    head_size = model_width // HEADS
    normed_rows, norm_back = jax.vjp(normed, stream, norm_gain.astype(jnp.float32))
    normed_low = normed_rows.astype(jnp.bfloat16)
    qkv_rows = matmul(normed_low, qkv_weight).astype(jnp.bfloat16)
    key_value = qkv_rows[..., model_width:]
    rim_rows = passed_along(key_value[:, tok_count - WINDOW + 1 :, :], "ctx", 1)
    extended = jnp.concatenate([rim_rows, key_value], axis=1)
    key_ext = extended[..., :model_width].reshape(micro_count, -1, HEADS, head_size)
    value_ext = extended[..., model_width:].reshape(micro_count, -1, HEADS, head_size)
    heads_query = qkv_rows[..., :model_width].reshape(micro_count, tok_count, HEADS, head_size)
    scores = window_scores(heads_query, key_ext, layout_info["window"], head_size)
    row_peak = jnp.max(scores, axis=-1, keepdims=True)
    exp_scores = jnp.exp(scores - row_peak)
    row_total = jnp.sum(exp_scores, axis=-1, keepdims=True)
    probabilities = (exp_scores / row_total).astype(jnp.bfloat16)
    attended = jnp.einsum(
        "mhij,mjhe->mihe", probabilities, value_ext, preferred_element_type=jnp.float32
    )
    attended = attended.astype(jnp.bfloat16).reshape(micro_count, tok_count, model_width)
    branch = matmul(attended, out_weight)
    return (
        stream + branch,
        (
            norm_back,
            normed_low,
            heads_query,
            key_ext,
            value_ext,
            row_peak + jnp.log(row_total),
            attended,
        ),
    )


def window_backward(grad_stream, residuals, weights, layout_info):
    norm_back, normed_low, heads_query, key_ext, value_ext, log_total, attended = residuals
    qkv_weight, out_weight = (weights[1], weights[2])
    micro_count, tok_count, model_width = grad_stream.shape
    head_size = model_width // HEADS
    grad_branch = grad_stream.astype(jnp.bfloat16)
    grad_out = summed_to_owner(attended, grad_branch)
    grad_attended = (
        matmul_back(grad_branch, out_weight)
        .astype(jnp.bfloat16)
        .reshape(micro_count, tok_count, HEADS, head_size)
    )
    scores = window_scores(heads_query, key_ext, layout_info["window"], head_size)
    probabilities = jnp.exp(scores - log_total)
    grad_probs = jnp.einsum(
        "mihe,mjhe->mhij", grad_attended, value_ext, preferred_element_type=jnp.float32
    )
    grad_value_ext = jnp.einsum(
        "mhij,mihe->mjhe",
        probabilities.astype(jnp.bfloat16),
        grad_attended,
        preferred_element_type=jnp.float32,
    )
    inner_sum = jnp.sum(grad_probs * probabilities, axis=-1, keepdims=True)
    grad_scores = (probabilities * (grad_probs - inner_sum)).astype(jnp.bfloat16)
    score_scale = head_size ** (-0.5)
    grad_query = (
        jnp.einsum("mhij,mjhe->mihe", grad_scores, key_ext, preferred_element_type=jnp.float32)
        * score_scale
    )
    grad_key_ext = (
        jnp.einsum("mhij,mihe->mjhe", grad_scores, heads_query, preferred_element_type=jnp.float32)
        * score_scale
    )
    rim_grads = jnp.concatenate(
        [
            grad_key_ext[:, : WINDOW - 1].reshape(micro_count, WINDOW - 1, model_width),
            grad_value_ext[:, : WINDOW - 1].reshape(micro_count, WINDOW - 1, model_width),
        ],
        axis=-1,
    )
    returned = passed_along(rim_grads.astype(jnp.bfloat16), "ctx", -1).astype(rim_grads.dtype)
    own_grads = jnp.concatenate(
        [
            grad_key_ext[:, WINDOW - 1 :].reshape(micro_count, tok_count, model_width),
            grad_value_ext[:, WINDOW - 1 :].reshape(micro_count, tok_count, model_width),
        ],
        axis=-1,
    )
    own_grads = own_grads.at[:, tok_count - WINDOW + 1 :, :].add(returned)
    grad_qkv = jnp.concatenate(
        [grad_query.reshape(micro_count, tok_count, model_width), own_grads], axis=-1
    ).astype(jnp.bfloat16)
    grad_qkv_weight = summed_to_owner(normed_low, grad_qkv)
    grad_input, grad_gain = norm_back(matmul_back(grad_qkv, qkv_weight))
    return (grad_stream + grad_input, (grad_gain, grad_qkv_weight, grad_out))


def ffn_forward(stream, weights):
    norm_gain, gate_up, down_weight = weights
    hidden_width = down_weight.shape[0]
    normed_rows, norm_back = jax.vjp(normed, stream, norm_gain.astype(jnp.float32))
    normed_low = normed_rows.astype(jnp.bfloat16)
    projected = matmul(normed_low, gate_up)
    hidden = (jax.nn.silu(projected[..., :hidden_width]) * projected[..., hidden_width:]).astype(
        jnp.bfloat16
    )
    branch = matmul(hidden, down_weight)
    return (stream + branch, (norm_back, normed_low, projected, hidden))


def ffn_backward(grad_stream, residuals, weights):
    norm_back, normed_low, projected, hidden = residuals
    gate_up, down_weight = (weights[1], weights[2])
    hidden_width = down_weight.shape[0]
    grad_branch = grad_stream.astype(jnp.bfloat16)
    grad_down = summed_to_owner(hidden, grad_branch)
    grad_hidden = matmul_back(grad_branch, down_weight)
    gate_part = projected[..., :hidden_width]
    up_part = projected[..., hidden_width:]
    sigmoid_gate = jax.nn.sigmoid(gate_part)
    grad_gate = grad_hidden * up_part * sigmoid_gate * (1.0 + gate_part * (1.0 - sigmoid_gate))
    grad_up = grad_hidden * gate_part * sigmoid_gate
    grad_projected = jnp.concatenate([grad_gate, grad_up], axis=-1).astype(jnp.bfloat16)
    grad_gate_up = summed_to_owner(normed_low, grad_projected)
    grad_input, grad_gain = norm_back(matmul_back(grad_projected, gate_up))
    return (grad_stream + grad_input, (grad_gain, grad_gate_up, grad_down))


def body(
    tokens_in,
    seq_lengths,
    norm_linear,
    proj_qk,
    proj_values,
    conv_taps,
    out_linear,
    norm_ffn_one,
    gate_up_one,
    down_one,
    norm_window,
    proj_qkv,
    out_window,
    norm_ffn_two,
    gate_up_two,
    down_two,
    cotangent,
):
    tok_count = tokens_in.shape[2]
    layout_info = layout(seq_lengths, tok_count)
    stream = tokens_in[:, 0].astype(jnp.float32)
    small = jnp.concatenate(
        [
            norm_linear[:, None],
            norm_ffn_one[:, None],
            norm_window[:, None],
            norm_ffn_two[:, None],
            conv_taps,
            jnp.zeros((conv_taps.shape[0], 121), jnp.bfloat16),
        ],
        axis=1,
    )
    shards = [
        small,
        proj_qk,
        proj_values,
        out_linear,
        gate_up_one,
        down_one,
        proj_qkv,
        out_window,
        gate_up_two,
        down_two,
    ]
    small, w_qk, w_values, w_out_linear, w_gu_one, w_dn_one, w_qkv, w_out_window, w_gu_two, w_dn_two = (
        gather_all(shards, lax.axis_size("dp"), lax.axis_size("ctx"), chunks_of(shards))
    )
    layer_one = (small[:, 0], w_qk, w_values, small[:, 4:7], w_out_linear, small[:, 1], w_gu_one, w_dn_one)
    layer_two = (small[:, 2], w_qkv, w_out_window, small[:, 3], w_gu_two, w_dn_two)
    middle, saved_linear = linear_forward(stream, layer_one[:5], layout_info)
    first_out, saved_ffn_one = ffn_forward(middle, layer_one[5:])
    second_mid, saved_window = window_forward(first_out, layer_two[:3], layout_info)
    closing, saved_ffn_two = ffn_forward(second_mid, layer_two[3:])
    valid_rows = layout_info["valid"][:, :, None]
    output = (closing * valid_rows).astype(jnp.bfloat16)[:, None]
    grad_stream = cotangent[:, 0].astype(jnp.float32) * valid_rows
    grad_stream, grads_ffn_two = ffn_backward(grad_stream, saved_ffn_two, layer_two[3:])
    grad_stream, grads_window = window_backward(
        grad_stream, saved_window, layer_two[:3], layout_info
    )
    grad_stream, grads_ffn_one = ffn_backward(grad_stream, saved_ffn_one, layer_one[5:])
    other_gains = jnp.stack([grads_ffn_one[0], grads_window[0], grads_ffn_two[0]], axis=1)
    grad_stream, grad_both, grad_out = linear_backward(
        grad_stream, saved_linear, layer_one[:5], layout_info, other_gains
    )
    qk_width, value_width = (proj_qk.shape[1], proj_values.shape[1])
    grad_small = grad_both[:, qk_width + value_width :]
    tokens_grad = grad_stream.astype(jnp.bfloat16)[:, None]
    return (
        output,
        tokens_grad,
        grad_small[:, 3],
        grad_both[:, :qk_width],
        grad_both[:, qk_width : qk_width + value_width],
        grad_small[:, 4:7],
        grad_out,
        grad_small[:, 0],
        grads_ffn_one[1],
        grads_ffn_one[2],
        grad_small[:, 1],
        grads_window[1],
        grads_window[2],
        grad_small[:, 2],
        grads_ffn_two[1],
        grads_ffn_two[2],
    )


def solution(mesh):
    placed = (
        P(None, "dp", "ctx", None),
        P(None, "dp", None),
        P(("dp", "ctx")),
        P(("dp", "ctx"), None),
        P(("dp", "ctx"), None),
        P(("dp", "ctx"), None),
        P(("dp", "ctx"), None),
        P(("dp", "ctx")),
        P(("dp", "ctx"), None),
        P(("dp", "ctx"), None),
        P(("dp", "ctx")),
        P(("dp", "ctx"), None),
        P(("dp", "ctx"), None),
        P(("dp", "ctx")),
        P(("dp", "ctx"), None),
        P(("dp", "ctx"), None),
        P(None, "dp", "ctx", None),
    )
    return jax.shard_map(
        body,
        mesh=mesh,
        in_specs=placed,
        out_specs=(
            P(None, "dp", "ctx", None),
            P(None, "dp", "ctx", None),
            P(("dp", "ctx")),
            P(("dp", "ctx"), None),
            P(("dp", "ctx"), None),
            P(("dp", "ctx"), None),
            P(("dp", "ctx"), None),
            P(("dp", "ctx")),
            P(("dp", "ctx"), None),
            P(("dp", "ctx"), None),
            P(("dp", "ctx")),
            P(("dp", "ctx"), None),
            P(("dp", "ctx"), None),
            P(("dp", "ctx")),
            P(("dp", "ctx"), None),
            P(("dp", "ctx"), None),
        ),
        check_vma=False,
    )
```

```python
from functools import partial
import math

import jax
import jax.numpy as jnp
from jax import lax
from jax.experimental import pallas as pl
from jax.experimental.pallas import tpu as pltpu
from jax.sharding import PartitionSpec as P

HEADS = 16
FEAT = 16
WINDOW = 64
CONV = 3


epsilon = 1e-05
masked_fill = -1e30
highest = lax.Precision.HIGHEST


MESH = pl.DeviceIdType.MESH

def gather_kernel(n_dp, n_ctx, chunks, lag, n_w, *refs):
    ins, outs = refs[:n_w], refs[n_w:2 * n_w]
    local_sem, send_sem, recv_sem = refs[2 * n_w:]
    dp, ctx = lax.axis_index("dp"), lax.axis_index("ctx")
    bits = [1 << i for i in range(n_dp.bit_length() - 1)]
    low_bits, (bit_x, bit_y) = bits[:-2], bits[-2:]
    barrier = pltpu.get_barrier_semaphore()
    greeted = 0
    for bit in bits:
        pl.semaphore_signal(barrier, inc=1, device_id=(dp ^ bit, ctx), device_id_type=MESH)
        greeted += 1
    for hop in range(1, n_ctx):
        pl.semaphore_signal(barrier, inc=1, device_id=(dp, lax.rem(ctx + hop, n_ctx)), device_id_type=MESH)
        greeted += 1
    pl.semaphore_wait(barrier, greeted)
    sends = []

    def piece(c, start, shards):
        w, col, width = chunks[c]
        return outs[w].at[pl.ds(start, shards), :, pl.ds(col, width)]

    def send(c, slot, start, rows, target, src=None):
        where = piece(c, start, rows)
        copy = pltpu.make_async_remote_copy(
            src_ref=where if src is None else src, dst_ref=where,
            send_sem=send_sem.at[c, slot], recv_sem=recv_sem.at[c, slot],
            device_id=target, device_id_type=MESH)
        copy.start()
        sends.append(copy)

    def arrive(c, slot, start, rows):
        where = piece(c, start, rows)
        pltpu.make_async_remote_copy(
            src_ref=where, dst_ref=where, send_sem=send_sem.at[c, slot], recv_sem=recv_sem.at[c, slot],
            device_id=(dp ^ 1, ctx), device_id_type=MESH).wait_recv()

    def stage_ctx(c):
        w, col, width = chunks[c]
        own = ins[w].at[:, :, pl.ds(col, width)]
        start = dp * n_ctx + ctx
        for hop in range(1, n_ctx):
            send(c, hop - 1, start, 1, (dp, lax.rem(ctx + hop, n_ctx)), src=own)
        pltpu.make_async_copy(own, piece(c, start, 1), local_sem.at[c]).start()

    base = n_ctx - 1
    SX, SY, SDX, SDY, SC = base, base + 1, base + 2, base + 3, base + 4

    def stage_sides(c):
        w, col, width = chunks[c]
        for hop in range(1, n_ctx):
            arrive(c, hop - 1, dp * n_ctx + lax.rem(ctx - hop + n_ctx, n_ctx), 1)
        own = ins[w].at[:, :, pl.ds(col, width)]
        pltpu.make_async_copy(own, piece(c, dp * n_ctx + ctx, 1), local_sem.at[c]).wait()
        group = n_ctx
        send(c, SX, dp * group, group, (dp ^ bit_x, ctx))
        send(c, SY, dp * group, group, (dp ^ bit_y, ctx))

    def stage_diag(c):
        group = n_ctx
        a0, an, b0, bn = 0, n_ctx // 2, n_ctx // 2, n_ctx - n_ctx // 2
        arrive(c, SX, (dp ^ bit_x) * group, group)
        send(c, SDY, (dp ^ bit_x) * group + a0, an, (dp ^ bit_y, ctx))
        arrive(c, SY, (dp ^ bit_y) * group, group)
        send(c, SDX, (dp ^ bit_y) * group + b0, bn, (dp ^ bit_x, ctx))

    def low_slot(level, j):
        return SC + 4 * ((1 << level) - 1) + j

    def quads(base_dp, level):
        out = []
        for top in range(4):
            for low in range(1 << level):
                flip = (bit_x if top & 1 else 0) | (bit_y if top & 2 else 0)
                for i in range(level):
                    if low >> i & 1:
                        flip |= low_bits[len(low_bits) - 1 - i]
                out.append(base_dp ^ flip)
        return out

    def stage_low(c, level):
        group = n_ctx
        if level == 0:
            a0, an, b0, bn = 0, n_ctx // 2, n_ctx // 2, n_ctx - n_ctx // 2
            arrive(c, SDY, (dp ^ bit_x ^ bit_y) * group + a0, an)
            arrive(c, SDX, (dp ^ bit_x ^ bit_y) * group + b0, bn)
        else:
            bit = low_bits[len(low_bits) - level]
            for j, block in enumerate(quads(dp ^ bit, level - 1)):
                arrive(c, low_slot(level - 1, j), block * group, group)
        if level < len(low_bits):
            bit = low_bits[len(low_bits) - 1 - level]
            for j, block in enumerate(quads(dp, level)):
                send(c, low_slot(level, j), block * group, group, (dp ^ bit, ctx))

    stages = [stage_ctx, stage_sides, stage_diag] + [partial(stage_low, level=l) for l in range(len(low_bits) + 1)]
    depth = len(stages)
    for t in range(len(chunks) + (depth - 1) * lag):
        for s in range(depth):
            c = t - s * lag
            if 0 <= c < len(chunks):
                stages[s](c)
    for copy in sends:
        copy.wait_send()

def gather_all(weights, n_dp, n_ctx, chunks, lag=1, cid=0):
    n = len(weights)
    places = n_dp * n_ctx
    slots = n_ctx - 1 + 4 + 4 * (n_dp // 4 - 1)
    full = pl.pallas_call(
        partial(gather_kernel, n_dp, n_ctx, chunks, lag, n),
        out_shape=[jax.ShapeDtypeStruct((places,) + w.shape, w.dtype) for w in weights],
        in_specs=[pl.BlockSpec(memory_space=pltpu.HBM)] * n,
        out_specs=[pl.BlockSpec(memory_space=pltpu.HBM)] * n,
        scratch_shapes=[pltpu.SemaphoreType.DMA((len(chunks),)), pltpu.SemaphoreType.DMA((len(chunks), slots)), pltpu.SemaphoreType.DMA((len(chunks), slots))],
        compiler_params=pltpu.CompilerParams(collective_id=cid, has_side_effects=True),
        name="gather_weights")(*[w[None] for w in weights])
    return [f.reshape(places * f.shape[1], f.shape[2]) for f in full]


WIDE = 512
SLOTS_HELD = 8


def scatter_kernel(n_dp, n_ctx, plan, lags, n_x, n_y, n_o, *refs):
    xs, ys, outs = refs[:n_x], refs[n_x : n_x + n_y], refs[n_x + n_y : n_x + n_y + n_o]
    refs = refs[n_x + n_y + n_o :]
    bits = [1 << i for i in range(n_dp.bit_length() - 1)]
    low_bits, (bit_x, bit_y) = bits[:-2], bits[-2:]
    n_low = len(low_bits)
    x_all, y_all = refs[0], refs[1]
    low_out, low_in = refs[2 : 2 + n_low], refs[2 + n_low : 2 + 2 * n_low]
    refs = refs[2 + 2 * n_low :]
    cross, cross_y, cross_x, side_x, side_y, came_x, came_y, shards, came_ctx, result = refs[:10]
    x_sem, y_sem, out_sem, sent, arrived, credit = refs[10:]
    held = y_all.shape[0]
    dp, ctx = lax.axis_index("dp"), lax.axis_index("ctx")
    group = cross.shape[1]
    half = group // 2
    rows = group // n_ctx
    f32, low = jnp.float32, jnp.bfloat16
    A_CY, A_CX, A_X, A_Y, A_Z = n_low, n_low + 1, n_low + 2, n_low + 3, n_low + 4
    C_X, C_Y, C_Z = n_low, n_low + 1, n_low + 2

    def at_ctx(hop):
        return (dp, lax.rem(ctx + hop, n_ctx))

    barrier = pltpu.get_barrier_semaphore()
    for bit in bits:
        pl.semaphore_signal(barrier, inc=1, device_id=(dp ^ bit, ctx), device_id_type=MESH)
    for hop in range(1, n_ctx):
        pl.semaphore_signal(barrier, inc=1, device_id=at_ctx(hop), device_id_type=MESH)
    pl.semaphore_wait(barrier, len(bits) + n_ctx - 1)

    bounds, count = [], 0
    for segment in plan:
        bounds.append((count, count + segment[5]))
        count += segment[5]
    x_first = [None] * n_x
    for segment, (first, _) in zip(plan, bounds):
        if x_first[segment[0]] is None:
            x_first[segment[0]] = first

    def x_copy(i):
        return pltpu.make_async_copy(xs[i], x_all.at[i], x_sem.at[i])

    for i in range(n_x):
        x_copy(i).start()

    def y_start(c):
        slot = lax.rem(c, held)
        for segment, (first, last) in zip(plan, bounds):

            @pl.when((c >= first) & (c < last))
            def _():
                where = pl.multiple_of((c - first) * WIDE, WIDE)
                pltpu.make_async_copy(
                    ys[segment[1]].at[:, pl.ds(where, WIDE)], y_all.at[slot], y_sem.at[slot]
                ).start()

    def x_place(c):
        return sum((c >= first).astype(jnp.int32) for first in x_first[1:])

    def partial_sum(c, flip):
        return jnp.dot(
            x_all[x_place(c), dp ^ flip], y_all[lax.rem(c, held)], preferred_element_type=f32
        )

    def rest(level):
        free = low_bits[level + 1 :] + [bit_x, bit_y]
        return [sum(b for i, b in enumerate(free) if n >> i & 1) for n in range(1 << len(free))]

    def summed(c, flip, levels):
        total = partial_sum(c, flip)
        for level in range(levels):
            total = total + low_in[level][lax.rem(c, held), rest(level).index(flip)].astype(f32)
        return total

    def remote(src, dst, slot, kind, target):
        return pltpu.make_async_remote_copy(
            src_ref=src,
            dst_ref=dst,
            send_sem=sent.at[slot, kind],
            recv_sem=arrived.at[slot, kind],
            device_id=target,
            device_id_type=MESH,
        )

    def copy_of(slot, kind):
        over_x, over_y = (dp ^ bit_x, ctx), (dp ^ bit_y, ctx)
        if kind < n_low:
            return remote(
                low_out[kind].at[slot], low_in[kind].at[slot], slot, kind, (dp ^ low_bits[kind], ctx)
            )
        if kind == A_CY:
            return remote(cross.at[slot, pl.ds(0, half)], cross_y.at[slot], slot, kind, over_y)
        if kind == A_CX:
            return remote(cross.at[slot, pl.ds(half, half)], cross_x.at[slot], slot, kind, over_x)
        if kind == A_X:
            return remote(side_x.at[slot], came_x.at[slot], slot, kind, over_x)
        if kind == A_Y:
            return remote(side_y.at[slot], came_y.at[slot], slot, kind, over_y)
        hop = kind - A_Z + 1
        there = lax.rem(ctx + hop, n_ctx)
        return remote(shards.at[slot, there], came_ctx.at[slot, hop - 1], slot, kind, (dp, there))

    def need_credit(c, kind):
        @pl.when(c >= held)
        def _():
            pl.semaphore_wait(credit.at[kind], 1)

    def step_low(level, c):
        slot = lax.rem(c, held)
        if level == 0:
            for i, first in enumerate(x_first):

                @pl.when(c == first)
                def _():
                    x_copy(i).wait()

            pltpu.make_async_copy(ys[0].at[:, pl.ds(0, WIDE)], y_all.at[slot], y_sem.at[slot]).wait()
        else:
            copy_of(slot, level - 1).wait_recv()
        need_credit(c, level)
        for j, flip in enumerate(rest(level)):
            low_out[level][slot, j] = summed(c, flip | low_bits[level], level).astype(low)
        copy_of(slot, level).start()

    def step_cross(c):
        slot = lax.rem(c, held)
        if n_low:
            copy_of(slot, n_low - 1).wait_recv()
        need_credit(c, C_X)
        need_credit(c, C_Y)
        cross[slot] = summed(c, bit_x | bit_y, n_low).astype(low)
        copy_of(slot, A_CY).start()
        copy_of(slot, A_CX).start()

    def step_sides(c):
        slot = lax.rem(c, held)
        over_x = summed(c, bit_x, n_low)
        over_y = summed(c, bit_y, n_low)
        copy_of(slot, A_CY).wait_recv()
        side_x[slot, :half] = (over_x[:half] + cross_y[slot].astype(f32)).astype(low)
        side_x[slot, half:] = over_x[half:].astype(low)
        copy_of(slot, A_X).start()
        copy_of(slot, A_CX).wait_recv()
        side_y[slot, :half] = over_y[:half].astype(low)
        side_y[slot, half:] = (over_y[half:] + cross_x[slot].astype(f32)).astype(low)
        copy_of(slot, A_Y).start()

    def step_own(c):
        slot = lax.rem(c, held)
        total = summed(c, 0, n_low)
        copy_of(slot, A_X).wait_recv()
        copy_of(slot, A_Y).wait_recv()
        total = total + came_x[slot].astype(f32) + came_y[slot].astype(f32)
        for j in range(n_ctx):
            shards[slot, j] = total[j * rows : (j + 1) * rows].astype(low)
        for hop in range(1, n_ctx):
            need_credit(c, C_Z + hop - 1)
            copy_of(slot, A_Z + hop - 1).start()

    def out_copy(c, slot, segment, first):
        where = pl.multiple_of((c - first) * WIDE, WIDE)
        _, _, o, row, n_rows, _ = segment
        return pltpu.make_async_copy(
            result.at[slot, pl.ds(0, n_rows)],
            outs[o].at[pl.ds(row, n_rows), pl.ds(where, WIDE)],
            out_sem.at[slot],
        )

    def each_segment(c, act):
        for segment, (first, last) in zip(plan, bounds):

            @pl.when((c >= first) & (c < last))
            def _():
                act(segment, first)

    def out_wait(c):
        slot = lax.rem(c, held)
        each_segment(c, lambda segment, first: out_copy(c, slot, segment, first).wait())

    def step_end(c):
        slot = lax.rem(c, held)

        @pl.when(c >= held)
        def _():
            out_wait(c - held)

        total = shards[slot, ctx].astype(f32)
        for hop in range(1, n_ctx):
            copy_of(slot, A_Z + hop - 1).wait_recv()
            total = total + came_ctx[slot, hop - 1].astype(f32)
        result[slot] = total
        each_segment(c, lambda segment, first: out_copy(c, slot, segment, first).start())
        for kind in range(A_Z + n_ctx - 1):
            copy_of(slot, kind).wait_send()

        @pl.when(c + held < count)
        def _():
            for level, bit in enumerate(low_bits):
                pl.semaphore_signal(credit.at[level], inc=1, device_id=(dp ^ bit, ctx), device_id_type=MESH)
            pl.semaphore_signal(credit.at[C_X], inc=1, device_id=(dp ^ bit_x, ctx), device_id_type=MESH)
            pl.semaphore_signal(credit.at[C_Y], inc=1, device_id=(dp ^ bit_y, ctx), device_id_type=MESH)
            for hop in range(1, n_ctx):
                pl.semaphore_signal(
                    credit.at[C_Z + hop - 1], inc=1, device_id=at_ctx(n_ctx - hop), device_id_type=MESH
                )

    steps = [partial(step_low, level) for level in range(n_low)] + [step_cross, step_sides, step_own, step_end]
    ahead = 2
    for c in range(ahead):
        y_start(jnp.int32(c))

    def turn(t, carry):
        @pl.when(t + ahead < count)
        def _():
            y_start(t + ahead)

        for step, lag in zip(steps, lags):
            c = t - lag

            @pl.when((c >= 0) & (c < count))
            def _():
                step(c)

        return carry

    lax.fori_loop(0, count + lags[-1], turn, 0)
    for c in range(max(0, count - held), count):
        out_wait(jnp.int32(c))


def scatter_sums(xs, ys, out_shapes, plan, n_dp, n_ctx, cid=1, lags=None, held=SLOTS_HELD):
    group, tokens = xs[0].shape[1:]
    n_low = n_dp.bit_length() - 3
    rows = group // n_ctx
    low, f32 = jnp.bfloat16, jnp.float32
    lags = lags or list(range(n_low + 4))
    low_shapes = [
        pltpu.VMEM((held, n_dp >> (level + 1), group, WIDE), low) for level in range(n_low)
    ]
    half = group // 2
    kinds = n_low + 4 + n_ctx - 1
    return pl.pallas_call(
        partial(scatter_kernel, n_dp, n_ctx, plan, lags, len(xs), len(ys), len(out_shapes)),
        out_shape=[jax.ShapeDtypeStruct(shape, f32) for shape in out_shapes],
        in_specs=[pl.BlockSpec(memory_space=pl.ANY)] * (len(xs) + len(ys)),
        out_specs=[pl.BlockSpec(memory_space=pltpu.HBM)] * len(out_shapes),
        scratch_shapes=[
            pltpu.VMEM((len(xs),) + xs[0].shape, low),
            pltpu.VMEM((held, tokens, WIDE), low),
            *low_shapes,
            *low_shapes,
            pltpu.VMEM((held, group, WIDE), low),
            pltpu.VMEM((held, half, WIDE), low),
            pltpu.VMEM((held, half, WIDE), low),
            pltpu.VMEM((held, group, WIDE), low),
            pltpu.VMEM((held, group, WIDE), low),
            pltpu.VMEM((held, group, WIDE), low),
            pltpu.VMEM((held, group, WIDE), low),
            pltpu.VMEM((held, n_ctx, rows, WIDE), low),
            pltpu.VMEM((held, n_ctx - 1, rows, WIDE), low),
            pltpu.VMEM((held, rows, WIDE), f32),
            pltpu.SemaphoreType.DMA((len(xs),)),
            pltpu.SemaphoreType.DMA((held,)),
            pltpu.SemaphoreType.DMA((held,)),
            pltpu.SemaphoreType.DMA((held, kinds)),
            pltpu.SemaphoreType.DMA((held, kinds)),
            pltpu.SemaphoreType.REGULAR((n_low + 2 + n_ctx - 1,)),
        ],
        compiler_params=pltpu.CompilerParams(
            collective_id=cid, has_side_effects=True, vmem_limit_bytes=56 * 2**20
        ),
        name="scatter_sums",
    )(*xs, *ys)


def passed_along(value, axis, steps):
    count = lax.axis_size(axis)
    leading, last = (max(0, -steps), min(count, count - steps))
    return lax.ppermute(value, axis, [(source, source + steps) for source in range(leading, last)])


def carried_in(x, flags, axis, join):
    count = lax.axis_size(axis)
    low = jax.tree.map(lambda a: a.astype(jnp.bfloat16), x)
    state = jax.tree.map(jnp.zeros_like, x) + (flags[0] * 0.0,)
    for hop in range(count - 1, 0, -1):
        pairs = [(source, source + hop) for source in range(count - hop)]
        came = jax.tree.map(lambda a, own: lax.ppermute(a, axis, pairs).astype(own.dtype), low, x)
        state = join(state, came + (flags[hop],))
    return state


def entering(x, flags, axis, join):
    count = lax.axis_size(axis)
    low = jax.tree.map(lambda a: a.astype(jnp.bfloat16), x)
    state = jax.tree.map(jnp.zeros_like, x) + (flags[0] * 0.0,)
    for hop in range(count - 1, 0, -1):
        pairs = [(source + hop, source) for source in range(count - hop)]
        came = jax.tree.map(lambda a, own: lax.ppermute(a, axis, pairs).astype(own.dtype), low, x)
        state = join(state, came + (flags[hop],))
    return state


def chunks_of(shards):
    out = []
    for place, shard in enumerate(shards):
        rows, columns = shard.shape
        unit = max(128, 1408 * 32 // rows // 128 * 128)
        width = -(-(columns // 128) // -(-columns // unit)) * 128
        for first in range(0, columns, width):
            out.append((place, first, min(width, columns - first)))
    return out


def chunk_plan(products, unit):
    places, n_dp = lax.axis_size("dp") * lax.axis_size("ctx"), lax.axis_size("dp")
    laid, first_laid, plan, shapes = [], {}, [], []
    for number, (operand, gradient) in enumerate(products):
        tokens, rows = operand.shape
        shard = rows // places
        shapes.append((shard, gradient.shape[1]))
        if id(operand) not in first_laid:
            first_laid[id(operand)] = len(laid)
            turned = operand.T.reshape(places, shard, tokens)
            for first in range(0, shard, unit):
                piece = turned[:, first : first + unit]
                piece = jnp.pad(piece, ((0, 0), (0, unit - piece.shape[1]), (0, 0)))
                laid.append(piece.reshape(n_dp, -1, tokens))
        for piece, first in enumerate(range(0, shard, unit)):
            plan.append(
                (
                    first_laid[id(operand)] + piece,
                    number,
                    number,
                    first,
                    min(unit, shard - first),
                    gradient.shape[1] // WIDE,
                )
            )
    return laid, plan, shapes


def summed_to_owners(products, small):
    n_dp, n_ctx = lax.axis_size("dp"), lax.axis_size("ctx")
    rows, few = small.shape
    tokens = products[0][0].shape[0]
    high = small.astype(jnp.bfloat16)
    rest = (small - high.astype(jnp.float32)).astype(jnp.bfloat16)
    both = jnp.zeros((tokens, rows), jnp.bfloat16).at[:few].set(high.T).at[few : 2 * few].set(rest.T)
    pick = jnp.zeros((tokens, WIDE), jnp.bfloat16)
    pick = pick.at[:few, :few].set(jnp.eye(few, dtype=jnp.bfloat16))
    pick = pick.at[few : 2 * few, :few].set(jnp.eye(few, dtype=jnp.bfloat16))
    products = [(both, pick)] + products
    laid, plan, shapes = chunk_plan(products, rows // (n_dp * n_ctx))
    sums = scatter_sums(laid, [gradient for _, gradient in products], shapes, plan, n_dp, n_ctx)
    return sums[0][:, :few], sums[1:]


def chunks_of(shards):
    out = []
    for place, shard in enumerate(shards):
        rows, columns = shard.shape
        unit = max(128, 1408 * 32 // rows // 128 * 128)
        width = -(-(columns // 128) // -(-columns // unit)) * 128
        for first in range(0, columns, width):
            out.append((place, first, min(width, columns - first)))
    return out


def flat(value):
    return value.reshape(-1, value.shape[-1])


def normed(stream, scale_gain):
    return (
        stream * lax.rsqrt(jnp.mean(stream * stream, axis=-1, keepdims=True) + epsilon) * scale_gain
    )


def matmul(operand, weight):
    return jnp.einsum("mtd,de->mte", operand, weight, preferred_element_type=jnp.float32)


def matmul_back(operand, weight):
    return jnp.einsum("mte,de->mtd", operand, weight, preferred_element_type=jnp.float32)


def weight_grad(operand, gradient):
    return jnp.einsum("mtd,mte->de", operand, gradient, preferred_element_type=jnp.float32)


def feature_map(source):
    feat_width = source.shape[-1]
    outer_prod = (source[..., :, None] * source[..., None, :]).reshape(
        source.shape[:-1] + (feat_width * feat_width,)
    )
    ones_col = jnp.ones(source.shape[:-1] + (1,), source.dtype)
    return jnp.concatenate(
        [ones_col, source * feat_width ** (-0.25), outer_prod / math.sqrt(2.0 * feat_width)],
        axis=-1,
    )


def chain_states(earlier, later):
    keep_part = 1.0 - later[2]
    return (
        later[0] + keep_part[:, None, None, None] * earlier[0],
        later[1] + keep_part[:, None, None] * earlier[1],
        jnp.maximum(earlier[2], later[2]),
    )


def layout(seq_lengths, tok_count):
    seq_ends = jnp.cumsum(seq_lengths[:, 0, :], axis=-1, dtype=jnp.int32)
    first_pos = lax.axis_index("ctx") * tok_count

    def segment_of(positions):
        return jnp.sum(
            (positions[None, :, None] >= seq_ends[:, None, :]).astype(jnp.int32),
            axis=-1,
            dtype=jnp.int32,
        )

    own_pos = first_pos + jnp.arange(tok_count, dtype=jnp.int32)
    own_seg = segment_of(own_pos)
    before_seg = segment_of(own_pos - 1)

    def flags(direction):
        out = []
        for hop in range(lax.axis_size("ctx")):
            first = first_pos + direction * hop * tok_count
            held = (seq_ends >= first) & (seq_ends < first + tok_count) & (seq_ends < total_len)
            out.append(jnp.any(held | (first == 0), axis=1).astype(jnp.float32))
        return out

    total_len = tok_count * lax.axis_size("ctx")
    tap_masks = []
    for offset in range(CONV):
        source = own_pos - offset
        tap_masks.append(
            ((segment_of(source) == own_seg) & (source >= 0)[None, :]).astype(jnp.float32)
        )
    key_pos = first_pos - (WINDOW - 1) + jnp.arange(tok_count + WINDOW - 1, dtype=jnp.int32)
    visible = (key_pos[None, :] <= own_pos[:, None]) & (
        key_pos[None, :] > own_pos[:, None] - WINDOW
    )
    visible = visible & (key_pos >= 0)[None, :]
    window_mask = visible[None] & (segment_of(key_pos)[:, None, :] == own_seg[:, :, None])
    causal = (own_pos[:, None] >= own_pos[None, :])[None] & (
        own_seg[:, :, None] == own_seg[:, None, :]
    )
    return {
        "valid": (own_pos[None, :] < seq_ends[:, -1:]).astype(jnp.float32),
        "flags_before": flags(-1),
        "flags_after": flags(1),
        "carried": ((own_seg == before_seg[:, :1]) & (first_pos > 0)).astype(jnp.float32),
        "last": (own_seg == own_seg[:, -1:]).astype(jnp.float32),
        "causal": causal,
        "taps": jnp.stack(tap_masks),
        "window": window_mask,
    }


def conv_gate(pre_values, rim_rows, tap_weights, tap_masks):
    tok_count = pre_values.shape[1]
    rim_width = rim_rows.shape[1]
    extended = jnp.concatenate([rim_rows, pre_values], axis=1)
    conv_sum = jnp.zeros_like(pre_values)
    for offset in range(rim_width + 1):
        shifted = extended[:, rim_width - offset : rim_width - offset + tok_count, :]
        conv_sum = conv_sum + tap_weights[:, offset] * shifted * tap_masks[offset][:, :, None]
    return conv_sum * jax.nn.silu(pre_values)


def end_state(key_rows, head_values, last_mask):
    features = feature_map(key_rows) * last_mask[:, :, None, None]
    return (
        jnp.einsum("mthr,mthe->mhre", features, head_values, precision=highest),
        jnp.sum(features, axis=1),
    )


def attend_linear(query_rows, key_rows, head_values, state_in, totals_in, causal, carried):
    micro_count, tok_count = (query_rows.shape[0], query_rows.shape[1])
    scores = jnp.einsum("mihf,mjhf->mhij", query_rows, key_rows, precision=highest) / math.sqrt(
        query_rows.shape[-1]
    )
    weights = (1.0 + scores + 0.5 * scores * scores) * causal[:, None].astype(jnp.float32)
    numerator = jnp.einsum("mhij,mjhe->mihe", weights, head_values, precision=highest)
    denominator = jnp.transpose(jnp.sum(weights, axis=-1), (0, 2, 1))
    features = feature_map(query_rows) * carried[:, :, None, None]
    numerator = numerator + jnp.einsum("mihr,mhre->mihe", features, state_in, precision=highest)
    denominator = denominator + jnp.einsum("mihr,mhr->mih", features, totals_in, precision=highest)
    return (numerator / denominator[..., None]).reshape(micro_count, tok_count, -1)


def linear_forward(stream, weights, layout_info):
    norm_gain, qk_weight, value_weight, tap_weights, out_weight = weights
    micro_count, tok_count, model_width = stream.shape
    normed_rows, norm_back = jax.vjp(normed, stream, norm_gain.astype(jnp.float32))
    normed_low = normed_rows.astype(jnp.bfloat16)
    qk_rows = matmul(normed_low, qk_weight).astype(jnp.bfloat16)
    pre_values = matmul(normed_low, value_weight)
    rim_rows = passed_along(pre_values[:, tok_count - CONV + 1 :, :], "ctx", 1)
    value_rows, conv_back = jax.vjp(
        partial(conv_gate, tap_masks=layout_info["taps"]),
        pre_values,
        rim_rows,
        tap_weights.astype(jnp.float32),
    )
    head_values = (
        value_rows.astype(jnp.bfloat16)
        .astype(jnp.float32)
        .reshape(micro_count, tok_count, HEADS, model_width // HEADS)
    )
    half_cols = qk_rows.shape[-1] // 2
    query_rows = (
        qk_rows[..., :half_cols].astype(jnp.float32).reshape(micro_count, tok_count, HEADS, FEAT)
    )
    key_rows = (
        qk_rows[..., half_cols:].astype(jnp.float32).reshape(micro_count, tok_count, HEADS, FEAT)
    )
    state_out, state_back = jax.vjp(
        partial(end_state, last_mask=layout_info["last"]), key_rows, head_values
    )
    incoming = carried_in(state_out, layout_info["flags_before"], "ctx", chain_states)
    attended, attend_back = jax.vjp(
        partial(attend_linear, causal=layout_info["causal"], carried=layout_info["carried"]),
        query_rows,
        key_rows,
        head_values,
        incoming[0],
        incoming[1],
    )
    attended_low = attended.astype(jnp.bfloat16)
    branch = matmul(attended_low, out_weight)
    return (
        stream + branch,
        (norm_back, normed_low, conv_back, state_back, attend_back, attended_low),
    )


def linear_backward(grad_stream, residuals, weights, layout_info, other_gains):
    norm_back, normed_low, conv_back, state_back, attend_back, attended_low = residuals
    qk_weight, value_weight, out_weight = (weights[1], weights[2], weights[4])
    micro_count, tok_count, model_width = grad_stream.shape
    grad_branch = grad_stream.astype(jnp.bfloat16)
    grad_out = (flat(attended_low), flat(grad_branch))
    grad_attended = matmul_back(grad_branch, out_weight)
    grad_query, grad_key, grad_value, grad_state, grad_totals = attend_back(grad_attended)
    later_grads = entering((grad_state, grad_totals), layout_info["flags_after"], "ctx", chain_states)
    key_more, value_more = state_back((later_grads[0], later_grads[1]))
    grad_key = grad_key + key_more
    grad_value = grad_value + value_more
    grad_qk = jnp.concatenate(
        [
            grad_query.reshape(micro_count, tok_count, -1),
            grad_key.reshape(micro_count, tok_count, -1),
        ],
        axis=-1,
    ).astype(jnp.bfloat16)
    grad_pre, grad_rim, grad_taps = conv_back(
        grad_value.reshape(micro_count, tok_count, model_width)
    )
    returned = passed_along(grad_rim, "ctx", -1)
    grad_pre = grad_pre.at[:, tok_count - CONV + 1 :, :].add(returned)
    grad_pre_low = grad_pre.astype(jnp.bfloat16)
    grad_normed = matmul_back(grad_qk, qk_weight) + matmul_back(grad_pre_low, value_weight)
    grad_input, grad_gain = norm_back(grad_normed)
    small = jnp.concatenate([grad_gain[:, None], other_gains, grad_taps], axis=1)
    operand = flat(normed_low)
    return (
        grad_stream + grad_input,
        (operand, flat(grad_qk)),
        (operand, flat(grad_pre_low)),
        grad_out,
        small,
    )


def window_scores(heads_query, key_ext, window_mask, head_size):
    raw_scores = jnp.einsum(
        "mihe,mjhe->mhij", heads_query, key_ext, preferred_element_type=jnp.float32
    ) * head_size ** (-0.5)
    return jnp.where(window_mask[:, None], raw_scores, masked_fill)


def window_forward(stream, weights, layout_info):
    norm_gain, qkv_weight, out_weight = weights
    micro_count, tok_count, model_width = stream.shape
    head_size = model_width // HEADS
    normed_rows, norm_back = jax.vjp(normed, stream, norm_gain.astype(jnp.float32))
    normed_low = normed_rows.astype(jnp.bfloat16)
    qkv_rows = matmul(normed_low, qkv_weight).astype(jnp.bfloat16)
    key_value = qkv_rows[..., model_width:]
    rim_rows = passed_along(key_value[:, tok_count - WINDOW + 1 :, :], "ctx", 1)
    extended = jnp.concatenate([rim_rows, key_value], axis=1)
    key_ext = extended[..., :model_width].reshape(micro_count, -1, HEADS, head_size)
    value_ext = extended[..., model_width:].reshape(micro_count, -1, HEADS, head_size)
    heads_query = qkv_rows[..., :model_width].reshape(micro_count, tok_count, HEADS, head_size)
    scores = window_scores(heads_query, key_ext, layout_info["window"], head_size)
    row_peak = jnp.max(scores, axis=-1, keepdims=True)
    exp_scores = jnp.exp(scores - row_peak)
    row_total = jnp.sum(exp_scores, axis=-1, keepdims=True)
    probabilities = (exp_scores / row_total).astype(jnp.bfloat16)
    attended = jnp.einsum(
        "mhij,mjhe->mihe", probabilities, value_ext, preferred_element_type=jnp.float32
    )
    attended = attended.astype(jnp.bfloat16).reshape(micro_count, tok_count, model_width)
    branch = matmul(attended, out_weight)
    return (
        stream + branch,
        (
            norm_back,
            normed_low,
            heads_query,
            key_ext,
            value_ext,
            row_peak + jnp.log(row_total),
            attended,
        ),
    )


def window_backward(grad_stream, residuals, weights, layout_info):
    norm_back, normed_low, heads_query, key_ext, value_ext, log_total, attended = residuals
    qkv_weight, out_weight = (weights[1], weights[2])
    micro_count, tok_count, model_width = grad_stream.shape
    head_size = model_width // HEADS
    grad_branch = grad_stream.astype(jnp.bfloat16)
    grad_out = (flat(attended), flat(grad_branch))
    grad_attended = (
        matmul_back(grad_branch, out_weight)
        .astype(jnp.bfloat16)
        .reshape(micro_count, tok_count, HEADS, head_size)
    )
    scores = window_scores(heads_query, key_ext, layout_info["window"], head_size)
    probabilities = jnp.exp(scores - log_total)
    grad_probs = jnp.einsum(
        "mihe,mjhe->mhij", grad_attended, value_ext, preferred_element_type=jnp.float32
    )
    grad_value_ext = jnp.einsum(
        "mhij,mihe->mjhe",
        probabilities.astype(jnp.bfloat16),
        grad_attended,
        preferred_element_type=jnp.float32,
    )
    inner_sum = jnp.sum(grad_probs * probabilities, axis=-1, keepdims=True)
    grad_scores = (probabilities * (grad_probs - inner_sum)).astype(jnp.bfloat16)
    score_scale = head_size ** (-0.5)
    grad_query = (
        jnp.einsum("mhij,mjhe->mihe", grad_scores, key_ext, preferred_element_type=jnp.float32)
        * score_scale
    )
    grad_key_ext = (
        jnp.einsum("mhij,mihe->mjhe", grad_scores, heads_query, preferred_element_type=jnp.float32)
        * score_scale
    )
    rim_grads = jnp.concatenate(
        [
            grad_key_ext[:, : WINDOW - 1].reshape(micro_count, WINDOW - 1, model_width),
            grad_value_ext[:, : WINDOW - 1].reshape(micro_count, WINDOW - 1, model_width),
        ],
        axis=-1,
    )
    returned = passed_along(rim_grads.astype(jnp.bfloat16), "ctx", -1).astype(rim_grads.dtype)
    own_grads = jnp.concatenate(
        [
            grad_key_ext[:, WINDOW - 1 :].reshape(micro_count, tok_count, model_width),
            grad_value_ext[:, WINDOW - 1 :].reshape(micro_count, tok_count, model_width),
        ],
        axis=-1,
    )
    own_grads = own_grads.at[:, tok_count - WINDOW + 1 :, :].add(returned)
    grad_qkv = jnp.concatenate(
        [grad_query.reshape(micro_count, tok_count, model_width), own_grads], axis=-1
    ).astype(jnp.bfloat16)
    grad_qkv_weight = (flat(normed_low), flat(grad_qkv))
    grad_input, grad_gain = norm_back(matmul_back(grad_qkv, qkv_weight))
    return (grad_stream + grad_input, (grad_gain, grad_qkv_weight, grad_out))


def ffn_forward(stream, weights):
    norm_gain, gate_up, down_weight = weights
    hidden_width = down_weight.shape[0]
    normed_rows, norm_back = jax.vjp(normed, stream, norm_gain.astype(jnp.float32))
    normed_low = normed_rows.astype(jnp.bfloat16)
    projected = matmul(normed_low, gate_up)
    hidden = (jax.nn.silu(projected[..., :hidden_width]) * projected[..., hidden_width:]).astype(
        jnp.bfloat16
    )
    branch = matmul(hidden, down_weight)
    return (stream + branch, (norm_back, normed_low, projected, hidden))


def ffn_backward(grad_stream, residuals, weights):
    norm_back, normed_low, projected, hidden = residuals
    gate_up, down_weight = (weights[1], weights[2])
    hidden_width = down_weight.shape[0]
    grad_branch = grad_stream.astype(jnp.bfloat16)
    grad_down = (flat(hidden), flat(grad_branch))
    grad_hidden = matmul_back(grad_branch, down_weight)
    gate_part = projected[..., :hidden_width]
    up_part = projected[..., hidden_width:]
    sigmoid_gate = jax.nn.sigmoid(gate_part)
    grad_gate = grad_hidden * up_part * sigmoid_gate * (1.0 + gate_part * (1.0 - sigmoid_gate))
    grad_up = grad_hidden * gate_part * sigmoid_gate
    grad_projected = jnp.concatenate([grad_gate, grad_up], axis=-1).astype(jnp.bfloat16)
    grad_gate_up = (flat(normed_low), flat(grad_projected))
    grad_input, grad_gain = norm_back(matmul_back(grad_projected, gate_up))
    return (grad_stream + grad_input, (grad_gain, grad_gate_up, grad_down))


def body(
    tokens_in,
    seq_lengths,
    norm_linear,
    proj_qk,
    proj_values,
    conv_taps,
    out_linear,
    norm_ffn_one,
    gate_up_one,
    down_one,
    norm_window,
    proj_qkv,
    out_window,
    norm_ffn_two,
    gate_up_two,
    down_two,
    cotangent,
):
    tok_count = tokens_in.shape[2]
    layout_info = layout(seq_lengths, tok_count)
    stream = tokens_in[:, 0].astype(jnp.float32)
    small = jnp.concatenate(
        [
            norm_linear[:, None],
            norm_ffn_one[:, None],
            norm_window[:, None],
            norm_ffn_two[:, None],
            conv_taps,
            jnp.zeros((conv_taps.shape[0], 121), jnp.bfloat16),
        ],
        axis=1,
    )
    shards = [
        small,
        proj_qk,
        proj_values,
        out_linear,
        gate_up_one,
        down_one,
        proj_qkv,
        out_window,
        gate_up_two,
        down_two,
    ]
    small, w_qk, w_values, w_out_linear, w_gu_one, w_dn_one, w_qkv, w_out_window, w_gu_two, w_dn_two = (
        gather_all(shards, lax.axis_size("dp"), lax.axis_size("ctx"), chunks_of(shards))
    )
    layer_one = (small[:, 0], w_qk, w_values, small[:, 4:7], w_out_linear, small[:, 1], w_gu_one, w_dn_one)
    layer_two = (small[:, 2], w_qkv, w_out_window, small[:, 3], w_gu_two, w_dn_two)
    middle, saved_linear = linear_forward(stream, layer_one[:5], layout_info)
    first_out, saved_ffn_one = ffn_forward(middle, layer_one[5:])
    second_mid, saved_window = window_forward(first_out, layer_two[:3], layout_info)
    closing, saved_ffn_two = ffn_forward(second_mid, layer_two[3:])
    valid_rows = layout_info["valid"][:, :, None]
    output = (closing * valid_rows).astype(jnp.bfloat16)[:, None]
    grad_stream = cotangent[:, 0].astype(jnp.float32) * valid_rows
    grad_stream, grads_ffn_two = ffn_backward(grad_stream, saved_ffn_two, layer_two[3:])
    grad_stream, grads_window = window_backward(
        grad_stream, saved_window, layer_two[:3], layout_info
    )
    grad_stream, grads_ffn_one = ffn_backward(grad_stream, saved_ffn_one, layer_one[5:])
    other_gains = jnp.stack([grads_ffn_one[0], grads_window[0], grads_ffn_two[0]], axis=1)
    grad_stream, of_qk, of_values, of_out, small = linear_backward(
        grad_stream, saved_linear, layer_one[:5], layout_info, other_gains
    )
    small, sums = summed_to_owners(
        [
            of_qk,
            of_values,
            of_out,
            grads_ffn_one[1],
            grads_ffn_one[2],
            grads_window[1],
            grads_window[2],
            grads_ffn_two[1],
            grads_ffn_two[2],
        ],
        small,
    )
    tokens_grad = grad_stream.astype(jnp.bfloat16)[:, None]
    return (
        output,
        tokens_grad,
        small[:, 0],
        sums[0],
        sums[1],
        small[:, 4:7],
        sums[2],
        small[:, 1],
        sums[3],
        sums[4],
        small[:, 2],
        sums[5],
        sums[6],
        small[:, 3],
        sums[7],
        sums[8],
    )


def solution(mesh):
    placed = (
        P(None, "dp", "ctx", None),
        P(None, "dp", None),
        P(("dp", "ctx")),
        P(("dp", "ctx"), None),
        P(("dp", "ctx"), None),
        P(("dp", "ctx"), None),
        P(("dp", "ctx"), None),
        P(("dp", "ctx")),
        P(("dp", "ctx"), None),
        P(("dp", "ctx"), None),
        P(("dp", "ctx")),
        P(("dp", "ctx"), None),
        P(("dp", "ctx"), None),
        P(("dp", "ctx")),
        P(("dp", "ctx"), None),
        P(("dp", "ctx"), None),
        P(None, "dp", "ctx", None),
    )
    return jax.shard_map(
        body,
        mesh=mesh,
        in_specs=placed,
        out_specs=(
            P(None, "dp", "ctx", None),
            P(None, "dp", "ctx", None),
            P(("dp", "ctx")),
            P(("dp", "ctx"), None),
            P(("dp", "ctx"), None),
            P(("dp", "ctx"), None),
            P(("dp", "ctx"), None),
            P(("dp", "ctx")),
            P(("dp", "ctx"), None),
            P(("dp", "ctx"), None),
            P(("dp", "ctx")),
            P(("dp", "ctx"), None),
            P(("dp", "ctx"), None),
            P(("dp", "ctx")),
            P(("dp", "ctx"), None),
            P(("dp", "ctx"), None),
        ),
        check_vma=False,
    )
```

```python
from functools import partial
import math

import jax
import jax.numpy as jnp
import numpy as np
from jax import lax
from jax.experimental import pallas as pl
from jax.experimental.pallas import tpu as pltpu
from jax.sharding import PartitionSpec as P

HEADS = 16
FEAT = 16
WINDOW = 64
CONV = 3


epsilon = 1e-05
masked_fill = -1e30
highest = lax.Precision.HIGHEST


MESH = pl.DeviceIdType.MESH

def carried(sign, n_ctx, dp, ctx, own, keep, out, came, total, sent, arrived):
    first, last = (0, n_ctx - 1) if sign > 0 else (n_ctx - 1, 0)
    low, f32 = jnp.bfloat16, jnp.float32
    planes, rows = own.shape[1:3]

    def copy(m):
        return pltpu.make_async_remote_copy(
            src_ref=total.at[m],
            dst_ref=came.at[m],
            send_sem=sent.at[m],
            recv_sem=arrived.at[m],
            device_id=(dp, lax.rem(ctx + sign + n_ctx, n_ctx)),
            device_id_type=MESH,
        )

    def act(m):
        @pl.when(ctx != first)
        def _():
            copy(m).wait_recv()
            for p in range(planes):
                value = came[m, p]
                out[m, p, :rows] = value
                total[m, p] = (own[m, p].astype(f32) + keep[m, 0:1] * value.astype(f32)).astype(low)

        @pl.when(ctx == first)
        def _():
            for p in range(planes):
                out[m, p, :rows] = jnp.zeros((rows, 128), low)
                total[m, p] = own[m, p]

        @pl.when(ctx != last)
        def _():
            copy(m).start()

    def finish():
        for m in range(own.shape[0]):
            for p in range(planes):
                out[m, p, rows:] = jnp.zeros((out.shape[2] - rows, 128), low)

        @pl.when(ctx != last)
        def _():
            for m in range(own.shape[0]):
                copy(m).wait_send()

    return act, finish


def carry_specs(state):
    whole = pl.BlockSpec(memory_space=pltpu.VMEM)
    shape = state.shape[:2] + (TERMS,) + state.shape[3:]
    held = pltpu.VMEM(state.shape, jnp.bfloat16)
    sems = pltpu.SemaphoreType.DMA((state.shape[0],))
    return [whole, whole], [whole], [jax.ShapeDtypeStruct(shape, jnp.bfloat16)], [held, held, sems, sems]


def gather_kernel(n_dp, n_ctx, chunks, lag, n_w, carry, *refs):
    n_c = 2 if carry else 0
    ins, outs = refs[:n_w], refs[n_w + n_c:2 * n_w + n_c]
    local_sem, send_sem, recv_sem = refs[2 * n_w + 3 * n_c // 2:][:3]
    dp, ctx = lax.axis_index("dp"), lax.axis_index("ctx")
    bits = [1 << i for i in range(n_dp.bit_length() - 1)]
    low_bits, (bit_x, bit_y) = bits[:-2], bits[-2:]
    barrier = pltpu.get_barrier_semaphore()
    greeted = 0
    for bit in bits:
        pl.semaphore_signal(barrier, inc=1, device_id=(dp ^ bit, ctx), device_id_type=MESH)
        greeted += 1
    for hop in range(1, n_ctx):
        pl.semaphore_signal(barrier, inc=1, device_id=(dp, lax.rem(ctx + hop, n_ctx)), device_id_type=MESH)
        greeted += 1
    pl.semaphore_wait(barrier, greeted)
    sends = []

    def piece(c, start, shards):
        w, col, width = chunks[c]
        return outs[w].at[pl.ds(start, shards), :, pl.ds(col, width)]

    def send(c, slot, start, rows, target, src=None):
        where = piece(c, start, rows)
        copy = pltpu.make_async_remote_copy(
            src_ref=where if src is None else src, dst_ref=where,
            send_sem=send_sem.at[c, slot], recv_sem=recv_sem.at[c, slot],
            device_id=target, device_id_type=MESH)
        copy.start()
        sends.append(copy)

    def arrive(c, slot, start, rows):
        where = piece(c, start, rows)
        pltpu.make_async_remote_copy(
            src_ref=where, dst_ref=where, send_sem=send_sem.at[c, slot], recv_sem=recv_sem.at[c, slot],
            device_id=(dp ^ 1, ctx), device_id_type=MESH).wait_recv()

    def stage_ctx(c):
        w, col, width = chunks[c]
        own = ins[w].at[:, :, pl.ds(col, width)]
        start = dp * n_ctx + ctx
        for hop in range(1, n_ctx):
            send(c, hop - 1, start, 1, (dp, lax.rem(ctx + hop, n_ctx)), src=own)
        pltpu.make_async_copy(own, piece(c, start, 1), local_sem.at[c]).start()

    base = n_ctx - 1
    SX, SY, SDX, SDY, SC = base, base + 1, base + 2, base + 3, base + 4

    def stage_sides(c):
        w, col, width = chunks[c]
        for hop in range(1, n_ctx):
            arrive(c, hop - 1, dp * n_ctx + lax.rem(ctx - hop + n_ctx, n_ctx), 1)
        own = ins[w].at[:, :, pl.ds(col, width)]
        pltpu.make_async_copy(own, piece(c, dp * n_ctx + ctx, 1), local_sem.at[c]).wait()
        group = n_ctx
        send(c, SX, dp * group, group, (dp ^ bit_x, ctx))
        send(c, SY, dp * group, group, (dp ^ bit_y, ctx))

    def stage_diag(c):
        group = n_ctx
        a0, an, b0, bn = 0, n_ctx // 2, n_ctx // 2, n_ctx - n_ctx // 2
        arrive(c, SX, (dp ^ bit_x) * group, group)
        send(c, SDY, (dp ^ bit_x) * group + a0, an, (dp ^ bit_y, ctx))
        arrive(c, SY, (dp ^ bit_y) * group, group)
        send(c, SDX, (dp ^ bit_y) * group + b0, bn, (dp ^ bit_x, ctx))

    def low_slot(level, j):
        return SC + 4 * ((1 << level) - 1) + j

    def quads(base_dp, level):
        out = []
        for top in range(4):
            for low in range(1 << level):
                flip = (bit_x if top & 1 else 0) | (bit_y if top & 2 else 0)
                for i in range(level):
                    if low >> i & 1:
                        flip |= low_bits[len(low_bits) - 1 - i]
                out.append(base_dp ^ flip)
        return out

    def stage_low(c, level):
        group = n_ctx
        if level == 0:
            a0, an, b0, bn = 0, n_ctx // 2, n_ctx // 2, n_ctx - n_ctx // 2
            arrive(c, SDY, (dp ^ bit_x ^ bit_y) * group + a0, an)
            arrive(c, SDX, (dp ^ bit_x ^ bit_y) * group + b0, bn)
        else:
            bit = low_bits[len(low_bits) - level]
            for j, block in enumerate(quads(dp ^ bit, level - 1)):
                arrive(c, low_slot(level - 1, j), block * group, group)
        if level < len(low_bits):
            bit = low_bits[len(low_bits) - 1 - level]
            for j, block in enumerate(quads(dp, level)):
                send(c, low_slot(level, j), block * group, group, (dp ^ bit, ctx))

    stages = [stage_ctx, stage_sides, stage_diag] + [partial(stage_low, level=l) for l in range(len(low_bits) + 1)]
    depth = len(stages)
    turns = len(chunks) + (depth - 1) * lag
    due = {}
    if carry:
        own, keep = refs[n_w:n_w + 2]
        act, finish = carried(carry, n_ctx, dp, ctx, own, keep, refs[2 * n_w + 2], *refs[2 * n_w + 6:])
        micro = own.shape[0]
        for n in range(n_ctx * micro):
            due.setdefault(n * turns // (n_ctx * micro), []).append((n // micro, n % micro))
    for t in range(turns):
        for place, m in due.get(t, []):
            @pl.when(ctx == (place if carry > 0 else n_ctx - 1 - place))
            def _():
                act(m)
        for s in range(depth):
            c = t - s * lag
            if 0 <= c < len(chunks):
                stages[s](c)
    if carry:
        finish()
    for copy in sends:
        copy.wait_send()

def gather_all(weights, n_dp, n_ctx, chunks, lag=1, cid=0, carry=0, state=()):
    n = len(weights)
    places = n_dp * n_ctx
    slots = n_ctx - 1 + 4 + 4 * (n_dp // 4 - 1)
    more_in, more_out, more_shape, more_scratch = carry_specs(state[0]) if carry else ([], [], [], [])
    full = pl.pallas_call(
        partial(gather_kernel, n_dp, n_ctx, chunks, lag, n, carry),
        out_shape=[jax.ShapeDtypeStruct((places,) + w.shape, w.dtype) for w in weights] + more_shape,
        in_specs=[pl.BlockSpec(memory_space=pltpu.HBM)] * n + more_in,
        out_specs=[pl.BlockSpec(memory_space=pltpu.HBM)] * n + more_out,
        scratch_shapes=[pltpu.SemaphoreType.DMA((len(chunks),)), pltpu.SemaphoreType.DMA((len(chunks), slots)), pltpu.SemaphoreType.DMA((len(chunks), slots))]
        + more_scratch,
        compiler_params=pltpu.CompilerParams(collective_id=cid, has_side_effects=True),
        name="gather_weights")(*[w[None] for w in weights], *state)
    return [f.reshape(places * f.shape[1], f.shape[2]) for f in full[:n]] + list(full[n:])


WIDE = 512
SLOTS_HELD = 8


def scatter_kernel(n_dp, n_ctx, plan, lags, n_x, n_y, n_o, carry, *refs):
    xs, ys, refs = refs[:n_x], refs[n_x : n_x + n_y], refs[n_x + n_y :]
    state, refs = (refs[:2], refs[2:]) if carry else ((), refs)
    outs, refs = refs[:n_o], refs[n_o:]
    state_out, refs = (refs[:1], refs[1:]) if carry else ((), refs)
    bits = [1 << i for i in range(n_dp.bit_length() - 1)]
    low_bits, (bit_x, bit_y) = bits[:-2], bits[-2:]
    n_low = len(low_bits)
    x_all, y_all = refs[0], refs[1]
    low_out, low_in = refs[2 : 2 + n_low], refs[2 + n_low : 2 + 2 * n_low]
    refs = refs[2 + 2 * n_low :]
    cross, cross_y, cross_x, side_x, side_y, came_x, came_y, shards, came_ctx, result = refs[:10]
    x_sem, y_sem, out_sem, sent, arrived, credit = refs[10:16]
    held = y_all.shape[0]
    dp, ctx = lax.axis_index("dp"), lax.axis_index("ctx")
    group = cross.shape[1]
    half = group // 2
    rows = group // n_ctx
    f32, low = jnp.float32, jnp.bfloat16
    A_CY, A_CX, A_X, A_Y, A_Z = n_low, n_low + 1, n_low + 2, n_low + 3, n_low + 4
    C_X, C_Y, C_Z = n_low, n_low + 1, n_low + 2

    def at_ctx(hop):
        return (dp, lax.rem(ctx + hop, n_ctx))

    barrier = pltpu.get_barrier_semaphore()
    for bit in bits:
        pl.semaphore_signal(barrier, inc=1, device_id=(dp ^ bit, ctx), device_id_type=MESH)
    for hop in range(1, n_ctx):
        pl.semaphore_signal(barrier, inc=1, device_id=at_ctx(hop), device_id_type=MESH)
    pl.semaphore_wait(barrier, len(bits) + n_ctx - 1)

    bounds, count = [], 0
    for segment in plan:
        bounds.append((count, count + segment[5]))
        count += segment[5]
    x_first = [None] * n_x
    for segment, (first, _) in zip(plan, bounds):
        if x_first[segment[0]] is None:
            x_first[segment[0]] = first

    def x_copy(i):
        return pltpu.make_async_copy(xs[i], x_all.at[i], x_sem.at[i])

    for i in range(n_x):
        x_copy(i).start()

    def y_start(c):
        slot = lax.rem(c, held)
        for segment, (first, last) in zip(plan, bounds):

            @pl.when((c >= first) & (c < last))
            def _():
                where = pl.multiple_of((c - first) * WIDE, WIDE)
                pltpu.make_async_copy(
                    ys[segment[1]].at[:, pl.ds(where, WIDE)], y_all.at[slot], y_sem.at[slot]
                ).start()

    def x_place(c):
        return sum((c >= first).astype(jnp.int32) for first in x_first[1:])

    def partial_sum(c, flip):
        return jnp.dot(
            x_all[x_place(c), dp ^ flip], y_all[lax.rem(c, held)], preferred_element_type=f32
        )

    def rest(level):
        free = low_bits[level + 1 :] + [bit_x, bit_y]
        return [sum(b for i, b in enumerate(free) if n >> i & 1) for n in range(1 << len(free))]

    def summed(c, flip, levels):
        total = partial_sum(c, flip)
        for level in range(levels):
            total = total + low_in[level][lax.rem(c, held), rest(level).index(flip)].astype(f32)
        return total

    def remote(src, dst, slot, kind, target):
        return pltpu.make_async_remote_copy(
            src_ref=src,
            dst_ref=dst,
            send_sem=sent.at[slot, kind],
            recv_sem=arrived.at[slot, kind],
            device_id=target,
            device_id_type=MESH,
        )

    def copy_of(slot, kind):
        over_x, over_y = (dp ^ bit_x, ctx), (dp ^ bit_y, ctx)
        if kind < n_low:
            return remote(
                low_out[kind].at[slot], low_in[kind].at[slot], slot, kind, (dp ^ low_bits[kind], ctx)
            )
        if kind == A_CY:
            return remote(cross.at[slot, pl.ds(0, half)], cross_y.at[slot], slot, kind, over_y)
        if kind == A_CX:
            return remote(cross.at[slot, pl.ds(half, half)], cross_x.at[slot], slot, kind, over_x)
        if kind == A_X:
            return remote(side_x.at[slot], came_x.at[slot], slot, kind, over_x)
        if kind == A_Y:
            return remote(side_y.at[slot], came_y.at[slot], slot, kind, over_y)
        hop = kind - A_Z + 1
        there = lax.rem(ctx + hop, n_ctx)
        return remote(shards.at[slot, there], came_ctx.at[slot, hop - 1], slot, kind, (dp, there))

    def need_credit(c, kind):
        @pl.when(c >= held)
        def _():
            pl.semaphore_wait(credit.at[kind], 1)

    def step_low(level, c):
        slot = lax.rem(c, held)
        if level == 0:
            for i, first in enumerate(x_first):

                @pl.when(c == first)
                def _():
                    x_copy(i).wait()

            pltpu.make_async_copy(ys[0].at[:, pl.ds(0, WIDE)], y_all.at[slot], y_sem.at[slot]).wait()
        else:
            copy_of(slot, level - 1).wait_recv()
        need_credit(c, level)
        for j, flip in enumerate(rest(level)):
            low_out[level][slot, j] = summed(c, flip | low_bits[level], level).astype(low)
        copy_of(slot, level).start()

    def step_cross(c):
        slot = lax.rem(c, held)
        if n_low:
            copy_of(slot, n_low - 1).wait_recv()
        need_credit(c, C_X)
        need_credit(c, C_Y)
        cross[slot] = summed(c, bit_x | bit_y, n_low).astype(low)
        copy_of(slot, A_CY).start()
        copy_of(slot, A_CX).start()

    def step_sides(c):
        slot = lax.rem(c, held)
        over_x = summed(c, bit_x, n_low)
        over_y = summed(c, bit_y, n_low)
        copy_of(slot, A_CY).wait_recv()
        side_x[slot, :half] = (over_x[:half] + cross_y[slot].astype(f32)).astype(low)
        side_x[slot, half:] = over_x[half:].astype(low)
        copy_of(slot, A_X).start()
        copy_of(slot, A_CX).wait_recv()
        side_y[slot, :half] = over_y[:half].astype(low)
        side_y[slot, half:] = (over_y[half:] + cross_x[slot].astype(f32)).astype(low)
        copy_of(slot, A_Y).start()

    def step_own(c):
        slot = lax.rem(c, held)
        total = summed(c, 0, n_low)
        copy_of(slot, A_X).wait_recv()
        copy_of(slot, A_Y).wait_recv()
        total = total + came_x[slot].astype(f32) + came_y[slot].astype(f32)
        for j in range(n_ctx):
            shards[slot, j] = total[j * rows : (j + 1) * rows].astype(low)
        for hop in range(1, n_ctx):
            need_credit(c, C_Z + hop - 1)
            copy_of(slot, A_Z + hop - 1).start()

    def out_copy(c, slot, segment, first):
        where = pl.multiple_of((c - first) * WIDE, WIDE)
        _, _, o, row, n_rows, _ = segment
        return pltpu.make_async_copy(
            result.at[slot, pl.ds(0, n_rows)],
            outs[o].at[pl.ds(row, n_rows), pl.ds(where, WIDE)],
            out_sem.at[slot],
        )

    def each_segment(c, act):
        for segment, (first, last) in zip(plan, bounds):

            @pl.when((c >= first) & (c < last))
            def _():
                act(segment, first)

    def out_wait(c):
        slot = lax.rem(c, held)
        each_segment(c, lambda segment, first: out_copy(c, slot, segment, first).wait())

    def step_end(c):
        slot = lax.rem(c, held)

        @pl.when(c >= held)
        def _():
            out_wait(c - held)

        total = shards[slot, ctx].astype(f32)
        for hop in range(1, n_ctx):
            copy_of(slot, A_Z + hop - 1).wait_recv()
            total = total + came_ctx[slot, hop - 1].astype(f32)
        result[slot] = total
        each_segment(c, lambda segment, first: out_copy(c, slot, segment, first).start())
        for kind in range(A_Z + n_ctx - 1):
            copy_of(slot, kind).wait_send()

        @pl.when(c + held < count)
        def _():
            for level, bit in enumerate(low_bits):
                pl.semaphore_signal(credit.at[level], inc=1, device_id=(dp ^ bit, ctx), device_id_type=MESH)
            pl.semaphore_signal(credit.at[C_X], inc=1, device_id=(dp ^ bit_x, ctx), device_id_type=MESH)
            pl.semaphore_signal(credit.at[C_Y], inc=1, device_id=(dp ^ bit_y, ctx), device_id_type=MESH)
            for hop in range(1, n_ctx):
                pl.semaphore_signal(
                    credit.at[C_Z + hop - 1], inc=1, device_id=at_ctx(n_ctx - hop), device_id_type=MESH
                )

    steps = [partial(step_low, level) for level in range(n_low)] + [step_cross, step_sides, step_own, step_end]
    ahead = 2
    for c in range(ahead):
        y_start(jnp.int32(c))

    turns = count + lags[-1]
    if carry:
        act, finish = carried(carry, n_ctx, dp, ctx, *state, *state_out, *refs[16:])
        micro = state[0].shape[0]
        stride = turns // (n_ctx * micro)
        place = ctx if carry > 0 else n_ctx - 1 - ctx

    def turn(t, none):
        if carry:
            for m in range(micro):

                @pl.when(t == (place * micro + m) * stride)
                def _():
                    act(m)

        @pl.when(t + ahead < count)
        def _():
            y_start(t + ahead)

        for step, lag in zip(steps, lags):
            c = t - lag

            @pl.when((c >= 0) & (c < count))
            def _():
                step(c)

        return none

    lax.fori_loop(0, turns, turn, 0)
    if carry:
        finish()
    for c in range(max(0, count - held), count):
        out_wait(jnp.int32(c))


def scatter_sums(xs, ys, out_shapes, plan, n_dp, n_ctx, cid=1, carry=0, state=(), lags=None, held=SLOTS_HELD):
    group, tokens = xs[0].shape[1:]
    n_low = n_dp.bit_length() - 3
    rows = group // n_ctx
    low, f32 = jnp.bfloat16, jnp.float32
    lags = lags or list(range(n_low + 4))
    low_shapes = [
        pltpu.VMEM((held, n_dp >> (level + 1), group, WIDE), low) for level in range(n_low)
    ]
    half = group // 2
    kinds = n_low + 4 + n_ctx - 1
    more_in, more_out, more_shape, more_scratch = carry_specs(state[0]) if carry else ([], [], [], [])
    return pl.pallas_call(
        partial(scatter_kernel, n_dp, n_ctx, plan, lags, len(xs), len(ys), len(out_shapes), carry),
        out_shape=[jax.ShapeDtypeStruct(shape, f32) for shape in out_shapes] + more_shape,
        in_specs=[pl.BlockSpec(memory_space=pl.ANY)] * (len(xs) + len(ys)) + more_in,
        out_specs=[pl.BlockSpec(memory_space=pltpu.HBM)] * len(out_shapes) + more_out,
        scratch_shapes=[
            pltpu.VMEM((len(xs),) + xs[0].shape, low),
            pltpu.VMEM((held, tokens, WIDE), low),
            *low_shapes,
            *low_shapes,
            pltpu.VMEM((held, group, WIDE), low),
            pltpu.VMEM((held, half, WIDE), low),
            pltpu.VMEM((held, half, WIDE), low),
            pltpu.VMEM((held, group, WIDE), low),
            pltpu.VMEM((held, group, WIDE), low),
            pltpu.VMEM((held, group, WIDE), low),
            pltpu.VMEM((held, group, WIDE), low),
            pltpu.VMEM((held, n_ctx, rows, WIDE), low),
            pltpu.VMEM((held, n_ctx - 1, rows, WIDE), low),
            pltpu.VMEM((held, rows, WIDE), f32),
            pltpu.SemaphoreType.DMA((len(xs),)),
            pltpu.SemaphoreType.DMA((held,)),
            pltpu.SemaphoreType.DMA((held,)),
            pltpu.SemaphoreType.DMA((held, kinds)),
            pltpu.SemaphoreType.DMA((held, kinds)),
            pltpu.SemaphoreType.REGULAR((n_low + 2 + n_ctx - 1,)),
            *more_scratch,
        ],
        compiler_params=pltpu.CompilerParams(
            collective_id=cid, has_side_effects=True, vmem_limit_bytes=56 * 2**20
        ),
        name="scatter_sums",
    )(*xs, *ys, *state)


def passed_along(value, axis, steps):
    count = lax.axis_size(axis)
    leading, last = (max(0, -steps), min(count, count - steps))
    return lax.ppermute(value, axis, [(source, source + steps) for source in range(leading, last)])


TERMS = 256
SENT = 160
PER = 2


def feature_tables():
    first = np.zeros((FEAT, TERMS), np.float32)
    second = np.zeros((FEAT, TERMS), np.float32)
    base = np.zeros((8, TERMS), np.float32)
    base[0, 0] = base[1, 0] = base[2, 0] = 1.0
    column = 1
    for f in range(FEAT):
        first[f, column] = base[1, column] = 1.0
        base[2, column] = 1.0 / math.sqrt(FEAT)
        column += 1
    for f in range(FEAT):
        for g in range(f, FEAT):
            first[f, column] = second[g, column] = 1.0
            base[2, column] = (0.5 if f == g else 1.0) / FEAT
            column += 1
    tile = np.stack([np.tile(first, (HEADS, 1)), np.tile(second, (HEADS, 1))])
    return jnp.asarray(tile, jnp.bfloat16), jnp.asarray(base)


def dot_nn(a, b):
    return jnp.dot(a, b, preferred_element_type=jnp.float32)


def dot_nt(a, b):
    return lax.dot_general(a, b, (((1,), (1,)), ((), ())), preferred_element_type=jnp.float32)


def dot_tn(a, b):
    return lax.dot_general(a, b, (((0,), (0,)), ((), ())), preferred_element_type=jnp.float32)


def lanes_of(shape, size):
    return lax.broadcasted_iota(jnp.int32, shape, len(shape) - 1) // size


def only(mask, value):
    return jnp.where(mask, value, jnp.zeros_like(value))


def pairs_of(step):
    return [(step * PER + n, slice(128 * n, 128 * (n + 1))) for n in range(PER)]


def factors(rows, tables, base):
    return (dot_nn(rows, tables[0]) + base[0:1], dot_nn(rows, tables[1]) + base[1:2])


def states_kernel(key_ref, value_ref, last_ref, table_ref, base_ref, state_ref):
    step = pl.program_id(1)
    low, f32 = jnp.bfloat16, jnp.float32
    keys = key_ref[0]
    last = last_ref[0]
    head_of = lanes_of(keys.shape, FEAT)
    lane = lanes_of((SENT, 128), 1)
    totals = state_ref[0, HEADS // 2]
    totals = jnp.where(step == 0, jnp.zeros_like(totals), totals)
    for pair, here in pairs_of(step):
        values = value_ref[0, :, here].astype(f32)
        held = jnp.concatenate([(values * last).astype(low), last.astype(low)], axis=1)
        both = []
        for side in range(2):
            head = 2 * pair + side
            one, two = factors(only(head_of == head, keys), table_ref, base_ref)
            part = dot_tn((one * two).astype(low), held)[:SENT]
            both.append(part[:, :128])
            totals = jnp.where(lane == head, part[:, 128:].astype(low), totals)
        state_ref[0, pair] = jnp.where(lane < 64, both[0], both[1]).astype(low)
    state_ref[0, HEADS // 2] = totals


def attend_kernel(
    query_ref, key_ref, value_ref, state_ref, mask_ref, carried_ref, table_ref, base_ref, out_ref, den_ref
):
    step = pl.program_id(1)
    low, f32 = jnp.bfloat16, jnp.float32
    queries, keys = query_ref[0], key_ref[0]
    mask, carried = mask_ref[0], carried_ref[0][:, :1]
    totals = state_ref[0, HEADS // 2]
    head_of = lanes_of(queries.shape, FEAT)
    lane = lanes_of(totals.shape, 1)
    for pair, here in pairs_of(step):
        state = state_ref[0, pair]
        values = value_ref[0, :, here]
        held = jnp.concatenate([values, jnp.ones_like(values)], axis=1)
        outs, dens = [], []
        for side in range(2):
            head = 2 * pair + side
            own = only(head_of == head, queries)
            score = dot_nt(own, keys) * (1.0 / math.sqrt(FEAT))
            weight = ((1.0 + score + 0.5 * score * score) * mask).astype(low)
            one, two = factors(own, table_ref, base_ref)
            terms = (one * two * base_ref[2:3] * carried).astype(low)
            total = jnp.sum(only(lane == head, totals.astype(f32)), axis=1, keepdims=True)
            total = jnp.broadcast_to(total, totals.shape).astype(low)
            result = dot_nn(weight, held) + dot_nn(terms, jnp.concatenate([state, total], axis=1))
            outs.append(result[:, :128] / result[:, 128:])
            dens.append(result[:, 128:])
        first = lanes_of(outs[0].shape, 64) == 0
        out_ref[0, :, here] = jnp.where(first, outs[0], outs[1]).astype(low)
        den_ref[0, :, here] = jnp.where(first, dens[0], dens[1])


def attend_back_kernel(
    query_ref, key_ref, value_ref, state_ref, mask_ref, carried_ref, table_ref, base_ref, grad_ref, out_ref,
    den_ref, dquery_ref, dkey_ref, dvalue_ref, dstate_ref,
):
    step = pl.program_id(1)
    low, f32 = jnp.bfloat16, jnp.float32
    queries, keys = query_ref[0], key_ref[0]
    mask, carried = mask_ref[0], carried_ref[0][:, :1]
    totals = state_ref[0, HEADS // 2]
    head_of = lanes_of(queries.shape, FEAT)
    lane = lanes_of(value_ref.shape[1:2] + (128,), 1)
    dquery = jnp.zeros(queries.shape, f32)
    dkey = jnp.zeros(queries.shape, f32)
    dtotals = dstate_ref[0, HEADS // 2]
    dtotals = jnp.where(step == 0, jnp.zeros_like(dtotals), dtotals)
    inv_root = 1.0 / math.sqrt(FEAT)
    for pair, here in pairs_of(step):
        values = value_ref[0, :, here]
        whole_state = jnp.concatenate([state_ref[0, pair], totals], axis=1)
        dnum = grad_ref[0, :, here] / den_ref[0, :, here]
        inner = dnum * out_ref[0, :, here].astype(f32)
        dvalue = jnp.zeros(dnum.shape, f32)
        dstate = jnp.zeros((SENT, 128), f32)
        for side in range(2):
            head = 2 * pair + side
            own_lanes = (lane < 64) if side == 0 else (lane >= 64)
            own, own_keys = only(head_of == head, queries), only(head_of == head, keys)
            dnum_own = only(own_lanes, dnum).astype(low)
            dden = -jnp.sum(only(own_lanes, inner), axis=1, keepdims=True)
            score = dot_nt(own, keys) * inv_root
            slope = (1.0 + score) * mask
            weight = ((1.0 + score + 0.5 * score * score) * mask).astype(low)
            dscore = ((dot_nt(dnum_own, values) + dden) * slope * inv_root).astype(low)
            dvalue += dot_tn(weight, dnum_own)
            dquery += dot_nn(dscore, own_keys)
            dkey += dot_tn(dscore, own)
            one, two = factors(own, table_ref, base_ref)
            scale = base_ref[2:3] * carried
            terms = (one * two * scale).astype(low)
            dden_all = jnp.broadcast_to(dden, dnum.shape)
            part = dot_tn(terms, jnp.concatenate([dnum_own, dden_all.astype(low)], axis=1))[:SENT]
            dstate += part[:, :128]
            dtotals = jnp.where(lanes_of(dtotals.shape, 1) == head, part[:, 128:].astype(low), dtotals)
            both = jnp.concatenate([dnum_own, only(lane == head, dden_all).astype(low)], axis=1)
            dterms = dot_nt(both, whole_state) * scale
            through = dot_nt((dterms * two).astype(low), table_ref[0])
            through += dot_nt((dterms * one).astype(low), table_ref[1])
            dquery += only(head_of == head, through)
        dvalue_ref[0, :, here] = dvalue
        dstate_ref[0, pair] = dstate.astype(low)
    dstate_ref[0, HEADS // 2] = dtotals

    @pl.when(step == 0)
    def _():
        dquery_ref[0] = dquery
        dkey_ref[0] = dkey

    @pl.when(step != 0)
    def _():
        dquery_ref[0] += dquery
        dkey_ref[0] += dkey


def states_back_kernel(
    key_ref, value_ref, last_ref, table_ref, base_ref, dstate_ref, dkey_in, dvalue_in, dkey_ref, dvalue_ref
):
    step = pl.program_id(1)
    low, f32 = jnp.bfloat16, jnp.float32
    keys = key_ref[0]
    last = last_ref[0]
    dtotals = dstate_ref[0, HEADS // 2]
    head_of = lanes_of(keys.shape, FEAT)
    lane = lanes_of(last.shape, 1)
    dkey = jnp.zeros(keys.shape, f32)
    for pair, here in pairs_of(step):
        values = value_ref[0, :, here]
        dstate = dstate_ref[0, pair]
        whole = jnp.concatenate([dstate, dtotals], axis=1)
        dvalue = dvalue_in[0, :, here]
        for side in range(2):
            head = 2 * pair + side
            own_lanes = (lane < 64) if side == 0 else (lane >= 64)
            one, two = factors(only(head_of == head, keys), table_ref, base_ref)
            terms = (one * two).astype(low)
            dvalue += only(own_lanes, dot_nn(terms, dstate)) * last
            both = jnp.concatenate([only(own_lanes, values), (lane == head).astype(low)], axis=1)
            dterms = dot_nt(both, whole) * last[:, :1]
            through = dot_nt((dterms * two).astype(low), table_ref[0])
            through += dot_nt((dterms * one).astype(low), table_ref[1])
            dkey += only(head_of == head, through)
        dvalue_ref[0, :, here] = dvalue

    @pl.when(step == 0)
    def _():
        dkey_ref[0] = dkey_in[0] + dkey

    @pl.when(step != 0)
    def _():
        dkey_ref[0] += dkey


def by_pair(kernel, name, ins, outs):
    def spec(kind, shape):
        if kind == "query":
            return pl.BlockSpec((1, shape[1], HEADS * FEAT), lambda m, p: (m, 0, 0))
        if kind == "key":
            return pl.BlockSpec((1, shape[1], HEADS * FEAT), lambda m, p: (m, 0, 1))
        if kind == "pair":
            return pl.BlockSpec((1, shape[1], PER * 128), lambda m, p: (m, 0, p))
        if kind == "micro":
            return pl.BlockSpec((1,) + shape[1:], lambda m, p: (m,) + (0,) * (len(shape) - 1))
        return pl.BlockSpec(shape, lambda m, p: (0,) * len(shape))

    return pl.pallas_call(
        kernel,
        grid=(ins[0][0].shape[0], HEADS // 2 // PER),
        in_specs=[spec(kind, array.shape) for array, kind in ins],
        out_specs=[spec(kind, shape) for shape, _, kind in outs],
        out_shape=[jax.ShapeDtypeStruct(shape, dtype) for shape, dtype, _ in outs],
        compiler_params=pltpu.CompilerParams(vmem_limit_bytes=48 * 2**20),
        name=name,
    )(*[array for array, _ in ins])


def chunk_plan(products, unit):
    places, n_dp = lax.axis_size("dp") * lax.axis_size("ctx"), lax.axis_size("dp")
    laid, first_laid, plan, shapes = [], {}, [], []
    for number, (operand, gradient) in enumerate(products):
        tokens, rows = operand.shape
        shard = rows // places
        shapes.append((shard, gradient.shape[1]))
        if id(operand) not in first_laid:
            first_laid[id(operand)] = len(laid)
            turned = operand.T.reshape(places, shard, tokens)
            for first in range(0, shard, unit):
                piece = turned[:, first : first + unit]
                piece = jnp.pad(piece, ((0, 0), (0, unit - piece.shape[1]), (0, 0)))
                laid.append(piece.reshape(n_dp, -1, tokens))
        for piece, first in enumerate(range(0, shard, unit)):
            plan.append(
                (
                    first_laid[id(operand)] + piece,
                    number,
                    number,
                    first,
                    min(unit, shard - first),
                    gradient.shape[1] // WIDE,
                )
            )
    return laid, plan, shapes


def as_product(small):
    rows, few = small.shape
    high = small.astype(jnp.bfloat16)
    rest = (small - high.astype(jnp.float32)).astype(jnp.bfloat16)

    def product(tokens):
        both = jnp.zeros((tokens, rows), jnp.bfloat16).at[:few].set(high.T).at[few : 2 * few].set(rest.T)
        pick = np.zeros((tokens, WIDE), np.float32)
        pick[:few, :few] = pick[few : 2 * few, :few] = np.eye(few)
        return both, jnp.asarray(pick, jnp.bfloat16)

    return product


def summed_to_owners(products, cid, unit, carry=0, state=()):
    n_dp, n_ctx = lax.axis_size("dp"), lax.axis_size("ctx")
    laid, plan, shapes = chunk_plan(products, unit)
    gradients = [gradient for _, gradient in products]
    return scatter_sums(laid, gradients, shapes, plan, n_dp, n_ctx, cid, carry, state)


def chunks_of(shards):
    out = []
    for place, shard in enumerate(shards):
        rows, columns = shard.shape
        unit = max(128, 1408 * 32 // rows // 128 * 128)
        width = -(-(columns // 128) // -(-columns // unit)) * 128
        for first in range(0, columns, width):
            out.append((place, first, min(width, columns - first)))
    return out


def flat(value):
    return value.reshape(-1, value.shape[-1])


def normed(stream, scale_gain):
    return (
        stream * lax.rsqrt(jnp.mean(stream * stream, axis=-1, keepdims=True) + epsilon) * scale_gain
    )


def matmul(operand, weight):
    return jnp.einsum("mtd,de->mte", operand, weight, preferred_element_type=jnp.float32)


def matmul_back(operand, weight):
    return jnp.einsum("mte,de->mtd", operand, weight, preferred_element_type=jnp.float32)


def weight_grad(operand, gradient):
    return jnp.einsum("mtd,mte->de", operand, gradient, preferred_element_type=jnp.float32)


def layout(seq_lengths, tok_count):
    seq_ends = jnp.cumsum(seq_lengths[:, 0, :], axis=-1, dtype=jnp.int32)
    first_pos = lax.axis_index("ctx") * tok_count

    def segment_of(positions):
        return jnp.sum(
            (positions[None, :, None] >= seq_ends[:, None, :]).astype(jnp.int32),
            axis=-1,
            dtype=jnp.int32,
        )

    own_pos = first_pos + jnp.arange(tok_count, dtype=jnp.int32)
    own_seg = segment_of(own_pos)
    before_seg = segment_of(own_pos - 1)

    def in_lanes(flag):
        return jnp.broadcast_to(flag[:, :, None].astype(jnp.float32), flag.shape + (128,))

    starts = (own_seg != before_seg) | (own_pos == 0)[None, :]
    keep = 1.0 - jnp.max(starts.astype(jnp.float32), axis=1)
    tap_masks = []
    for offset in range(CONV):
        source = own_pos - offset
        tap_masks.append(
            ((segment_of(source) == own_seg) & (source >= 0)[None, :]).astype(jnp.float32)
        )
    key_pos = first_pos - BAND + jnp.arange(tok_count + BAND, dtype=jnp.int32)
    key_seg = jnp.where(key_pos >= 0, segment_of(key_pos), -1)
    window_mask = []
    for first in range(0, tok_count, BAND):
        queries, keys = slice(first, first + BAND), slice(first, first + 2 * BAND)
        ahead = own_pos[queries][:, None] - key_pos[keys][None, :]
        same = own_seg[:, queries][:, :, None] == key_seg[:, keys][:, None, :]
        window_mask.append(((ahead >= 0) & (ahead < WINDOW))[None] & same)
    window_mask = jnp.concatenate(window_mask, axis=1).astype(jnp.float32)
    causal = (own_pos[:, None] >= own_pos[None, :])[None] & (
        own_seg[:, :, None] == own_seg[:, None, :]
    )
    return {
        "valid": (own_pos[None, :] < seq_ends[:, -1:]).astype(jnp.float32),
        "keep": jnp.broadcast_to(keep[:, None, None], keep.shape + (8, 128)),
        "carried": in_lanes((own_seg == before_seg[:, :1]) & (first_pos > 0)),
        "last": in_lanes(own_seg == own_seg[:, -1:]),
        "causal": causal.astype(jnp.float32),
        "taps": jnp.stack(tap_masks),
        "window": window_mask,
    }


def conv_gate(pre_values, rim_rows, tap_weights, tap_masks):
    tok_count = pre_values.shape[1]
    rim_width = rim_rows.shape[1]
    extended = jnp.concatenate([rim_rows, pre_values], axis=1)
    conv_sum = jnp.zeros_like(pre_values)
    for offset in range(rim_width + 1):
        shifted = extended[:, rim_width - offset : rim_width - offset + tok_count, :]
        conv_sum = conv_sum + tap_weights[:, offset] * shifted * tap_masks[offset][:, :, None]
    return conv_sum * jax.nn.silu(pre_values)


def linear_forward(stream, weights, layout_info, gather_more):
    norm_gain, qk_weight, value_weight, tap_weights = weights
    micro_count, tok_count, model_width = stream.shape
    normed_rows, norm_back = jax.vjp(normed, stream, norm_gain.astype(jnp.float32))
    normed_low = normed_rows.astype(jnp.bfloat16)
    qk_rows = matmul(normed_low, qk_weight).astype(jnp.bfloat16)
    pre_values = matmul(normed_low, value_weight)
    rim_rows = passed_along(pre_values[:, tok_count - CONV + 1 :, :], "ctx", 1)
    value_rows, conv_back = jax.vjp(
        partial(conv_gate, tap_masks=layout_info["taps"]),
        pre_values,
        rim_rows,
        tap_weights.astype(jnp.float32),
    )
    values = value_rows.astype(jnp.bfloat16)
    tables, base = feature_tables()
    state_shape = (micro_count, HEADS // 2 + 1, SENT, 128)
    (state,) = by_pair(
        states_kernel,
        "states",
        [(qk_rows, "key"), (values, "pair"), (layout_info["last"], "micro"), (tables, "whole"), (base, "whole")],
        [(state_shape, jnp.bfloat16, "micro")],
    )
    *more, state_in = gather_more((state, layout_info["keep"]))
    out_weight = more[0]
    shared = [
        (qk_rows, "query"),
        (qk_rows, "key"),
        (values, "pair"),
        (state_in, "micro"),
        (layout_info["causal"], "micro"),
        (layout_info["carried"], "micro"),
        (tables, "whole"),
        (base, "whole"),
    ]
    attended_low, den = by_pair(
        attend_kernel,
        "linear_attend",
        shared,
        [(values.shape, jnp.bfloat16, "pair"), (values.shape, jnp.float32, "pair")],
    )
    branch = matmul(attended_low, out_weight)
    return (
        stream + branch,
        (norm_back, normed_low, conv_back, shared, attended_low, den),
        more,
    )


def linear_backward(grad_stream, residuals, weights, layout_info, other_gains, sum_others):
    norm_back, normed_low, conv_back, shared, attended_low, den = residuals
    qk_weight, value_weight, out_weight = (weights[1], weights[2], weights[4])
    micro_count, tok_count, model_width = grad_stream.shape
    grad_branch = grad_stream.astype(jnp.bfloat16)
    grad_out = (flat(attended_low), flat(grad_branch))
    grad_attended = matmul_back(grad_branch, out_weight)
    f32, low = jnp.float32, jnp.bfloat16
    feat_shape = (micro_count, tok_count, HEADS * FEAT)
    state_shape = (micro_count, HEADS // 2 + 1, SENT, 128)
    grad_query, grad_key, grad_value, grad_state = by_pair(
        attend_back_kernel,
        "linear_attend_back",
        shared + [(grad_attended, "pair"), (attended_low, "pair"), (den, "pair")],
        [
            (feat_shape, f32, "micro"),
            (feat_shape, f32, "micro"),
            (grad_stream.shape, f32, "pair"),
            (state_shape, low, "micro"),
        ],
    )
    *sums, later = sum_others(grad_out, (grad_state, layout_info["keep"]))
    grad_key, grad_value = by_pair(
        states_back_kernel,
        "states_back",
        [shared[1], shared[2], (layout_info["last"], "micro"), shared[6], shared[7], (later, "micro")]
        + [(grad_key, "micro"), (grad_value, "pair")],
        [(feat_shape, f32, "micro"), (grad_stream.shape, f32, "pair")],
    )
    grad_qk = jnp.concatenate([grad_query, grad_key], axis=-1).astype(low)
    grad_pre, grad_rim, grad_taps = conv_back(grad_value)
    returned = passed_along(grad_rim, "ctx", -1)
    grad_pre = grad_pre.at[:, tok_count - CONV + 1 :, :].add(returned)
    grad_pre_low = grad_pre.astype(jnp.bfloat16)
    grad_normed = matmul_back(grad_qk, qk_weight) + matmul_back(grad_pre_low, value_weight)
    grad_input, grad_gain = norm_back(grad_normed)
    small = jnp.concatenate([grad_gain[:, None], other_gains, grad_taps], axis=1)
    operand = flat(normed_low)
    own = summed_to_owners(
        [
            as_product(small)(operand.shape[0]),
            (operand, flat(grad_qk)),
            (operand, flat(grad_pre_low)),
        ],
        3,
        model_width // (lax.axis_size("dp") * lax.axis_size("ctx")),
    )
    return (grad_stream + grad_input, own, sums)


BAND = 128
RIM = 64


def band_probabilities(queries, keys, mask):
    score = jnp.where(mask > 0, dot_nt(queries, keys) * 0.125, masked_fill)
    power = jnp.exp(score - jnp.max(score, axis=1, keepdims=True))
    return power / jnp.sum(power, axis=1, keepdims=True)


def band_attend(queries, keys, values, mask):
    lane = lanes_of(queries.shape, 1)
    outs = []
    for own in (lane < 64, lane >= 64):
        chance = band_probabilities(only(own, queries), keys, mask)
        outs.append(dot_nn(chance.astype(jnp.bfloat16), values))
    return jnp.where(lane < 64, outs[0], outs[1]).astype(jnp.bfloat16)


def band_back(queries, grads, keys, values, mask):
    low = jnp.bfloat16
    lane = lanes_of(queries.shape, 1)
    dqueries, dkeys, dvalues = [], 0.0, 0.0
    for own in (lane < 64, lane >= 64):
        own_queries, own_grads = only(own, queries), only(own, grads)
        chance = band_probabilities(own_queries, keys, mask)
        dchance = dot_nt(own_grads, values)
        inner = jnp.sum(dchance * chance, axis=1, keepdims=True)
        dscore = (chance * (dchance - inner)).astype(low)
        dqueries.append(dot_nn(dscore, keys) * 0.125)
        dkeys += dot_tn(dscore, own_queries) * 0.125
        dvalues += dot_tn(chance.astype(low), own_grads)
    return jnp.where(lane < 64, dqueries[0], dqueries[1]).astype(low), dkeys, dvalues


def with_rim(own_ref, rim_ref, here):
    own, rim = own_ref[0, :, here], rim_ref[0, :, here]
    return jnp.concatenate([jnp.zeros((BAND - RIM, 128), own.dtype), rim, own], axis=0)


def first_band_kernel(query_ref, key_ref, value_ref, rim_key_ref, rim_value_ref, mask_ref, out_ref):
    for _, here in pairs_of(0):
        keys, values = with_rim(key_ref, rim_key_ref, here), with_rim(value_ref, rim_value_ref, here)
        out_ref[0, :, here] = band_attend(query_ref[0, :, here], keys, values, mask_ref[0])


def later_bands_kernel(query_ref, key_ref, value_ref, mask_ref, out_ref):
    for _, here in pairs_of(0):
        for first in range(BAND, query_ref.shape[1], BAND):
            rows, near = slice(first, first + BAND), slice(first - BAND, first + BAND)
            out_ref[0, first - BAND : first, here] = band_attend(
                query_ref[0, rows, here], key_ref[0, near, here], value_ref[0, near, here], mask_ref[0, rows]
            )


def first_band_back_kernel(
    query_ref, key_ref, value_ref, rim_key_ref, rim_value_ref, mask_ref, grad_ref, dquery_ref, dkey_ref,
    dvalue_ref, drim_key_ref, drim_value_ref,
):
    for _, here in pairs_of(0):
        keys, values = with_rim(key_ref, rim_key_ref, here), with_rim(value_ref, rim_value_ref, here)
        dquery, dkey, dvalue = band_back(
            query_ref[0, :, here], grad_ref[0, :, here], keys, values, mask_ref[0]
        )
        dquery_ref[0, :, here] = dquery
        dkey_ref[0, :, here] = dkey[BAND:]
        dvalue_ref[0, :, here] = dvalue[BAND:]
        drim_key_ref[0, :, here] = dkey[BAND - RIM : BAND].astype(jnp.bfloat16)
        drim_value_ref[0, :, here] = dvalue[BAND - RIM : BAND].astype(jnp.bfloat16)


def later_bands_back_kernel(
    query_ref, key_ref, value_ref, mask_ref, grad_ref, first_dkey_ref, first_dvalue_ref, dquery_ref, dkey_ref,
    dvalue_ref,
):
    for _, here in pairs_of(0):
        dkey_ref[0, :BAND, here] = first_dkey_ref[0, :, here]
        dvalue_ref[0, :BAND, here] = first_dvalue_ref[0, :, here]
        for first in range(BAND, query_ref.shape[1], BAND):
            rows, before, near = (
                slice(first, first + BAND),
                slice(first - BAND, first),
                slice(first - BAND, first + BAND),
            )
            dquery, dkey, dvalue = band_back(
                query_ref[0, rows, here],
                grad_ref[0, rows, here],
                key_ref[0, near, here],
                value_ref[0, near, here],
                mask_ref[0, rows],
            )
            dquery_ref[0, before, here] = dquery
            dkey_ref[0, before, here] += dkey[:BAND]
            dvalue_ref[0, before, here] += dvalue[:BAND]
            dkey_ref[0, rows, here] = dkey[BAND:]
            dvalue_ref[0, rows, here] = dvalue[BAND:]


def by_window(kernel, name, ins, outs):
    micro, steps = ins[0][0].shape[0], HEADS // 2 // PER

    def spec(rows, place, width):
        if place is None:
            return pl.BlockSpec((1, rows, width), lambda m, p: (m, 0, 0))
        return pl.BlockSpec((1, rows, PER * 128), lambda m, p: (m, 0, p + place * steps))

    return pl.pallas_call(
        kernel,
        grid=(micro, steps),
        in_specs=[spec(rows, place, array.shape[2]) for array, rows, place in ins],
        out_specs=[spec(rows, 0, 0) for rows, _ in outs],
        out_shape=[jax.ShapeDtypeStruct((micro, rows, HEADS * 64), dtype) for rows, dtype in outs],
        compiler_params=pltpu.CompilerParams(vmem_limit_bytes=48 * 2**20),
        name=name,
    )(*[array for array, _, _ in ins])


def window_forward(stream, weights, layout_info):
    norm_gain, qkv_weight, out_weight = weights
    micro_count, tok_count, model_width = stream.shape
    normed_rows, norm_back = jax.vjp(normed, stream, norm_gain.astype(jnp.float32))
    normed_low = normed_rows.astype(jnp.bfloat16)
    qkv_rows = matmul(normed_low, qkv_weight).astype(jnp.bfloat16)
    rim_rows = passed_along(qkv_rows[:, tok_count - RIM :, model_width:], "ctx", 1)
    mask = layout_info["window"]
    parts = []
    if tok_count > BAND:
        parts = by_window(
            later_bands_kernel,
            "window_later",
            [(qkv_rows, tok_count, 0), (qkv_rows, tok_count, 1), (qkv_rows, tok_count, 2), (mask, tok_count, None)],
            [(tok_count - BAND, jnp.bfloat16)],
        )
        rim_rows, parts = lax.optimization_barrier((rim_rows, parts))
    (start,) = by_window(
        first_band_kernel,
        "window_first",
        [(qkv_rows, BAND, 0), (qkv_rows, BAND, 1), (qkv_rows, BAND, 2), (rim_rows, RIM, 0), (rim_rows, RIM, 1)]
        + [(mask, BAND, None)],
        [(BAND, jnp.bfloat16)],
    )
    attended = jnp.concatenate([start] + list(parts), axis=1)
    branch = matmul(attended, out_weight)
    return (stream + branch, (norm_back, normed_low, qkv_rows, rim_rows, attended))


def window_backward(grad_stream, residuals, weights, layout_info):
    norm_back, normed_low, qkv_rows, rim_rows, attended = residuals
    qkv_weight, out_weight = (weights[1], weights[2])
    micro_count, tok_count, model_width = grad_stream.shape
    f32, low = jnp.float32, jnp.bfloat16
    grad_branch = grad_stream.astype(low)
    grad_out = (flat(attended), flat(grad_branch))
    grad_attended = matmul_back(grad_branch, out_weight).astype(low)
    mask = layout_info["window"]
    grad_query, grad_key, grad_value, rim_key, rim_value = by_window(
        first_band_back_kernel,
        "window_first_back",
        [(qkv_rows, BAND, 0), (qkv_rows, BAND, 1), (qkv_rows, BAND, 2), (rim_rows, RIM, 0), (rim_rows, RIM, 1)]
        + [(mask, BAND, None), (grad_attended, BAND, 0)],
        [(BAND, low), (BAND, f32), (BAND, f32), (RIM, low), (RIM, low)],
    )
    returned = passed_along(jnp.concatenate([rim_key, rim_value], axis=-1), "ctx", -1)
    if tok_count > BAND:
        more_query, grad_key, grad_value = by_window(
            later_bands_back_kernel,
            "window_later_back",
            [(qkv_rows, tok_count, 0), (qkv_rows, tok_count, 1), (qkv_rows, tok_count, 2), (mask, tok_count, None)]
            + [(grad_attended, tok_count, 0), (grad_key, BAND, 0), (grad_value, BAND, 0)],
            [(tok_count - BAND, low), (tok_count, f32), (tok_count, f32)],
        )
        grad_query = jnp.concatenate([grad_query, more_query], axis=1)
        returned, grad_key = lax.optimization_barrier((returned, grad_key))
    returned = returned.astype(f32)
    returned = jnp.pad(returned, ((0, 0), (tok_count - RIM, 0), (0, 0)))
    grad_qkv = jnp.concatenate(
        [
            grad_query,
            (grad_key + returned[..., :model_width]).astype(low),
            (grad_value + returned[..., model_width:]).astype(low),
        ],
        axis=-1,
    )
    grad_qkv_weight = (flat(normed_low), flat(grad_qkv))
    grad_input, grad_gain = norm_back(matmul_back(grad_qkv, qkv_weight))
    return (grad_stream + grad_input, (grad_gain, grad_qkv_weight, grad_out))


def ffn_forward(stream, weights):
    norm_gain, gate_up, down_weight = weights
    hidden_width = down_weight.shape[0]
    normed_rows, norm_back = jax.vjp(normed, stream, norm_gain.astype(jnp.float32))
    normed_low = normed_rows.astype(jnp.bfloat16)
    projected = matmul(normed_low, gate_up)
    hidden = (jax.nn.silu(projected[..., :hidden_width]) * projected[..., hidden_width:]).astype(
        jnp.bfloat16
    )
    branch = matmul(hidden, down_weight)
    return (stream + branch, (norm_back, normed_low, projected, hidden))


def ffn_backward(grad_stream, residuals, weights):
    norm_back, normed_low, projected, hidden = residuals
    gate_up, down_weight = (weights[1], weights[2])
    hidden_width = down_weight.shape[0]
    grad_branch = grad_stream.astype(jnp.bfloat16)
    grad_down = (flat(hidden), flat(grad_branch))
    grad_hidden = matmul_back(grad_branch, down_weight)
    gate_part = projected[..., :hidden_width]
    up_part = projected[..., hidden_width:]
    sigmoid_gate = jax.nn.sigmoid(gate_part)
    grad_gate = grad_hidden * up_part * sigmoid_gate * (1.0 + gate_part * (1.0 - sigmoid_gate))
    grad_up = grad_hidden * gate_part * sigmoid_gate
    grad_projected = jnp.concatenate([grad_gate, grad_up], axis=-1).astype(jnp.bfloat16)
    grad_gate_up = (flat(normed_low), flat(grad_projected))
    grad_input, grad_gain = norm_back(matmul_back(grad_projected, gate_up))
    return (grad_stream + grad_input, (grad_gain, grad_gate_up, grad_down))


def body(
    tokens_in,
    seq_lengths,
    norm_linear,
    proj_qk,
    proj_values,
    conv_taps,
    out_linear,
    norm_ffn_one,
    gate_up_one,
    down_one,
    norm_window,
    proj_qkv,
    out_window,
    norm_ffn_two,
    gate_up_two,
    down_two,
    cotangent,
):
    tok_count = tokens_in.shape[2]
    layout_info = layout(seq_lengths, tok_count)
    stream = tokens_in[:, 0].astype(jnp.float32)
    small = jnp.concatenate(
        [
            norm_linear[:, None],
            norm_ffn_one[:, None],
            norm_window[:, None],
            norm_ffn_two[:, None],
            conv_taps,
            jnp.zeros((conv_taps.shape[0], 121), jnp.bfloat16),
        ],
        axis=1,
    )
    n_dp, n_ctx = lax.axis_size("dp"), lax.axis_size("ctx")
    first_shards = [small, proj_qk, proj_values]
    small, w_qk, w_values = gather_all(first_shards, n_dp, n_ctx, chunks_of(first_shards), cid=0)

    def gather_more(state):
        shards = [out_linear, gate_up_one, down_one, proj_qkv, out_window, down_two]
        return gather_all(shards, n_dp, n_ctx, chunks_of(shards), cid=2, carry=1, state=state)

    middle, saved_linear, more = linear_forward(
        stream, (small[:, 0], w_qk, w_values, small[:, 4:7]), layout_info, gather_more
    )
    w_out_linear, w_gu_one, w_dn_one, w_qkv, w_out_window, w_dn_two = more
    w_out_linear, late = lax.optimization_barrier((w_out_linear, gate_up_two))
    w_gu_two = lax.all_gather(late, ("dp", "ctx"), axis=0, tiled=True)
    layer_one = (small[:, 0], w_qk, w_values, small[:, 4:7], w_out_linear, small[:, 1], w_gu_one, w_dn_one)
    layer_two = (small[:, 2], w_qkv, w_out_window, small[:, 3], w_gu_two, w_dn_two)
    first_out, saved_ffn_one = ffn_forward(middle, layer_one[5:])
    second_mid, saved_window = window_forward(first_out, layer_two[:3], layout_info)
    closing, saved_ffn_two = ffn_forward(second_mid, layer_two[3:])
    valid_rows = layout_info["valid"][:, :, None]
    output = (closing * valid_rows).astype(jnp.bfloat16)[:, None]
    grad_stream = cotangent[:, 0].astype(jnp.float32) * valid_rows
    grad_stream, grads_ffn_two = ffn_backward(grad_stream, saved_ffn_two, layer_two[3:])
    grad_stream, grads_window = window_backward(
        grad_stream, saved_window, layer_two[:3], layout_info
    )
    grad_stream, grads_ffn_one = ffn_backward(grad_stream, saved_ffn_one, layer_one[5:])
    other_gains = jnp.stack([grads_ffn_one[0], grads_window[0], grads_ffn_two[0]], axis=1)

    def sum_others(of_out, state):
        products = [
            of_out,
            grads_ffn_one[1],
            grads_ffn_one[2],
            grads_window[1],
            grads_window[2],
            grads_ffn_two[1],
            grads_ffn_two[2],
        ]
        return summed_to_owners(products, 1, out_linear.shape[0], -1, state)

    grad_stream, own_sums, sums = linear_backward(
        grad_stream, saved_linear, layer_one[:5], layout_info, other_gains, sum_others
    )
    small, grad_qk, grad_values = own_sums
    tokens_grad = grad_stream.astype(jnp.bfloat16)[:, None]
    return (
        output,
        tokens_grad,
        small[:, 0],
        grad_qk,
        grad_values,
        small[:, 4:7],
        sums[0],
        small[:, 1],
        sums[1],
        sums[2],
        small[:, 2],
        sums[3],
        sums[4],
        small[:, 3],
        sums[5],
        sums[6],
    )


def solution(mesh):
    placed = (
        P(None, "dp", "ctx", None),
        P(None, "dp", None),
        P(("dp", "ctx")),
        P(("dp", "ctx"), None),
        P(("dp", "ctx"), None),
        P(("dp", "ctx"), None),
        P(("dp", "ctx"), None),
        P(("dp", "ctx")),
        P(("dp", "ctx"), None),
        P(("dp", "ctx"), None),
        P(("dp", "ctx")),
        P(("dp", "ctx"), None),
        P(("dp", "ctx"), None),
        P(("dp", "ctx")),
        P(("dp", "ctx"), None),
        P(("dp", "ctx"), None),
        P(None, "dp", "ctx", None),
    )
    return jax.shard_map(
        body,
        mesh=mesh,
        in_specs=placed,
        out_specs=(
            P(None, "dp", "ctx", None),
            P(None, "dp", "ctx", None),
            P(("dp", "ctx")),
            P(("dp", "ctx"), None),
            P(("dp", "ctx"), None),
            P(("dp", "ctx"), None),
            P(("dp", "ctx"), None),
            P(("dp", "ctx")),
            P(("dp", "ctx"), None),
            P(("dp", "ctx"), None),
            P(("dp", "ctx")),
            P(("dp", "ctx"), None),
            P(("dp", "ctx"), None),
            P(("dp", "ctx")),
            P(("dp", "ctx"), None),
            P(("dp", "ctx"), None),
        ),
        check_vma=False,
    )
```

```python
from functools import partial
import math

import jax
import jax.numpy as jnp
import numpy as np
from jax import lax
from jax.experimental import pallas as pl
from jax.experimental.pallas import tpu as pltpu
from jax.sharding import PartitionSpec as P

HEADS = 16
FEAT = 16
WINDOW = 64
CONV = 3


epsilon = 1e-05
masked_fill = -1e30
highest = lax.Precision.HIGHEST


MESH = pl.DeviceIdType.MESH

def carried(sign, n_ctx, dp, ctx, own, keep, out, came, total, sent, arrived):
    first, last = (0, n_ctx - 1) if sign > 0 else (n_ctx - 1, 0)
    low, f32 = jnp.bfloat16, jnp.float32
    micro, planes, rows = own.shape[:3]

    def copy(m, p):
        return pltpu.make_async_remote_copy(
            src_ref=total.at[m, p],
            dst_ref=came.at[m, p],
            send_sem=sent.at[m, p],
            recv_sem=arrived.at[m, p],
            device_id=(dp, lax.rem(ctx + sign + n_ctx, n_ctx)),
            device_id_type=MESH,
        )

    def act(i):
        m, p = i // planes, i % planes

        @pl.when(ctx != first)
        def _():
            copy(m, p).wait_recv()
            value = came[m, p]
            out[m, p, :rows] = value
            total[m, p] = (own[m, p].astype(f32) + keep[m, 0:1] * value.astype(f32)).astype(low)

        @pl.when(ctx == first)
        def _():
            out[m, p, :rows] = jnp.zeros((rows, 128), low)
            total[m, p] = own[m, p]

        @pl.when(ctx != last)
        def _():
            copy(m, p).start()

    def finish():
        for m in range(micro):
            for p in range(planes):
                out[m, p, rows:] = jnp.zeros((out.shape[2] - rows, 128), low)

        @pl.when(ctx != last)
        def _():
            for m in range(micro):
                for p in range(planes):
                    copy(m, p).wait_send()

    return micro * planes, act, finish


def carry_specs(state):
    whole = pl.BlockSpec(memory_space=pltpu.VMEM)
    shape = state.shape[:2] + (TERMS,) + state.shape[3:]
    held = pltpu.VMEM(state.shape, jnp.bfloat16)
    sems = pltpu.SemaphoreType.DMA(state.shape[:2])
    return [whole, whole], [whole], [jax.ShapeDtypeStruct(shape, jnp.bfloat16)], [held, held, sems, sems]


def gather_kernel(n_dp, n_ctx, chunks, lag, n_w, carry, *refs):
    n_c = 2 if carry else 0
    ins, outs = refs[:n_w], refs[n_w + n_c:2 * n_w + n_c]
    local_sem, send_sem, recv_sem = refs[2 * n_w + 3 * n_c // 2:][:3]
    dp, ctx = lax.axis_index("dp"), lax.axis_index("ctx")
    bits = [1 << i for i in range(n_dp.bit_length() - 1)]
    low_bits, (bit_x, bit_y) = bits[:-2], bits[-2:]
    barrier = pltpu.get_barrier_semaphore()
    greeted = 0
    for bit in bits:
        pl.semaphore_signal(barrier, inc=1, device_id=(dp ^ bit, ctx), device_id_type=MESH)
        greeted += 1
    for hop in range(1, n_ctx):
        pl.semaphore_signal(barrier, inc=1, device_id=(dp, lax.rem(ctx + hop, n_ctx)), device_id_type=MESH)
        greeted += 1
    pl.semaphore_wait(barrier, greeted)
    sends = []

    def piece(c, start, shards):
        w, col, width = chunks[c]
        return outs[w].at[pl.ds(start, shards), :, pl.ds(col, width)]

    def send(c, slot, start, rows, target, src=None):
        where = piece(c, start, rows)
        copy = pltpu.make_async_remote_copy(
            src_ref=where if src is None else src, dst_ref=where,
            send_sem=send_sem.at[c, slot], recv_sem=recv_sem.at[c, slot],
            device_id=target, device_id_type=MESH)
        copy.start()
        sends.append(copy)

    def arrive(c, slot, start, rows):
        where = piece(c, start, rows)
        pltpu.make_async_remote_copy(
            src_ref=where, dst_ref=where, send_sem=send_sem.at[c, slot], recv_sem=recv_sem.at[c, slot],
            device_id=(dp ^ 1, ctx), device_id_type=MESH).wait_recv()

    def stage_ctx(c):
        w, col, width = chunks[c]
        own = ins[w].at[:, :, pl.ds(col, width)]
        start = dp * n_ctx + ctx
        for hop in range(1, n_ctx):
            send(c, hop - 1, start, 1, (dp, lax.rem(ctx + hop, n_ctx)), src=own)
        pltpu.make_async_copy(own, piece(c, start, 1), local_sem.at[c]).start()

    base = n_ctx - 1
    SX, SY, SDX, SDY, SC = base, base + 1, base + 2, base + 3, base + 4

    def stage_sides(c):
        w, col, width = chunks[c]
        for hop in range(1, n_ctx):
            arrive(c, hop - 1, dp * n_ctx + lax.rem(ctx - hop + n_ctx, n_ctx), 1)
        own = ins[w].at[:, :, pl.ds(col, width)]
        pltpu.make_async_copy(own, piece(c, dp * n_ctx + ctx, 1), local_sem.at[c]).wait()
        group = n_ctx
        send(c, SX, dp * group, group, (dp ^ bit_x, ctx))
        send(c, SY, dp * group, group, (dp ^ bit_y, ctx))

    def stage_diag(c):
        group = n_ctx
        a0, an, b0, bn = 0, n_ctx // 2, n_ctx // 2, n_ctx - n_ctx // 2
        arrive(c, SX, (dp ^ bit_x) * group, group)
        send(c, SDY, (dp ^ bit_x) * group + a0, an, (dp ^ bit_y, ctx))
        arrive(c, SY, (dp ^ bit_y) * group, group)
        send(c, SDX, (dp ^ bit_y) * group + b0, bn, (dp ^ bit_x, ctx))

    def low_slot(level, j):
        return SC + 4 * ((1 << level) - 1) + j

    def quads(base_dp, level):
        out = []
        for top in range(4):
            for low in range(1 << level):
                flip = (bit_x if top & 1 else 0) | (bit_y if top & 2 else 0)
                for i in range(level):
                    if low >> i & 1:
                        flip |= low_bits[len(low_bits) - 1 - i]
                out.append(base_dp ^ flip)
        return out

    def stage_low(c, level):
        group = n_ctx
        if level == 0:
            a0, an, b0, bn = 0, n_ctx // 2, n_ctx // 2, n_ctx - n_ctx // 2
            arrive(c, SDY, (dp ^ bit_x ^ bit_y) * group + a0, an)
            arrive(c, SDX, (dp ^ bit_x ^ bit_y) * group + b0, bn)
        else:
            bit = low_bits[len(low_bits) - level]
            for j, block in enumerate(quads(dp ^ bit, level - 1)):
                arrive(c, low_slot(level - 1, j), block * group, group)
        if level < len(low_bits):
            bit = low_bits[len(low_bits) - 1 - level]
            for j, block in enumerate(quads(dp, level)):
                send(c, low_slot(level, j), block * group, group, (dp ^ bit, ctx))

    stages = [stage_ctx, stage_sides, stage_diag] + [partial(stage_low, level=l) for l in range(len(low_bits) + 1)]
    depth = len(stages)
    turns = len(chunks) + (depth - 1) * lag
    due = {}
    if carry:
        own, keep = refs[n_w:n_w + 2]
        n_pieces, act, finish = carried(carry, n_ctx, dp, ctx, own, keep, refs[2 * n_w + 2], *refs[2 * n_w + 6:])
        for place in range(n_ctx):
            for i in range(n_pieces):
                due.setdefault(place + i // 2, []).append((place, i))
        turns = max(turns, max(due) + 1)
    for t in range(turns):
        for place, i in due.get(t, []):
            @pl.when(ctx == (place if carry > 0 else n_ctx - 1 - place))
            def _():
                act(i)
        for s in range(depth):
            c = t - s * lag
            if 0 <= c < len(chunks):
                stages[s](c)
    if carry:
        finish()
    for copy in sends:
        copy.wait_send()

def gather_all(weights, n_dp, n_ctx, chunks, lag=1, cid=0, carry=0, state=()):
    n = len(weights)
    places = n_dp * n_ctx
    slots = n_ctx - 1 + 4 + 4 * (n_dp // 4 - 1)
    more_in, more_out, more_shape, more_scratch = carry_specs(state[0]) if carry else ([], [], [], [])
    full = pl.pallas_call(
        partial(gather_kernel, n_dp, n_ctx, chunks, lag, n, carry),
        out_shape=[jax.ShapeDtypeStruct((places,) + w.shape, w.dtype) for w in weights] + more_shape,
        in_specs=[pl.BlockSpec(memory_space=pltpu.HBM)] * n + more_in,
        out_specs=[pl.BlockSpec(memory_space=pltpu.HBM)] * n + more_out,
        scratch_shapes=[pltpu.SemaphoreType.DMA((len(chunks),)), pltpu.SemaphoreType.DMA((len(chunks), slots)), pltpu.SemaphoreType.DMA((len(chunks), slots))]
        + more_scratch,
        compiler_params=pltpu.CompilerParams(collective_id=cid, has_side_effects=True),
        name="gather_weights")(*[w[None] for w in weights], *state)
    return [f.reshape(places * f.shape[1], f.shape[2]) for f in full[:n]] + list(full[n:])


WIDE = 512
SLOTS_HELD = 8
APART = 4


def scatter_kernel(n_dp, n_ctx, plan, lags, pieces, n_y, n_o, carry, *refs):
    n_x = len(pieces)
    xs, ys, refs = refs[:n_x], refs[n_x : n_x + n_y], refs[n_x + n_y :]
    state, refs = (refs[:2], refs[2:]) if carry else ((), refs)
    outs, refs = refs[:n_o], refs[n_o:]
    state_out, refs = (refs[:1], refs[1:]) if carry else ((), refs)
    bits = [1 << i for i in range(n_dp.bit_length() - 1)]
    low_bits, (bit_x, bit_y) = bits[:-2], bits[-2:]
    n_low = len(low_bits)
    x_all, y_all, natural = refs[0], refs[1], refs[-1]
    low_out, low_in = refs[2 : 2 + n_low], refs[2 + n_low : 2 + 2 * n_low]
    refs = refs[2 + 2 * n_low :]
    cross, cross_y, cross_x, side_x, side_y, came_x, came_y, shards, came_ctx, result = refs[:10]
    x_sem, y_sem, out_sem, sent, arrived, credit = refs[10:16]
    held = y_all.shape[0]
    dp, ctx = lax.axis_index("dp"), lax.axis_index("ctx")
    group = cross.shape[1]
    half = group // 2
    rows = group // n_ctx
    f32, low = jnp.float32, jnp.bfloat16
    A_CY, A_CX, A_X, A_Y, A_Z = n_low, n_low + 1, n_low + 2, n_low + 3, n_low + 4
    C_X, C_Y, C_Z = n_low, n_low + 1, n_low + 2

    def at_ctx(hop):
        return (dp, lax.rem(ctx + hop, n_ctx))

    barrier = pltpu.get_barrier_semaphore()
    for bit in bits:
        pl.semaphore_signal(barrier, inc=1, device_id=(dp ^ bit, ctx), device_id_type=MESH)
    for hop in range(1, n_ctx):
        pl.semaphore_signal(barrier, inc=1, device_id=at_ctx(hop), device_id_type=MESH)
    pl.semaphore_wait(barrier, len(bits) + n_ctx - 1)

    bounds, count = [], 0
    for segment in plan:
        bounds.append((count, count + segment[5]))
        count += segment[5]
    laid_at = [sum(max(1, n) for n in pieces[:i]) for i in range(n_x)]
    x_first = {}
    for segment, (first, _) in zip(plan, bounds):
        x_first.setdefault(segment[0], first)

    def x_copy(i):
        if pieces[i]:
            return pltpu.make_async_copy(xs[i], x_all.at[pl.ds(laid_at[i], pieces[i])], x_sem.at[i])
        return pltpu.make_async_copy(xs[i], natural.at[pieces[:i].count(0)], x_sem.at[i])

    def x_ready(i):
        x_copy(i).wait()
        if not pieces[i]:
            for place in range(n_dp):
                value = natural[pieces[:i].count(0), :, place * group : (place + 1) * group]
                x_all[laid_at[i], place] = value.T

    for i in range(n_x):
        x_copy(i).start()

    def y_start(c):
        slot = lax.rem(c, held)
        for segment, (first, last) in zip(plan, bounds):

            @pl.when((c >= first) & (c < last))
            def _():
                where = pl.multiple_of((c - first) * WIDE, WIDE)
                pltpu.make_async_copy(
                    ys[segment[1]].at[:, pl.ds(where, WIDE)], y_all.at[slot], y_sem.at[slot]
                ).start()

    def x_place(c):
        return sum((c >= first).astype(jnp.int32) for first in sorted(x_first.values())[1:])

    def partial_sum(c, flip):
        return jnp.dot(
            x_all[x_place(c), dp ^ flip], y_all[lax.rem(c, held)], preferred_element_type=f32
        )

    def rest(level):
        free = low_bits[level + 1 :] + [bit_x, bit_y]
        return [sum(b for i, b in enumerate(free) if n >> i & 1) for n in range(1 << len(free))]

    def summed(c, flip, levels):
        total = partial_sum(c, flip)
        for level in range(levels):
            total = total + low_in[level][lax.rem(c, held), rest(level).index(flip)].astype(f32)
        return total

    def remote(src, dst, slot, kind, target):
        return pltpu.make_async_remote_copy(
            src_ref=src,
            dst_ref=dst,
            send_sem=sent.at[slot, kind],
            recv_sem=arrived.at[slot, kind],
            device_id=target,
            device_id_type=MESH,
        )

    def copy_of(slot, kind):
        over_x, over_y = (dp ^ bit_x, ctx), (dp ^ bit_y, ctx)
        if kind < n_low:
            return remote(
                low_out[kind].at[slot], low_in[kind].at[slot], slot, kind, (dp ^ low_bits[kind], ctx)
            )
        if kind == A_CY:
            return remote(cross.at[slot, pl.ds(0, half)], cross_y.at[slot], slot, kind, over_y)
        if kind == A_CX:
            return remote(cross.at[slot, pl.ds(half, half)], cross_x.at[slot], slot, kind, over_x)
        if kind == A_X:
            return remote(side_x.at[slot], came_x.at[slot], slot, kind, over_x)
        if kind == A_Y:
            return remote(side_y.at[slot], came_y.at[slot], slot, kind, over_y)
        hop = kind - A_Z + 1
        there = lax.rem(ctx + hop, n_ctx)
        return remote(shards.at[slot, there], came_ctx.at[slot, hop - 1], slot, kind, (dp, there))

    def need_credit(c, kind):
        @pl.when(c >= held)
        def _():
            pl.semaphore_wait(credit.at[kind], 1)

    def step_low(level, c):
        slot = lax.rem(c, held)
        if level == 0:
            for i in range(n_x):

                @pl.when(c == x_first[laid_at[i]])
                def _():
                    x_ready(i)

            pltpu.make_async_copy(ys[0].at[:, pl.ds(0, WIDE)], y_all.at[slot], y_sem.at[slot]).wait()
        else:
            copy_of(slot, level - 1).wait_recv()
        need_credit(c, level)
        for j, flip in enumerate(rest(level)):
            low_out[level][slot, j] = summed(c, flip | low_bits[level], level).astype(low)
        copy_of(slot, level).start()

    def step_cross(c):
        slot = lax.rem(c, held)
        if n_low:
            copy_of(slot, n_low - 1).wait_recv()
        need_credit(c, C_X)
        need_credit(c, C_Y)
        cross[slot] = summed(c, bit_x | bit_y, n_low).astype(low)
        copy_of(slot, A_CY).start()
        copy_of(slot, A_CX).start()

    def step_sides(c):
        slot = lax.rem(c, held)
        over_x = summed(c, bit_x, n_low)
        over_y = summed(c, bit_y, n_low)
        copy_of(slot, A_CY).wait_recv()
        side_x[slot, :half] = (over_x[:half] + cross_y[slot].astype(f32)).astype(low)
        side_x[slot, half:] = over_x[half:].astype(low)
        copy_of(slot, A_X).start()
        copy_of(slot, A_CX).wait_recv()
        side_y[slot, :half] = over_y[:half].astype(low)
        side_y[slot, half:] = (over_y[half:] + cross_x[slot].astype(f32)).astype(low)
        copy_of(slot, A_Y).start()

    def step_own(c):
        slot = lax.rem(c, held)
        total = summed(c, 0, n_low)
        copy_of(slot, A_X).wait_recv()
        copy_of(slot, A_Y).wait_recv()
        total = total + came_x[slot].astype(f32) + came_y[slot].astype(f32)
        for j in range(n_ctx):
            shards[slot, j] = total[j * rows : (j + 1) * rows].astype(low)
        for hop in range(1, n_ctx):
            need_credit(c, C_Z + hop - 1)
            copy_of(slot, A_Z + hop - 1).start()

    def out_copy(c, slot, segment, first):
        where = pl.multiple_of((c - first) * WIDE, WIDE)
        _, _, o, row, n_rows, _ = segment
        return pltpu.make_async_copy(
            result.at[slot, pl.ds(0, n_rows)],
            outs[o].at[pl.ds(row, n_rows), pl.ds(where, WIDE)],
            out_sem.at[slot],
        )

    def each_segment(c, act):
        for segment, (first, last) in zip(plan, bounds):

            @pl.when((c >= first) & (c < last))
            def _():
                act(segment, first)

    def out_wait(c):
        slot = lax.rem(c, held)
        each_segment(c, lambda segment, first: out_copy(c, slot, segment, first).wait())

    def step_end(c):
        slot = lax.rem(c, held)

        @pl.when(c >= held)
        def _():
            out_wait(c - held)

        total = shards[slot, ctx].astype(f32)
        for hop in range(1, n_ctx):
            copy_of(slot, A_Z + hop - 1).wait_recv()
            total = total + came_ctx[slot, hop - 1].astype(f32)
        result[slot] = total
        each_segment(c, lambda segment, first: out_copy(c, slot, segment, first).start())
        for kind in range(A_Z + n_ctx - 1):
            copy_of(slot, kind).wait_send()

        @pl.when(c + held < count)
        def _():
            for level, bit in enumerate(low_bits):
                pl.semaphore_signal(credit.at[level], inc=1, device_id=(dp ^ bit, ctx), device_id_type=MESH)
            pl.semaphore_signal(credit.at[C_X], inc=1, device_id=(dp ^ bit_x, ctx), device_id_type=MESH)
            pl.semaphore_signal(credit.at[C_Y], inc=1, device_id=(dp ^ bit_y, ctx), device_id_type=MESH)
            for hop in range(1, n_ctx):
                pl.semaphore_signal(
                    credit.at[C_Z + hop - 1], inc=1, device_id=at_ctx(n_ctx - hop), device_id_type=MESH
                )

    steps = [partial(step_low, level) for level in range(n_low)] + [step_cross, step_sides, step_own, step_end]
    ahead = 2
    for c in range(ahead):
        y_start(jnp.int32(c))

    turns = count + lags[-1]
    if carry:
        n_pieces, act, finish = carried(carry, n_ctx, dp, ctx, *state, *state_out, *refs[16:-1])
        place = ctx if carry > 0 else n_ctx - 1 - ctx
        turns = max(turns, n_pieces + APART * (n_ctx - 1))

    def turn(t, none):
        if carry:
            i = t - APART * place

            @pl.when((i >= 0) & (i < n_pieces))
            def _():
                act(i)

        @pl.when(t + ahead < count)
        def _():
            y_start(t + ahead)

        for step, lag in zip(steps, lags):
            c = t - lag

            @pl.when((c >= 0) & (c < count))
            def _():
                step(c)

        return none

    lax.fori_loop(0, turns, turn, 0)
    if carry:
        finish()
    for c in range(max(0, count - held), count):
        out_wait(jnp.int32(c))


def scatter_sums(xs, ys, out_shapes, plan, n_dp, n_ctx, cid=1, carry=0, state=(), lags=None, held=SLOTS_HELD):
    pieces = [n for _, n in xs]
    tokens = ys[0].shape[0]
    group = [x.shape[1] // n_dp for x, n in xs if not n][0]
    n_low = n_dp.bit_length() - 3
    rows = group // n_ctx
    low, f32 = jnp.bfloat16, jnp.float32
    lags = lags or list(range(n_low + 4))
    low_shapes = [
        pltpu.VMEM((held, n_dp >> (level + 1), group, WIDE), low) for level in range(n_low)
    ]
    half = group // 2
    kinds = n_low + 4 + n_ctx - 1
    more_in, more_out, more_shape, more_scratch = carry_specs(state[0]) if carry else ([], [], [], [])
    return pl.pallas_call(
        partial(scatter_kernel, n_dp, n_ctx, plan, lags, pieces, len(ys), len(out_shapes), carry),
        out_shape=[jax.ShapeDtypeStruct(shape, f32) for shape in out_shapes] + more_shape,
        in_specs=[pl.BlockSpec(memory_space=pl.ANY)] * (len(xs) + len(ys)) + more_in,
        out_specs=[pl.BlockSpec(memory_space=pltpu.HBM)] * len(out_shapes) + more_out,
        scratch_shapes=[
            pltpu.VMEM((sum(max(1, n) for n in pieces), n_dp, group, tokens), low),
            pltpu.VMEM((held, tokens, WIDE), low),
            *low_shapes,
            *low_shapes,
            pltpu.VMEM((held, group, WIDE), low),
            pltpu.VMEM((held, half, WIDE), low),
            pltpu.VMEM((held, half, WIDE), low),
            pltpu.VMEM((held, group, WIDE), low),
            pltpu.VMEM((held, group, WIDE), low),
            pltpu.VMEM((held, group, WIDE), low),
            pltpu.VMEM((held, group, WIDE), low),
            pltpu.VMEM((held, n_ctx, rows, WIDE), low),
            pltpu.VMEM((held, n_ctx - 1, rows, WIDE), low),
            pltpu.VMEM((held, rows, WIDE), f32),
            pltpu.SemaphoreType.DMA((len(xs),)),
            pltpu.SemaphoreType.DMA((held,)),
            pltpu.SemaphoreType.DMA((held,)),
            pltpu.SemaphoreType.DMA((held, kinds)),
            pltpu.SemaphoreType.DMA((held, kinds)),
            pltpu.SemaphoreType.REGULAR((n_low + 2 + n_ctx - 1,)),
            *more_scratch,
            pltpu.VMEM((pieces.count(0), tokens, n_dp * group), low),
        ],
        compiler_params=pltpu.CompilerParams(
            collective_id=cid, has_side_effects=True, vmem_limit_bytes=56 * 2**20
        ),
        name="scatter_sums",
    )(*[x for x, _ in xs], *ys, *state)


def passed_along(value, axis, steps):
    count = lax.axis_size(axis)
    leading, last = (max(0, -steps), min(count, count - steps))
    return lax.ppermute(value, axis, [(source, source + steps) for source in range(leading, last)])


TERMS = 256
SENT = 160
PER = 2


def feature_tables():
    first = np.zeros((FEAT, TERMS), np.float32)
    second = np.zeros((FEAT, TERMS), np.float32)
    base = np.zeros((8, TERMS), np.float32)
    base[0, 0] = base[1, 0] = base[2, 0] = 1.0
    column = 1
    for f in range(FEAT):
        first[f, column] = base[1, column] = 1.0
        base[2, column] = 1.0 / math.sqrt(FEAT)
        column += 1
    for f in range(FEAT):
        for g in range(f, FEAT):
            first[f, column] = second[g, column] = 1.0
            base[2, column] = (0.5 if f == g else 1.0) / FEAT
            column += 1
    tile = np.stack([np.tile(first, (HEADS, 1)), np.tile(second, (HEADS, 1))])
    return jnp.asarray(tile, jnp.bfloat16), jnp.asarray(base)


def dot_nn(a, b):
    return jnp.dot(a, b, preferred_element_type=jnp.float32)


def dot_nt(a, b):
    return lax.dot_general(a, b, (((1,), (1,)), ((), ())), preferred_element_type=jnp.float32)


def dot_tn(a, b):
    return lax.dot_general(a, b, (((0,), (0,)), ((), ())), preferred_element_type=jnp.float32)


def lanes_of(shape, size):
    return lax.broadcasted_iota(jnp.int32, shape, len(shape) - 1) // size


def only(mask, value):
    return jnp.where(mask, value, jnp.zeros_like(value))


def pairs_of(step):
    return [(step * PER + n, slice(128 * n, 128 * (n + 1))) for n in range(PER)]


def factors(rows, tables, base):
    return (dot_nn(rows, tables[0]) + base[0:1], dot_nn(rows, tables[1]) + base[1:2])


def states_kernel(key_ref, value_ref, last_ref, table_ref, base_ref, state_ref):
    step = pl.program_id(1)
    low, f32 = jnp.bfloat16, jnp.float32
    keys = key_ref[0]
    last = last_ref[0]
    head_of = lanes_of(keys.shape, FEAT)
    lane = lanes_of((SENT, 128), 1)
    totals = state_ref[0, HEADS // 2]
    totals = jnp.where(step == 0, jnp.zeros_like(totals), totals)
    for pair, here in pairs_of(step):
        values = value_ref[0, :, here].astype(f32)
        held = jnp.concatenate([(values * last).astype(low), last.astype(low)], axis=1)
        both = []
        for side in range(2):
            head = 2 * pair + side
            one, two = factors(only(head_of == head, keys), table_ref, base_ref)
            part = dot_tn((one * two).astype(low), held)[:SENT]
            both.append(part[:, :128])
            totals = jnp.where(lane == head, part[:, 128:].astype(low), totals)
        state_ref[0, pair] = jnp.where(lane < 64, both[0], both[1]).astype(low)
    state_ref[0, HEADS // 2] = totals


def attend_kernel(
    query_ref, key_ref, value_ref, state_ref, mask_ref, carried_ref, table_ref, base_ref, out_ref, den_ref
):
    step = pl.program_id(1)
    low, f32 = jnp.bfloat16, jnp.float32
    queries, keys = query_ref[0], key_ref[0]
    mask, carried = mask_ref[0], carried_ref[0][:, :1]
    totals = state_ref[0, HEADS // 2]
    head_of = lanes_of(queries.shape, FEAT)
    lane = lanes_of(totals.shape, 1)
    for pair, here in pairs_of(step):
        state = state_ref[0, pair]
        values = value_ref[0, :, here]
        held = jnp.concatenate([values, jnp.ones_like(values)], axis=1)
        outs, dens = [], []
        for side in range(2):
            head = 2 * pair + side
            own = only(head_of == head, queries)
            score = dot_nt(own, keys) * (1.0 / math.sqrt(FEAT))
            weight = ((1.0 + score + 0.5 * score * score) * mask).astype(low)
            one, two = factors(own, table_ref, base_ref)
            terms = (one * two * base_ref[2:3] * carried).astype(low)
            total = jnp.sum(only(lane == head, totals.astype(f32)), axis=1, keepdims=True)
            total = jnp.broadcast_to(total, totals.shape).astype(low)
            result = dot_nn(weight, held) + dot_nn(terms, jnp.concatenate([state, total], axis=1))
            outs.append(result[:, :128] / result[:, 128:])
            dens.append(result[:, 128:])
        first = lanes_of(outs[0].shape, 64) == 0
        out_ref[0, :, here] = jnp.where(first, outs[0], outs[1]).astype(low)
        den_ref[0, :, here] = jnp.where(first, dens[0], dens[1])


def attend_back_kernel(
    query_ref, key_ref, value_ref, state_ref, mask_ref, carried_ref, table_ref, base_ref, grad_ref, out_ref,
    den_ref, dquery_ref, dkey_ref, dvalue_ref, dstate_ref,
):
    step = pl.program_id(1)
    low, f32 = jnp.bfloat16, jnp.float32
    queries, keys = query_ref[0], key_ref[0]
    mask, carried = mask_ref[0], carried_ref[0][:, :1]
    totals = state_ref[0, HEADS // 2]
    head_of = lanes_of(queries.shape, FEAT)
    lane = lanes_of(value_ref.shape[1:2] + (128,), 1)
    dquery = jnp.zeros(queries.shape, f32)
    dkey = jnp.zeros(queries.shape, f32)
    dtotals = dstate_ref[0, HEADS // 2]
    dtotals = jnp.where(step == 0, jnp.zeros_like(dtotals), dtotals)
    inv_root = 1.0 / math.sqrt(FEAT)
    for pair, here in pairs_of(step):
        values = value_ref[0, :, here]
        whole_state = jnp.concatenate([state_ref[0, pair], totals], axis=1)
        dnum = grad_ref[0, :, here] / den_ref[0, :, here]
        inner = dnum * out_ref[0, :, here].astype(f32)
        dvalue = jnp.zeros(dnum.shape, f32)
        dstate = jnp.zeros((SENT, 128), f32)
        for side in range(2):
            head = 2 * pair + side
            own_lanes = (lane < 64) if side == 0 else (lane >= 64)
            own, own_keys = only(head_of == head, queries), only(head_of == head, keys)
            dnum_own = only(own_lanes, dnum).astype(low)
            dden = -jnp.sum(only(own_lanes, inner), axis=1, keepdims=True)
            score = dot_nt(own, keys) * inv_root
            slope = (1.0 + score) * mask
            weight = ((1.0 + score + 0.5 * score * score) * mask).astype(low)
            dscore = ((dot_nt(dnum_own, values) + dden) * slope * inv_root).astype(low)
            dvalue += dot_tn(weight, dnum_own)
            dquery += dot_nn(dscore, own_keys)
            dkey += dot_tn(dscore, own)
            one, two = factors(own, table_ref, base_ref)
            scale = base_ref[2:3] * carried
            terms = (one * two * scale).astype(low)
            dden_all = jnp.broadcast_to(dden, dnum.shape)
            part = dot_tn(terms, jnp.concatenate([dnum_own, dden_all.astype(low)], axis=1))[:SENT]
            dstate += part[:, :128]
            dtotals = jnp.where(lanes_of(dtotals.shape, 1) == head, part[:, 128:].astype(low), dtotals)
            both = jnp.concatenate([dnum_own, only(lane == head, dden_all).astype(low)], axis=1)
            dterms = dot_nt(both, whole_state) * scale
            through = dot_nt((dterms * two).astype(low), table_ref[0])
            through += dot_nt((dterms * one).astype(low), table_ref[1])
            dquery += only(head_of == head, through)
        dvalue_ref[0, :, here] = dvalue
        dstate_ref[0, pair] = dstate.astype(low)
    dstate_ref[0, HEADS // 2] = dtotals

    @pl.when(step == 0)
    def _():
        dquery_ref[0] = dquery
        dkey_ref[0] = dkey

    @pl.when(step != 0)
    def _():
        dquery_ref[0] += dquery
        dkey_ref[0] += dkey


def states_back_kernel(
    key_ref, value_ref, last_ref, table_ref, base_ref, dstate_ref, dkey_in, dvalue_in, dkey_ref, dvalue_ref
):
    step = pl.program_id(1)
    low, f32 = jnp.bfloat16, jnp.float32
    keys = key_ref[0]
    last = last_ref[0]
    dtotals = dstate_ref[0, HEADS // 2]
    head_of = lanes_of(keys.shape, FEAT)
    lane = lanes_of(last.shape, 1)
    dkey = jnp.zeros(keys.shape, f32)
    for pair, here in pairs_of(step):
        values = value_ref[0, :, here]
        dstate = dstate_ref[0, pair]
        whole = jnp.concatenate([dstate, dtotals], axis=1)
        dvalue = dvalue_in[0, :, here]
        for side in range(2):
            head = 2 * pair + side
            own_lanes = (lane < 64) if side == 0 else (lane >= 64)
            one, two = factors(only(head_of == head, keys), table_ref, base_ref)
            terms = (one * two).astype(low)
            dvalue += only(own_lanes, dot_nn(terms, dstate)) * last
            both = jnp.concatenate([only(own_lanes, values), (lane == head).astype(low)], axis=1)
            dterms = dot_nt(both, whole) * last[:, :1]
            through = dot_nt((dterms * two).astype(low), table_ref[0])
            through += dot_nt((dterms * one).astype(low), table_ref[1])
            dkey += only(head_of == head, through)
        dvalue_ref[0, :, here] = dvalue

    @pl.when(step == 0)
    def _():
        dkey_ref[0] = dkey_in[0] + dkey

    @pl.when(step != 0)
    def _():
        dkey_ref[0] += dkey


def by_pair(kernel, name, ins, outs):
    def spec(kind, shape):
        if kind == "query":
            return pl.BlockSpec((1, shape[1], HEADS * FEAT), lambda m, p: (m, 0, 0))
        if kind == "key":
            return pl.BlockSpec((1, shape[1], HEADS * FEAT), lambda m, p: (m, 0, 1))
        if kind == "pair":
            return pl.BlockSpec((1, shape[1], PER * 128), lambda m, p: (m, 0, p))
        if kind == "micro":
            return pl.BlockSpec((1,) + shape[1:], lambda m, p: (m,) + (0,) * (len(shape) - 1))
        return pl.BlockSpec(shape, lambda m, p: (0,) * len(shape))

    return pl.pallas_call(
        kernel,
        grid=(ins[0][0].shape[0], HEADS // 2 // PER),
        in_specs=[spec(kind, array.shape) for array, kind in ins],
        out_specs=[spec(kind, shape) for shape, _, kind in outs],
        out_shape=[jax.ShapeDtypeStruct(shape, dtype) for shape, dtype, _ in outs],
        compiler_params=pltpu.CompilerParams(vmem_limit_bytes=48 * 2**20),
        name=name,
    )(*[array for array, _ in ins])


def turn_kernel(places, unit, value_ref, out_ref, turned):
    tokens, rows = value_ref.shape
    for first in range(0, rows, 128):
        turned[first : first + 128] = value_ref[:, first : first + 128].T.astype(jnp.float32)
    pieces, n_dp = out_ref.shape[:2]
    n_ctx, shard = places // n_dp, rows // places
    for place in range(places):
        for piece in range(pieces):
            start, count = piece * unit, min(unit, shard - piece * unit)
            value = turned[place * shard + start : place * shard + start + count]
            if count < unit:
                value = jnp.concatenate([value, jnp.zeros((unit - count, tokens), jnp.float32)], axis=0)
            where = place % n_ctx * unit
            out_ref[piece, place // n_ctx, where : where + unit] = value.astype(jnp.bfloat16)


def turned_pieces(value, places, n_dp, unit):
    tokens, rows = value.shape
    pieces = -(-(rows // places) // unit)
    return pl.pallas_call(
        partial(turn_kernel, places, unit),
        out_shape=jax.ShapeDtypeStruct((pieces, n_dp, places // n_dp * unit, tokens), jnp.bfloat16),
        in_specs=[pl.BlockSpec(memory_space=pltpu.VMEM)],
        out_specs=pl.BlockSpec(memory_space=pltpu.VMEM),
        scratch_shapes=[pltpu.VMEM((rows, tokens), jnp.float32)],
        compiler_params=pltpu.CompilerParams(vmem_limit_bytes=48 * 2**20),
        name="turn",
    )(value)


def chunk_plan(products, unit):
    n_dp = lax.axis_size("dp")
    places = n_dp * lax.axis_size("ctx")
    operands, first_laid, plan, shapes, count = [], {}, [], [], 0
    for number, (operand, gradient) in enumerate(products):
        shard = operand.shape[1] // places
        pieces = -(-shard // unit)
        shapes.append((shard, gradient.shape[1]))
        if id(operand) not in first_laid:
            first_laid[id(operand)] = count
            count += pieces
            if pieces > 1:
                operands.append((turned_pieces(operand, places, n_dp, unit), pieces))
            else:
                operands.append((operand, 0))
        for piece in range(pieces):
            first = piece * unit
            plan.append(
                (
                    first_laid[id(operand)] + piece,
                    number,
                    number,
                    first,
                    min(unit, shard - first),
                    gradient.shape[1] // WIDE,
                )
            )
    return operands, plan, shapes


def as_product(small):
    rows, few = small.shape
    high = small.astype(jnp.bfloat16)
    rest = (small - high.astype(jnp.float32)).astype(jnp.bfloat16)

    def product(tokens):
        both = jnp.zeros((tokens, rows), jnp.bfloat16).at[:few].set(high.T).at[few : 2 * few].set(rest.T)
        pick = np.zeros((tokens, WIDE), np.float32)
        pick[:few, :few] = pick[few : 2 * few, :few] = np.eye(few)
        return both, jnp.asarray(pick, jnp.bfloat16)

    return product


def summed_to_owners(products, cid, unit, carry=0, state=()):
    n_dp, n_ctx = lax.axis_size("dp"), lax.axis_size("ctx")
    laid, plan, shapes = chunk_plan(products, unit)
    gradients = [gradient for _, gradient in products]
    return scatter_sums(laid, gradients, shapes, plan, n_dp, n_ctx, cid, carry, state)


def chunks_of(shards):
    out = []
    for place, shard in enumerate(shards):
        rows, columns = shard.shape
        unit = max(128, 1408 * 32 // rows // 128 * 128)
        width = -(-(columns // 128) // -(-columns // unit)) * 128
        for first in range(0, columns, width):
            out.append((place, first, min(width, columns - first)))
    return out


def flat(value):
    return value.reshape(-1, value.shape[-1])


def normed(stream, scale_gain):
    return (
        stream * lax.rsqrt(jnp.mean(stream * stream, axis=-1, keepdims=True) + epsilon) * scale_gain
    )


def matmul(operand, weight):
    return jnp.einsum("mtd,de->mte", operand, weight, preferred_element_type=jnp.float32)


def matmul_back(operand, weight):
    return jnp.einsum("mte,de->mtd", operand, weight, preferred_element_type=jnp.float32)


def weight_grad(operand, gradient):
    return jnp.einsum("mtd,mte->de", operand, gradient, preferred_element_type=jnp.float32)


def layout(seq_lengths, tok_count):
    seq_ends = jnp.cumsum(seq_lengths[:, 0, :], axis=-1, dtype=jnp.int32)
    first_pos = lax.axis_index("ctx") * tok_count

    def segment_of(positions):
        return jnp.sum(
            (positions[None, :, None] >= seq_ends[:, None, :]).astype(jnp.int32),
            axis=-1,
            dtype=jnp.int32,
        )

    own_pos = first_pos + jnp.arange(tok_count, dtype=jnp.int32)
    own_seg = segment_of(own_pos)
    before_seg = segment_of(own_pos - 1)

    def in_lanes(flag):
        return jnp.broadcast_to(flag[:, :, None].astype(jnp.float32), flag.shape + (128,))

    starts = (own_seg != before_seg) | (own_pos == 0)[None, :]
    keep = 1.0 - jnp.max(starts.astype(jnp.float32), axis=1)
    tap_masks = []
    for offset in range(CONV):
        source = own_pos - offset
        tap_masks.append(
            ((segment_of(source) == own_seg) & (source >= 0)[None, :]).astype(jnp.float32)
        )
    key_pos = first_pos - BAND + jnp.arange(tok_count + BAND, dtype=jnp.int32)
    key_seg = jnp.where(key_pos >= 0, segment_of(key_pos), -1)
    window_mask = []
    for first in range(0, tok_count, BAND):
        queries, keys = slice(first, first + BAND), slice(first, first + 2 * BAND)
        ahead = own_pos[queries][:, None] - key_pos[keys][None, :]
        same = own_seg[:, queries][:, :, None] == key_seg[:, keys][:, None, :]
        window_mask.append(((ahead >= 0) & (ahead < WINDOW))[None] & same)
    window_mask = jnp.concatenate(window_mask, axis=1).astype(jnp.float32)
    causal = (own_pos[:, None] >= own_pos[None, :])[None] & (
        own_seg[:, :, None] == own_seg[:, None, :]
    )
    return {
        "valid": (own_pos[None, :] < seq_ends[:, -1:]).astype(jnp.float32),
        "keep": jnp.broadcast_to(keep[:, None, None], keep.shape + (8, 128)),
        "carried": in_lanes((own_seg == before_seg[:, :1]) & (first_pos > 0)),
        "last": in_lanes(own_seg == own_seg[:, -1:]),
        "causal": causal.astype(jnp.float32),
        "taps": jnp.stack(tap_masks),
        "window": window_mask,
    }


def conv_gate(pre_values, rim_rows, tap_weights, tap_masks):
    tok_count = pre_values.shape[1]
    rim_width = rim_rows.shape[1]
    extended = jnp.concatenate([rim_rows, pre_values], axis=1)
    conv_sum = jnp.zeros_like(pre_values)
    for offset in range(rim_width + 1):
        shifted = extended[:, rim_width - offset : rim_width - offset + tok_count, :]
        conv_sum = conv_sum + tap_weights[:, offset] * shifted * tap_masks[offset][:, :, None]
    return conv_sum * jax.nn.silu(pre_values)


def linear_forward(stream, weights, layout_info, gather_more):
    norm_gain, qk_weight, value_weight, tap_weights = weights
    micro_count, tok_count, model_width = stream.shape
    normed_rows, norm_back = jax.vjp(normed, stream, norm_gain.astype(jnp.float32))
    normed_low = normed_rows.astype(jnp.bfloat16)
    qk_rows = matmul(normed_low, qk_weight).astype(jnp.bfloat16)
    pre_values = matmul(normed_low, value_weight)
    rim_rows = passed_along(pre_values[:, tok_count - CONV + 1 :, :], "ctx", 1)
    value_rows, conv_back = jax.vjp(
        partial(conv_gate, tap_masks=layout_info["taps"]),
        pre_values,
        rim_rows,
        tap_weights.astype(jnp.float32),
    )
    values = value_rows.astype(jnp.bfloat16)
    tables, base = feature_tables()
    state_shape = (micro_count, HEADS // 2 + 1, SENT, 128)
    (state,) = by_pair(
        states_kernel,
        "states",
        [(qk_rows, "key"), (values, "pair"), (layout_info["last"], "micro"), (tables, "whole"), (base, "whole")],
        [(state_shape, jnp.bfloat16, "micro")],
    )
    *more, state_in = gather_more((state, layout_info["keep"]))
    out_weight = more[0]
    shared = [
        (qk_rows, "query"),
        (qk_rows, "key"),
        (values, "pair"),
        (state_in, "micro"),
        (layout_info["causal"], "micro"),
        (layout_info["carried"], "micro"),
        (tables, "whole"),
        (base, "whole"),
    ]
    attended_low, den = by_pair(
        attend_kernel,
        "linear_attend",
        shared,
        [(values.shape, jnp.bfloat16, "pair"), (values.shape, jnp.float32, "pair")],
    )
    branch = matmul(attended_low, out_weight)
    return (
        stream + branch,
        (norm_back, normed_low, conv_back, shared, attended_low, den),
        more,
    )


def linear_backward(grad_stream, residuals, weights, layout_info, other_gains, sum_others):
    norm_back, normed_low, conv_back, shared, attended_low, den = residuals
    qk_weight, value_weight, out_weight = (weights[1], weights[2], weights[4])
    micro_count, tok_count, model_width = grad_stream.shape
    grad_branch = grad_stream.astype(jnp.bfloat16)
    grad_out = (flat(attended_low), flat(grad_branch))
    grad_attended = matmul_back(grad_branch, out_weight)
    f32, low = jnp.float32, jnp.bfloat16
    feat_shape = (micro_count, tok_count, HEADS * FEAT)
    state_shape = (micro_count, HEADS // 2 + 1, SENT, 128)
    grad_query, grad_key, grad_value, grad_state = by_pair(
        attend_back_kernel,
        "linear_attend_back",
        shared + [(grad_attended, "pair"), (attended_low, "pair"), (den, "pair")],
        [
            (feat_shape, f32, "micro"),
            (feat_shape, f32, "micro"),
            (grad_stream.shape, f32, "pair"),
            (state_shape, low, "micro"),
        ],
    )
    *sums, later = sum_others(grad_out, (grad_state, layout_info["keep"]))
    grad_key, grad_value = by_pair(
        states_back_kernel,
        "states_back",
        [shared[1], shared[2], (layout_info["last"], "micro"), shared[6], shared[7], (later, "micro")]
        + [(grad_key, "micro"), (grad_value, "pair")],
        [(feat_shape, f32, "micro"), (grad_stream.shape, f32, "pair")],
    )
    grad_qk = jnp.concatenate([grad_query, grad_key], axis=-1).astype(low)
    grad_pre, grad_rim, grad_taps = conv_back(grad_value)
    returned = passed_along(grad_rim, "ctx", -1)
    grad_pre = grad_pre.at[:, tok_count - CONV + 1 :, :].add(returned)
    grad_pre_low = grad_pre.astype(jnp.bfloat16)
    grad_normed = matmul_back(grad_qk, qk_weight) + matmul_back(grad_pre_low, value_weight)
    grad_input, grad_gain = norm_back(grad_normed)
    small = jnp.concatenate([grad_gain[:, None], other_gains, grad_taps], axis=1)
    operand = flat(normed_low)
    own = summed_to_owners(
        [
            as_product(small)(operand.shape[0]),
            (operand, flat(grad_qk)),
            (operand, flat(grad_pre_low)),
        ],
        3,
        model_width // (lax.axis_size("dp") * lax.axis_size("ctx")),
    )
    return (grad_stream + grad_input, own, sums)


BAND = 128
RIM = 64


def band_probabilities(queries, keys, mask):
    score = jnp.where(mask > 0, dot_nt(queries, keys) * 0.125, masked_fill)
    power = jnp.exp(score - jnp.max(score, axis=1, keepdims=True))
    return power / jnp.sum(power, axis=1, keepdims=True)


def band_attend(queries, keys, values, mask):
    lane = lanes_of(queries.shape, 1)
    outs = []
    for own in (lane < 64, lane >= 64):
        chance = band_probabilities(only(own, queries), keys, mask)
        outs.append(dot_nn(chance.astype(jnp.bfloat16), values))
    return jnp.where(lane < 64, outs[0], outs[1]).astype(jnp.bfloat16)


def band_back(queries, grads, keys, values, mask):
    low = jnp.bfloat16
    lane = lanes_of(queries.shape, 1)
    dqueries, dkeys, dvalues = [], 0.0, 0.0
    for own in (lane < 64, lane >= 64):
        own_queries, own_grads = only(own, queries), only(own, grads)
        chance = band_probabilities(own_queries, keys, mask)
        dchance = dot_nt(own_grads, values)
        inner = jnp.sum(dchance * chance, axis=1, keepdims=True)
        dscore = (chance * (dchance - inner)).astype(low)
        dqueries.append(dot_nn(dscore, keys) * 0.125)
        dkeys += dot_tn(dscore, own_queries) * 0.125
        dvalues += dot_tn(chance.astype(low), own_grads)
    return jnp.where(lane < 64, dqueries[0], dqueries[1]).astype(low), dkeys, dvalues


def with_rim(own_ref, rim_ref, here):
    own, rim = own_ref[0, :, here], rim_ref[0, :, here]
    return jnp.concatenate([jnp.zeros((BAND - RIM, 128), own.dtype), rim, own], axis=0)


def first_band_kernel(query_ref, key_ref, value_ref, rim_key_ref, rim_value_ref, mask_ref, out_ref):
    for _, here in pairs_of(0):
        keys, values = with_rim(key_ref, rim_key_ref, here), with_rim(value_ref, rim_value_ref, here)
        out_ref[0, :, here] = band_attend(query_ref[0, :, here], keys, values, mask_ref[0])


def later_bands_kernel(query_ref, key_ref, value_ref, mask_ref, out_ref):
    for _, here in pairs_of(0):
        for first in range(BAND, query_ref.shape[1], BAND):
            rows, near = slice(first, first + BAND), slice(first - BAND, first + BAND)
            out_ref[0, first - BAND : first, here] = band_attend(
                query_ref[0, rows, here], key_ref[0, near, here], value_ref[0, near, here], mask_ref[0, rows]
            )


def first_band_back_kernel(
    query_ref, key_ref, value_ref, rim_key_ref, rim_value_ref, mask_ref, grad_ref, dquery_ref, dkey_ref,
    dvalue_ref, drim_key_ref, drim_value_ref,
):
    for _, here in pairs_of(0):
        keys, values = with_rim(key_ref, rim_key_ref, here), with_rim(value_ref, rim_value_ref, here)
        dquery, dkey, dvalue = band_back(
            query_ref[0, :, here], grad_ref[0, :, here], keys, values, mask_ref[0]
        )
        dquery_ref[0, :, here] = dquery
        dkey_ref[0, :, here] = dkey[BAND:]
        dvalue_ref[0, :, here] = dvalue[BAND:]
        drim_key_ref[0, :, here] = dkey[BAND - RIM : BAND].astype(jnp.bfloat16)
        drim_value_ref[0, :, here] = dvalue[BAND - RIM : BAND].astype(jnp.bfloat16)


def later_bands_back_kernel(
    query_ref, key_ref, value_ref, mask_ref, grad_ref, first_dkey_ref, first_dvalue_ref, dquery_ref, dkey_ref,
    dvalue_ref,
):
    for _, here in pairs_of(0):
        dkey_ref[0, :BAND, here] = first_dkey_ref[0, :, here]
        dvalue_ref[0, :BAND, here] = first_dvalue_ref[0, :, here]
        for first in range(BAND, query_ref.shape[1], BAND):
            rows, before, near = (
                slice(first, first + BAND),
                slice(first - BAND, first),
                slice(first - BAND, first + BAND),
            )
            dquery, dkey, dvalue = band_back(
                query_ref[0, rows, here],
                grad_ref[0, rows, here],
                key_ref[0, near, here],
                value_ref[0, near, here],
                mask_ref[0, rows],
            )
            dquery_ref[0, before, here] = dquery
            dkey_ref[0, before, here] += dkey[:BAND]
            dvalue_ref[0, before, here] += dvalue[:BAND]
            dkey_ref[0, rows, here] = dkey[BAND:]
            dvalue_ref[0, rows, here] = dvalue[BAND:]


def by_window(kernel, name, ins, outs):
    micro, steps = ins[0][0].shape[0], HEADS // 2 // PER

    def spec(rows, place, width):
        if place is None:
            return pl.BlockSpec((1, rows, width), lambda m, p: (m, 0, 0))
        return pl.BlockSpec((1, rows, PER * 128), lambda m, p: (m, 0, p + place * steps))

    return pl.pallas_call(
        kernel,
        grid=(micro, steps),
        in_specs=[spec(rows, place, array.shape[2]) for array, rows, place in ins],
        out_specs=[spec(rows, 0, 0) for rows, _ in outs],
        out_shape=[jax.ShapeDtypeStruct((micro, rows, HEADS * 64), dtype) for rows, dtype in outs],
        compiler_params=pltpu.CompilerParams(vmem_limit_bytes=48 * 2**20),
        name=name,
    )(*[array for array, _, _ in ins])


def window_forward(stream, weights, layout_info):
    norm_gain, qkv_weight, out_weight = weights
    micro_count, tok_count, model_width = stream.shape
    normed_rows, norm_back = jax.vjp(normed, stream, norm_gain.astype(jnp.float32))
    normed_low = normed_rows.astype(jnp.bfloat16)
    qkv_rows = matmul(normed_low, qkv_weight).astype(jnp.bfloat16)
    rim_rows = passed_along(qkv_rows[:, tok_count - RIM :, model_width:], "ctx", 1)
    mask = layout_info["window"]
    parts = []
    if tok_count > BAND:
        parts = by_window(
            later_bands_kernel,
            "window_later",
            [(qkv_rows, tok_count, 0), (qkv_rows, tok_count, 1), (qkv_rows, tok_count, 2), (mask, tok_count, None)],
            [(tok_count - BAND, jnp.bfloat16)],
        )
        rim_rows, parts = lax.optimization_barrier((rim_rows, parts))
    (start,) = by_window(
        first_band_kernel,
        "window_first",
        [(qkv_rows, BAND, 0), (qkv_rows, BAND, 1), (qkv_rows, BAND, 2), (rim_rows, RIM, 0), (rim_rows, RIM, 1)]
        + [(mask, BAND, None)],
        [(BAND, jnp.bfloat16)],
    )
    attended = jnp.concatenate([start] + list(parts), axis=1)
    branch = matmul(attended, out_weight)
    return (stream + branch, (norm_back, normed_low, qkv_rows, rim_rows, attended))


def window_backward(grad_stream, residuals, weights, layout_info):
    norm_back, normed_low, qkv_rows, rim_rows, attended = residuals
    qkv_weight, out_weight = (weights[1], weights[2])
    micro_count, tok_count, model_width = grad_stream.shape
    f32, low = jnp.float32, jnp.bfloat16
    grad_branch = grad_stream.astype(low)
    grad_out = (flat(attended), flat(grad_branch))
    grad_attended = matmul_back(grad_branch, out_weight).astype(low)
    mask = layout_info["window"]
    grad_query, grad_key, grad_value, rim_key, rim_value = by_window(
        first_band_back_kernel,
        "window_first_back",
        [(qkv_rows, BAND, 0), (qkv_rows, BAND, 1), (qkv_rows, BAND, 2), (rim_rows, RIM, 0), (rim_rows, RIM, 1)]
        + [(mask, BAND, None), (grad_attended, BAND, 0)],
        [(BAND, low), (BAND, f32), (BAND, f32), (RIM, low), (RIM, low)],
    )
    returned = passed_along(jnp.concatenate([rim_key, rim_value], axis=-1), "ctx", -1)
    if tok_count > BAND:
        more_query, grad_key, grad_value = by_window(
            later_bands_back_kernel,
            "window_later_back",
            [(qkv_rows, tok_count, 0), (qkv_rows, tok_count, 1), (qkv_rows, tok_count, 2), (mask, tok_count, None)]
            + [(grad_attended, tok_count, 0), (grad_key, BAND, 0), (grad_value, BAND, 0)],
            [(tok_count - BAND, low), (tok_count, f32), (tok_count, f32)],
        )
        grad_query = jnp.concatenate([grad_query, more_query], axis=1)
        returned, grad_key = lax.optimization_barrier((returned, grad_key))
    returned = returned.astype(f32)
    returned = jnp.pad(returned, ((0, 0), (tok_count - RIM, 0), (0, 0)))
    grad_qkv = jnp.concatenate(
        [
            grad_query,
            (grad_key + returned[..., :model_width]).astype(low),
            (grad_value + returned[..., model_width:]).astype(low),
        ],
        axis=-1,
    )
    grad_qkv_weight = (flat(normed_low), flat(grad_qkv))
    grad_input, grad_gain = norm_back(lax.optimization_barrier(matmul_back(grad_qkv, qkv_weight)))
    return (grad_stream + grad_input, (grad_gain, grad_qkv_weight, grad_out))


def ffn_forward(stream, weights):
    norm_gain, gate_up, down_weight = weights
    hidden_width = down_weight.shape[0]
    normed_rows, norm_back = jax.vjp(normed, stream, norm_gain.astype(jnp.float32))
    normed_low = normed_rows.astype(jnp.bfloat16)
    projected = matmul(normed_low, gate_up)
    hidden = (jax.nn.silu(projected[..., :hidden_width]) * projected[..., hidden_width:]).astype(
        jnp.bfloat16
    )
    hidden, projected = lax.optimization_barrier((hidden, projected.astype(jnp.bfloat16)))
    branch = matmul(hidden, down_weight)
    return (stream + branch, (norm_back, normed_low, projected, hidden))


def ffn_backward(grad_stream, residuals, weights):
    norm_back, normed_low, projected, hidden = residuals
    gate_up, down_weight = (weights[1], weights[2])
    hidden_width = down_weight.shape[0]
    grad_branch = grad_stream.astype(jnp.bfloat16)
    grad_down = (flat(hidden), flat(grad_branch))
    grad_hidden = matmul_back(grad_branch, down_weight)
    gate_part = projected[..., :hidden_width].astype(jnp.float32)
    up_part = projected[..., hidden_width:].astype(jnp.float32)
    sigmoid_gate = jax.nn.sigmoid(gate_part)
    grad_gate = grad_hidden * up_part * sigmoid_gate * (1.0 + gate_part * (1.0 - sigmoid_gate))
    grad_up = grad_hidden * gate_part * sigmoid_gate
    grad_projected = jnp.concatenate([grad_gate, grad_up], axis=-1).astype(jnp.bfloat16)
    grad_gate_up = (flat(normed_low), flat(grad_projected))
    grad_input, grad_gain = norm_back(lax.optimization_barrier(matmul_back(grad_projected, gate_up)))
    return (grad_stream + grad_input, (grad_gain, grad_gate_up, grad_down))


def body(
    tokens_in,
    seq_lengths,
    norm_linear,
    proj_qk,
    proj_values,
    conv_taps,
    out_linear,
    norm_ffn_one,
    gate_up_one,
    down_one,
    norm_window,
    proj_qkv,
    out_window,
    norm_ffn_two,
    gate_up_two,
    down_two,
    cotangent,
):
    tok_count = tokens_in.shape[2]
    layout_info = layout(seq_lengths, tok_count)
    stream = tokens_in[:, 0].astype(jnp.float32)
    small = jnp.concatenate(
        [
            norm_linear[:, None],
            norm_ffn_one[:, None],
            norm_window[:, None],
            norm_ffn_two[:, None],
            conv_taps,
            jnp.zeros((conv_taps.shape[0], 121), jnp.bfloat16),
        ],
        axis=1,
    )
    n_dp, n_ctx = lax.axis_size("dp"), lax.axis_size("ctx")
    first_shards = [small, proj_qk, proj_values]
    small, w_qk, w_values = gather_all(first_shards, n_dp, n_ctx, chunks_of(first_shards), cid=0)

    def gather_more(state):
        shards = [out_linear, gate_up_one, down_one, proj_qkv, out_window, down_two]
        return gather_all(shards, n_dp, n_ctx, chunks_of(shards), cid=2, carry=1, state=state)

    middle, saved_linear, more = linear_forward(
        stream, (small[:, 0], w_qk, w_values, small[:, 4:7]), layout_info, gather_more
    )
    w_out_linear, w_gu_one, w_dn_one, w_qkv, w_out_window, w_dn_two = more
    w_gu_two = lax.all_gather(gate_up_two, ("dp", "ctx"), axis=0, tiled=True)
    layer_one = (small[:, 0], w_qk, w_values, small[:, 4:7], w_out_linear, small[:, 1], w_gu_one, w_dn_one)
    layer_two = (small[:, 2], w_qkv, w_out_window, small[:, 3], w_gu_two, w_dn_two)
    first_out, saved_ffn_one = ffn_forward(middle, layer_one[5:])
    second_mid, saved_window = window_forward(first_out, layer_two[:3], layout_info)
    closing, saved_ffn_two = ffn_forward(second_mid, layer_two[3:])
    valid_rows = layout_info["valid"][:, :, None]
    output = (closing * valid_rows).astype(jnp.bfloat16)[:, None]
    grad_stream = cotangent[:, 0].astype(jnp.float32) * valid_rows
    grad_stream, grads_ffn_two = ffn_backward(grad_stream, saved_ffn_two, layer_two[3:])
    operand, gradient = grads_ffn_two[1]
    partial_sums = jnp.einsum("tr,te->re", operand, gradient, preferred_element_type=jnp.float32)
    partial_sums = partial_sums.astype(jnp.bfloat16)
    for axis in ("dp", "ctx"):
        partial_sums = lax.psum_scatter(partial_sums, axis, scatter_dimension=0, tiled=True)
    sum_gate_up_two = partial_sums.astype(jnp.float32)
    grad_stream, grads_window = window_backward(
        grad_stream, saved_window, layer_two[:3], layout_info
    )
    grad_stream, grads_ffn_one = ffn_backward(grad_stream, saved_ffn_one, layer_one[5:])
    other_gains = jnp.stack([grads_ffn_one[0], grads_window[0], grads_ffn_two[0]], axis=1)

    def sum_others(of_out, state):
        products = [
            of_out,
            grads_ffn_one[1],
            grads_ffn_one[2],
            grads_window[1],
            grads_window[2],
            grads_ffn_two[2],
        ]
        return summed_to_owners(products, 1, out_linear.shape[0], -1, state)

    grad_stream, own_sums, sums = linear_backward(
        grad_stream, saved_linear, layer_one[:5], layout_info, other_gains, sum_others
    )
    small, grad_qk, grad_values = own_sums
    tokens_grad = grad_stream.astype(jnp.bfloat16)[:, None]
    return (
        output,
        tokens_grad,
        small[:, 0],
        grad_qk,
        grad_values,
        small[:, 4:7],
        sums[0],
        small[:, 1],
        sums[1],
        sums[2],
        small[:, 2],
        sums[3],
        sums[4],
        small[:, 3],
        sum_gate_up_two,
        sums[5],
    )


def solution(mesh):
    placed = (
        P(None, "dp", "ctx", None),
        P(None, "dp", None),
        P(("dp", "ctx")),
        P(("dp", "ctx"), None),
        P(("dp", "ctx"), None),
        P(("dp", "ctx"), None),
        P(("dp", "ctx"), None),
        P(("dp", "ctx")),
        P(("dp", "ctx"), None),
        P(("dp", "ctx"), None),
        P(("dp", "ctx")),
        P(("dp", "ctx"), None),
        P(("dp", "ctx"), None),
        P(("dp", "ctx")),
        P(("dp", "ctx"), None),
        P(("dp", "ctx"), None),
        P(None, "dp", "ctx", None),
    )
    return jax.shard_map(
        body,
        mesh=mesh,
        in_specs=placed,
        out_specs=(
            P(None, "dp", "ctx", None),
            P(None, "dp", "ctx", None),
            P(("dp", "ctx")),
            P(("dp", "ctx"), None),
            P(("dp", "ctx"), None),
            P(("dp", "ctx"), None),
            P(("dp", "ctx"), None),
            P(("dp", "ctx")),
            P(("dp", "ctx"), None),
            P(("dp", "ctx"), None),
            P(("dp", "ctx")),
            P(("dp", "ctx"), None),
            P(("dp", "ctx"), None),
            P(("dp", "ctx")),
            P(("dp", "ctx"), None),
            P(("dp", "ctx"), None),
        ),
        check_vma=False,
    )
```

```python
from functools import partial
import math

import jax
import jax.numpy as jnp
import numpy as np
from jax import lax
from jax.experimental import pallas as pl
from jax.experimental.pallas import tpu as pltpu
from jax.sharding import PartitionSpec as P

HEADS = 16
FEAT = 16
WINDOW = 64
CONV = 3


epsilon = 1e-05
masked_fill = -1e30
highest = lax.Precision.HIGHEST


MESH = pl.DeviceIdType.MESH

def carried(sign, n_ctx, dp, ctx, own, keep, out, came, total, sent, arrived):
    first, last = (0, n_ctx - 1) if sign > 0 else (n_ctx - 1, 0)
    low, f32 = jnp.bfloat16, jnp.float32
    micro, planes, rows = own.shape[:3]

    def copy(m, p):
        return pltpu.make_async_remote_copy(
            src_ref=total.at[m, p],
            dst_ref=came.at[m, p],
            send_sem=sent.at[m, p],
            recv_sem=arrived.at[m, p],
            device_id=(dp, lax.rem(ctx + sign + n_ctx, n_ctx)),
            device_id_type=MESH,
        )

    def act(i):
        m, p = i // planes, i % planes

        @pl.when(ctx != first)
        def _():
            copy(m, p).wait_recv()
            value = came[m, p]
            out[m, p, :rows] = value
            total[m, p] = (own[m, p].astype(f32) + keep[m, 0:1] * value.astype(f32)).astype(low)

        @pl.when(ctx == first)
        def _():
            out[m, p, :rows] = jnp.zeros((rows, 128), low)
            total[m, p] = own[m, p]

        @pl.when(ctx != last)
        def _():
            copy(m, p).start()

    def finish():
        for m in range(micro):
            for p in range(planes):
                out[m, p, rows:] = jnp.zeros((out.shape[2] - rows, 128), low)

        @pl.when(ctx != last)
        def _():
            for m in range(micro):
                for p in range(planes):
                    copy(m, p).wait_send()

    return micro * planes, act, finish


def carry_specs(state):
    whole = pl.BlockSpec(memory_space=pltpu.VMEM)
    shape = state.shape[:2] + (TERMS,) + state.shape[3:]
    held = pltpu.VMEM(state.shape, jnp.bfloat16)
    sems = pltpu.SemaphoreType.DMA(state.shape[:2])
    return [whole, whole], [whole], [jax.ShapeDtypeStruct(shape, jnp.bfloat16)], [held, held, sems, sems]


def gather_kernel(n_dp, n_ctx, chunks, lag, n_w, carry, *refs):
    n_c = 2 if carry else 0
    ins, outs = refs[:n_w], refs[n_w + n_c:2 * n_w + n_c]
    local_sem, send_sem, recv_sem = refs[2 * n_w + 3 * n_c // 2:][:3]
    dp, ctx = lax.axis_index("dp"), lax.axis_index("ctx")
    bits = [1 << i for i in range(n_dp.bit_length() - 1)]
    low_bits, (bit_x, bit_y) = bits[:-2], bits[-2:]
    barrier = pltpu.get_barrier_semaphore()
    greeted = 0
    for bit in bits:
        pl.semaphore_signal(barrier, inc=1, device_id=(dp ^ bit, ctx), device_id_type=MESH)
        greeted += 1
    for hop in range(1, n_ctx):
        pl.semaphore_signal(barrier, inc=1, device_id=(dp, lax.rem(ctx + hop, n_ctx)), device_id_type=MESH)
        greeted += 1
    pl.semaphore_wait(barrier, greeted)
    sends = []

    def piece(c, start, shards):
        w, col, width = chunks[c]
        return outs[w].at[pl.ds(start, shards), :, pl.ds(col, width)]

    def send(c, slot, start, rows, target, src=None):
        where = piece(c, start, rows)
        copy = pltpu.make_async_remote_copy(
            src_ref=where if src is None else src, dst_ref=where,
            send_sem=send_sem.at[c, slot], recv_sem=recv_sem.at[c, slot],
            device_id=target, device_id_type=MESH)
        copy.start()
        sends.append(copy)

    def arrive(c, slot, start, rows):
        where = piece(c, start, rows)
        pltpu.make_async_remote_copy(
            src_ref=where, dst_ref=where, send_sem=send_sem.at[c, slot], recv_sem=recv_sem.at[c, slot],
            device_id=(dp ^ 1, ctx), device_id_type=MESH).wait_recv()

    def stage_ctx(c):
        w, col, width = chunks[c]
        own = ins[w].at[:, :, pl.ds(col, width)]
        start = dp * n_ctx + ctx
        for hop in range(1, n_ctx):
            send(c, hop - 1, start, 1, (dp, lax.rem(ctx + hop, n_ctx)), src=own)
        pltpu.make_async_copy(own, piece(c, start, 1), local_sem.at[c]).start()

    base = n_ctx - 1
    SX, SY, SDX, SDY, SC = base, base + 1, base + 2, base + 3, base + 4

    def stage_sides(c):
        w, col, width = chunks[c]
        for hop in range(1, n_ctx):
            arrive(c, hop - 1, dp * n_ctx + lax.rem(ctx - hop + n_ctx, n_ctx), 1)
        own = ins[w].at[:, :, pl.ds(col, width)]
        pltpu.make_async_copy(own, piece(c, dp * n_ctx + ctx, 1), local_sem.at[c]).wait()
        group = n_ctx
        send(c, SX, dp * group, group, (dp ^ bit_x, ctx))
        send(c, SY, dp * group, group, (dp ^ bit_y, ctx))

    def stage_diag(c):
        group = n_ctx
        a0, an, b0, bn = 0, n_ctx // 2, n_ctx // 2, n_ctx - n_ctx // 2
        arrive(c, SX, (dp ^ bit_x) * group, group)
        send(c, SDY, (dp ^ bit_x) * group + a0, an, (dp ^ bit_y, ctx))
        arrive(c, SY, (dp ^ bit_y) * group, group)
        send(c, SDX, (dp ^ bit_y) * group + b0, bn, (dp ^ bit_x, ctx))

    def low_slot(level, j):
        return SC + 4 * ((1 << level) - 1) + j

    def quads(base_dp, level):
        out = []
        for top in range(4):
            for low in range(1 << level):
                flip = (bit_x if top & 1 else 0) | (bit_y if top & 2 else 0)
                for i in range(level):
                    if low >> i & 1:
                        flip |= low_bits[len(low_bits) - 1 - i]
                out.append(base_dp ^ flip)
        return out

    def stage_low(c, level):
        group = n_ctx
        if level == 0:
            a0, an, b0, bn = 0, n_ctx // 2, n_ctx // 2, n_ctx - n_ctx // 2
            arrive(c, SDY, (dp ^ bit_x ^ bit_y) * group + a0, an)
            arrive(c, SDX, (dp ^ bit_x ^ bit_y) * group + b0, bn)
        else:
            bit = low_bits[len(low_bits) - level]
            for j, block in enumerate(quads(dp ^ bit, level - 1)):
                arrive(c, low_slot(level - 1, j), block * group, group)
        if level < len(low_bits):
            bit = low_bits[len(low_bits) - 1 - level]
            for j, block in enumerate(quads(dp, level)):
                send(c, low_slot(level, j), block * group, group, (dp ^ bit, ctx))

    stages = [stage_ctx, stage_sides, stage_diag] + [partial(stage_low, level=l) for l in range(len(low_bits) + 1)]
    depth = len(stages)
    turns = len(chunks) + (depth - 1) * lag
    due = {}
    if carry:
        own, keep = refs[n_w:n_w + 2]
        n_pieces, act, finish = carried(carry, n_ctx, dp, ctx, own, keep, refs[2 * n_w + 2], *refs[2 * n_w + 6:])
        for place in range(n_ctx):
            for i in range(n_pieces):
                due.setdefault(place + i // 2, []).append((place, i))
        turns = max(turns, max(due) + 1)
    for t in range(turns):
        for place, i in due.get(t, []):
            @pl.when(ctx == (place if carry > 0 else n_ctx - 1 - place))
            def _():
                act(i)
        for s in range(depth):
            c = t - s * lag
            if 0 <= c < len(chunks):
                stages[s](c)
    if carry:
        finish()
    for copy in sends:
        copy.wait_send()

def gather_all(weights, n_dp, n_ctx, chunks, lag=1, cid=0, carry=0, state=()):
    n = len(weights)
    places = n_dp * n_ctx
    slots = n_ctx - 1 + 4 + 4 * (n_dp // 4 - 1)
    more_in, more_out, more_shape, more_scratch = carry_specs(state[0]) if carry else ([], [], [], [])
    full = pl.pallas_call(
        partial(gather_kernel, n_dp, n_ctx, chunks, lag, n, carry),
        out_shape=[jax.ShapeDtypeStruct((places,) + w.shape, w.dtype) for w in weights] + more_shape,
        in_specs=[pl.BlockSpec(memory_space=pltpu.HBM)] * n + more_in,
        out_specs=[pl.BlockSpec(memory_space=pltpu.HBM)] * n + more_out,
        scratch_shapes=[pltpu.SemaphoreType.DMA((len(chunks),)), pltpu.SemaphoreType.DMA((len(chunks), slots)), pltpu.SemaphoreType.DMA((len(chunks), slots))]
        + more_scratch,
        compiler_params=pltpu.CompilerParams(collective_id=cid, has_side_effects=True),
        name="gather_weights")(*[w[None] for w in weights], *state)
    return [f.reshape(places * f.shape[1], f.shape[2]) for f in full[:n]] + list(full[n:])


WIDE = 512
SLOTS_HELD = 8
APART = 4


def scatter_kernel(n_dp, n_ctx, plan, lags, pieces, n_y, n_o, carry, *refs):
    n_x = len(pieces)
    xs, ys, refs = refs[:n_x], refs[n_x : n_x + n_y], refs[n_x + n_y :]
    state, refs = (refs[:2], refs[2:]) if carry else ((), refs)
    outs, refs = refs[:n_o], refs[n_o:]
    state_out, refs = (refs[:1], refs[1:]) if carry else ((), refs)
    bits = [1 << i for i in range(n_dp.bit_length() - 1)]
    low_bits, (bit_x, bit_y) = bits[:-2], bits[-2:]
    n_low = len(low_bits)
    x_all, y_all, natural = refs[0], refs[1], refs[-1]
    low_out, low_in = refs[2 : 2 + n_low], refs[2 + n_low : 2 + 2 * n_low]
    refs = refs[2 + 2 * n_low :]
    cross, cross_y, cross_x, side_x, side_y, came_x, came_y, shards, came_ctx, result = refs[:10]
    x_sem, y_sem, out_sem, sent, arrived, credit = refs[10:16]
    held = y_all.shape[0]
    dp, ctx = lax.axis_index("dp"), lax.axis_index("ctx")
    group = cross.shape[1]
    half = group // 2
    rows = group // n_ctx
    f32, low = jnp.float32, jnp.bfloat16
    A_CY, A_CX, A_X, A_Y, A_Z = n_low, n_low + 1, n_low + 2, n_low + 3, n_low + 4
    C_X, C_Y, C_Z = n_low, n_low + 1, n_low + 2

    def at_ctx(hop):
        return (dp, lax.rem(ctx + hop, n_ctx))

    barrier = pltpu.get_barrier_semaphore()
    for bit in bits:
        pl.semaphore_signal(barrier, inc=1, device_id=(dp ^ bit, ctx), device_id_type=MESH)
    for hop in range(1, n_ctx):
        pl.semaphore_signal(barrier, inc=1, device_id=at_ctx(hop), device_id_type=MESH)
    pl.semaphore_wait(barrier, len(bits) + n_ctx - 1)

    bounds, count = [], 0
    for segment in plan:
        bounds.append((count, count + segment[5]))
        count += segment[5]
    laid_at = [sum(max(1, n) for n in pieces[:i]) for i in range(n_x)]
    x_first = {}
    for segment, (first, _) in zip(plan, bounds):
        x_first.setdefault(segment[0], first)

    def x_copy(i):
        if pieces[i]:
            return pltpu.make_async_copy(xs[i], x_all.at[pl.ds(laid_at[i], pieces[i])], x_sem.at[i])
        return pltpu.make_async_copy(xs[i], natural.at[pieces[:i].count(0)], x_sem.at[i])

    def x_ready(i):
        x_copy(i).wait()
        if not pieces[i]:
            for place in range(n_dp):
                value = natural[pieces[:i].count(0), :, place * group : (place + 1) * group]
                x_all[laid_at[i], place] = value.T

    for i in range(n_x):
        x_copy(i).start()

    def y_part(slot, number, where, to, width):
        pltpu.make_async_copy(
            ys[number].at[:, pl.ds(where, width)], y_all.at[slot, :, pl.ds(to, width)], y_sem.at[slot]
        ).start()

    def y_fetch(k, slot, numbers):
        if len(numbers) == 1:
            y_part(slot, numbers[0], pl.multiple_of(k * WIDE, WIDE), 0, WIDE)
            return
        width = ys[numbers[0]].shape[1]
        whole, left = width // WIDE, width % WIDE

        @pl.when(k < whole)
        def _():
            y_part(slot, numbers[0], pl.multiple_of(k * WIDE, WIDE), 0, WIDE)

        if left:

            @pl.when(k == whole)
            def _():
                y_part(slot, numbers[0], whole * WIDE, 0, left)
                y_part(slot, numbers[1], 0, left, WIDE - left)

        @pl.when(k >= whole + (1 if left else 0))
        def _():
            y_part(slot, numbers[1], pl.multiple_of(k * WIDE - width, 128), 0, WIDE)

    def y_start(c):
        slot = lax.rem(c, held)
        for segment, (first, last) in zip(plan, bounds):

            @pl.when((c >= first) & (c < last))
            def _():
                y_fetch(c - first, slot, segment[1])

    def x_place(c):
        return sum((c >= first).astype(jnp.int32) for first in sorted(x_first.values())[1:])

    def partial_sum(c, flip):
        return jnp.dot(
            x_all[x_place(c), dp ^ flip], y_all[lax.rem(c, held)], preferred_element_type=f32
        )

    def rest(level):
        free = low_bits[level + 1 :] + [bit_x, bit_y]
        return [sum(b for i, b in enumerate(free) if n >> i & 1) for n in range(1 << len(free))]

    def summed(c, flip, levels):
        total = partial_sum(c, flip)
        for level in range(levels):
            total = total + low_in[level][lax.rem(c, held), rest(level).index(flip)].astype(f32)
        return total

    def remote(src, dst, slot, kind, target):
        return pltpu.make_async_remote_copy(
            src_ref=src,
            dst_ref=dst,
            send_sem=sent.at[slot, kind],
            recv_sem=arrived.at[slot, kind],
            device_id=target,
            device_id_type=MESH,
        )

    def copy_of(slot, kind):
        over_x, over_y = (dp ^ bit_x, ctx), (dp ^ bit_y, ctx)
        if kind < n_low:
            return remote(
                low_out[kind].at[slot], low_in[kind].at[slot], slot, kind, (dp ^ low_bits[kind], ctx)
            )
        if kind == A_CY:
            return remote(cross.at[slot, pl.ds(0, half)], cross_y.at[slot], slot, kind, over_y)
        if kind == A_CX:
            return remote(cross.at[slot, pl.ds(half, half)], cross_x.at[slot], slot, kind, over_x)
        if kind == A_X:
            return remote(side_x.at[slot], came_x.at[slot], slot, kind, over_x)
        if kind == A_Y:
            return remote(side_y.at[slot], came_y.at[slot], slot, kind, over_y)
        hop = kind - A_Z + 1
        there = lax.rem(ctx + hop, n_ctx)
        return remote(shards.at[slot, there], came_ctx.at[slot, hop - 1], slot, kind, (dp, there))

    def need_credit(c, kind):
        @pl.when(c >= held)
        def _():
            pl.semaphore_wait(credit.at[kind], 1)

    def step_low(level, c):
        slot = lax.rem(c, held)
        if level == 0:
            for i in range(n_x):

                @pl.when(c == x_first[laid_at[i]])
                def _():
                    x_ready(i)

            pltpu.make_async_copy(y_all.at[slot], y_all.at[slot], y_sem.at[slot]).wait()
        else:
            copy_of(slot, level - 1).wait_recv()
        need_credit(c, level)
        for j, flip in enumerate(rest(level)):
            low_out[level][slot, j] = summed(c, flip | low_bits[level], level).astype(low)
        copy_of(slot, level).start()

    def step_cross(c):
        slot = lax.rem(c, held)
        if n_low:
            copy_of(slot, n_low - 1).wait_recv()
        need_credit(c, C_X)
        need_credit(c, C_Y)
        cross[slot] = summed(c, bit_x | bit_y, n_low).astype(low)
        copy_of(slot, A_CY).start()
        copy_of(slot, A_CX).start()

    def step_sides(c):
        slot = lax.rem(c, held)
        over_x = summed(c, bit_x, n_low)
        over_y = summed(c, bit_y, n_low)
        copy_of(slot, A_CY).wait_recv()
        side_x[slot, :half] = (over_x[:half] + cross_y[slot].astype(f32)).astype(low)
        side_x[slot, half:] = over_x[half:].astype(low)
        copy_of(slot, A_X).start()
        copy_of(slot, A_CX).wait_recv()
        side_y[slot, :half] = over_y[:half].astype(low)
        side_y[slot, half:] = (over_y[half:] + cross_x[slot].astype(f32)).astype(low)
        copy_of(slot, A_Y).start()

    def step_own(c):
        slot = lax.rem(c, held)
        total = summed(c, 0, n_low)
        copy_of(slot, A_X).wait_recv()
        copy_of(slot, A_Y).wait_recv()
        total = total + came_x[slot].astype(f32) + came_y[slot].astype(f32)
        for j in range(n_ctx):
            shards[slot, j] = total[j * rows : (j + 1) * rows].astype(low)
        for hop in range(1, n_ctx):
            need_credit(c, C_Z + hop - 1)
            copy_of(slot, A_Z + hop - 1).start()

    def out_copy(c, slot, segment, first):
        where = pl.multiple_of((c - first) * WIDE, WIDE)
        _, _, o, row, n_rows, _ = segment
        return pltpu.make_async_copy(
            result.at[slot, pl.ds(0, n_rows)],
            outs[o].at[pl.ds(row, n_rows), pl.ds(where, WIDE)],
            out_sem.at[slot],
        )

    def each_segment(c, act):
        for segment, (first, last) in zip(plan, bounds):

            @pl.when((c >= first) & (c < last))
            def _():
                act(segment, first)

    def out_wait(c):
        slot = lax.rem(c, held)
        each_segment(c, lambda segment, first: out_copy(c, slot, segment, first).wait())

    def step_end(c):
        slot = lax.rem(c, held)

        @pl.when(c >= held)
        def _():
            out_wait(c - held)

        total = shards[slot, ctx].astype(f32)
        for hop in range(1, n_ctx):
            copy_of(slot, A_Z + hop - 1).wait_recv()
            total = total + came_ctx[slot, hop - 1].astype(f32)
        result[slot] = total
        each_segment(c, lambda segment, first: out_copy(c, slot, segment, first).start())
        for kind in range(A_Z + n_ctx - 1):
            copy_of(slot, kind).wait_send()

        @pl.when(c + held < count)
        def _():
            for level, bit in enumerate(low_bits):
                pl.semaphore_signal(credit.at[level], inc=1, device_id=(dp ^ bit, ctx), device_id_type=MESH)
            pl.semaphore_signal(credit.at[C_X], inc=1, device_id=(dp ^ bit_x, ctx), device_id_type=MESH)
            pl.semaphore_signal(credit.at[C_Y], inc=1, device_id=(dp ^ bit_y, ctx), device_id_type=MESH)
            for hop in range(1, n_ctx):
                pl.semaphore_signal(
                    credit.at[C_Z + hop - 1], inc=1, device_id=at_ctx(n_ctx - hop), device_id_type=MESH
                )

    steps = [partial(step_low, level) for level in range(n_low)] + [step_cross, step_sides, step_own, step_end]
    ahead = 2
    for c in range(ahead):
        y_start(jnp.int32(c))

    turns = count + lags[-1]
    if carry:
        n_pieces, act, finish = carried(carry, n_ctx, dp, ctx, *state, *state_out, *refs[16:-1])
        place = ctx if carry > 0 else n_ctx - 1 - ctx
        turns = max(turns, n_pieces + APART * (n_ctx - 1))

    def turn(t, none):
        if carry:
            i = t - APART * place

            @pl.when((i >= 0) & (i < n_pieces))
            def _():
                act(i)

        @pl.when(t + ahead < count)
        def _():
            y_start(t + ahead)

        for step, lag in zip(steps, lags):
            c = t - lag

            @pl.when((c >= 0) & (c < count))
            def _():
                step(c)

        return none

    lax.fori_loop(0, turns, turn, 0)
    if carry:
        finish()
    for c in range(max(0, count - held), count):
        out_wait(jnp.int32(c))


def scatter_sums(xs, ys, out_shapes, plan, n_dp, n_ctx, cid=1, carry=0, state=(), lags=None, held=SLOTS_HELD):
    pieces = [n for _, n in xs]
    tokens = ys[0].shape[0]
    group = [x.shape[1] // n_dp for x, n in xs if not n][0]
    n_low = n_dp.bit_length() - 3
    rows = group // n_ctx
    low, f32 = jnp.bfloat16, jnp.float32
    lags = lags or list(range(n_low + 4))
    low_shapes = [
        pltpu.VMEM((held, n_dp >> (level + 1), group, WIDE), low) for level in range(n_low)
    ]
    half = group // 2
    kinds = n_low + 4 + n_ctx - 1
    more_in, more_out, more_shape, more_scratch = carry_specs(state[0]) if carry else ([], [], [], [])
    return pl.pallas_call(
        partial(scatter_kernel, n_dp, n_ctx, plan, lags, pieces, len(ys), len(out_shapes), carry),
        out_shape=[jax.ShapeDtypeStruct(shape, f32) for shape in out_shapes] + more_shape,
        in_specs=[pl.BlockSpec(memory_space=pl.ANY)] * (len(xs) + len(ys)) + more_in,
        out_specs=[pl.BlockSpec(memory_space=pltpu.HBM)] * len(out_shapes) + more_out,
        scratch_shapes=[
            pltpu.VMEM((sum(max(1, n) for n in pieces), n_dp, group, tokens), low),
            pltpu.VMEM((held, tokens, WIDE), low),
            *low_shapes,
            *low_shapes,
            pltpu.VMEM((held, group, WIDE), low),
            pltpu.VMEM((held, half, WIDE), low),
            pltpu.VMEM((held, half, WIDE), low),
            pltpu.VMEM((held, group, WIDE), low),
            pltpu.VMEM((held, group, WIDE), low),
            pltpu.VMEM((held, group, WIDE), low),
            pltpu.VMEM((held, group, WIDE), low),
            pltpu.VMEM((held, n_ctx, rows, WIDE), low),
            pltpu.VMEM((held, n_ctx - 1, rows, WIDE), low),
            pltpu.VMEM((held, rows, WIDE), f32),
            pltpu.SemaphoreType.DMA((len(xs),)),
            pltpu.SemaphoreType.DMA((held,)),
            pltpu.SemaphoreType.DMA((held,)),
            pltpu.SemaphoreType.DMA((held, kinds)),
            pltpu.SemaphoreType.DMA((held, kinds)),
            pltpu.SemaphoreType.REGULAR((n_low + 2 + n_ctx - 1,)),
            *more_scratch,
            pltpu.VMEM((pieces.count(0), tokens, n_dp * group), low),
        ],
        compiler_params=pltpu.CompilerParams(
            collective_id=cid, has_side_effects=True, vmem_limit_bytes=56 * 2**20
        ),
        name="scatter_sums",
    )(*[x for x, _ in xs], *ys, *state)


def passed_along(value, axis, steps):
    count = lax.axis_size(axis)
    leading, last = (max(0, -steps), min(count, count - steps))
    return lax.ppermute(value, axis, [(source, source + steps) for source in range(leading, last)])


TERMS = 256
SENT = 160
PER = 2


def feature_tables():
    first = np.zeros((FEAT, TERMS), np.float32)
    second = np.zeros((FEAT, TERMS), np.float32)
    base = np.zeros((8, TERMS), np.float32)
    base[0, 0] = base[1, 0] = base[2, 0] = 1.0
    column = 1
    for f in range(FEAT):
        first[f, column] = base[1, column] = 1.0
        base[2, column] = 1.0 / math.sqrt(FEAT)
        column += 1
    for f in range(FEAT):
        for g in range(f, FEAT):
            first[f, column] = second[g, column] = 1.0
            base[2, column] = (0.5 if f == g else 1.0) / FEAT
            column += 1
    tile = np.stack([np.tile(first, (HEADS, 1)), np.tile(second, (HEADS, 1))])
    return jnp.asarray(tile, jnp.bfloat16), jnp.asarray(base)


def dot_nn(a, b):
    return jnp.dot(a, b, preferred_element_type=jnp.float32)


def dot_nt(a, b):
    return lax.dot_general(a, b, (((1,), (1,)), ((), ())), preferred_element_type=jnp.float32)


def dot_tn(a, b):
    return lax.dot_general(a, b, (((0,), (0,)), ((), ())), preferred_element_type=jnp.float32)


def lanes_of(shape, size):
    return lax.broadcasted_iota(jnp.int32, shape, len(shape) - 1) // size


def only(mask, value):
    return jnp.where(mask, value, jnp.zeros_like(value))


def pairs_of(step):
    return [(step * PER + n, slice(128 * n, 128 * (n + 1))) for n in range(PER)]


def twice(value):
    return jnp.concatenate([value, value], axis=0)


def features_apart(value, pair):
    head = lanes_of(value.shape, FEAT)
    return jnp.concatenate([only(head == 2 * pair, value), only(head == 2 * pair + 1, value)], axis=0)


def features_joined(value, pair):
    rows = value.shape[0] // 2
    head = lanes_of((rows, value.shape[1]), FEAT)
    return only(head == 2 * pair, value[:rows]) + only(head == 2 * pair + 1, value[rows:])


def heads_apart(value):
    lane = lanes_of(value.shape, 64)
    return jnp.concatenate([only(lane == 0, value), only(lane == 1, value)], axis=0)


def heads_joined(value):
    rows = value.shape[0] // 2
    return jnp.where(lanes_of((rows, value.shape[1]), 64) == 0, value[:rows], value[rows:])


def at_head(value, pair):
    rows = value.shape[0] // 2
    lane = lanes_of((rows, 128), 1)
    return jnp.concatenate(
        [
            only(lane == 2 * pair, jnp.broadcast_to(value[:rows], (rows, 128))),
            only(lane == 2 * pair + 1, jnp.broadcast_to(value[rows:], (rows, 128))),
        ],
        axis=0,
    )


def factors(rows, tables, base):
    return (dot_nn(rows, tables[0]) + base[0:1], dot_nn(rows, tables[1]) + base[1:2])


def states_kernel(key_ref, value_ref, last_ref, table_ref, base_ref, state_ref):
    step = pl.program_id(1)
    low, f32 = jnp.bfloat16, jnp.float32
    keys, last = key_ref[0], last_ref[0]
    rows = keys.shape[0]
    lane = lanes_of((SENT, 128), 1)
    totals = state_ref[0, HEADS // 2]
    totals = jnp.where(step == 0, jnp.zeros_like(totals), totals)
    for pair, here in pairs_of(step):
        values = value_ref[0, :, here].astype(f32)
        held = jnp.concatenate([(values * last).astype(low), last.astype(low)], axis=1)
        one, two = factors(features_apart(keys, pair), table_ref, base_ref)
        terms = (one * two).astype(low)
        parts = [dot_tn(terms[:rows], held)[:SENT], dot_tn(terms[rows:], held)[:SENT]]
        state_ref[0, pair] = jnp.where(lane < 64, parts[0][:, :128], parts[1][:, :128]).astype(low)
        for side in range(2):
            totals = jnp.where(lane == 2 * pair + side, parts[side][:, 128:].astype(low), totals)
    state_ref[0, HEADS // 2] = totals


def attend_kernel(
    query_ref, key_ref, value_ref, state_ref, mask_ref, carried_ref, table_ref, base_ref, out_ref, den_ref
):
    step = pl.program_id(1)
    low = jnp.bfloat16
    queries, keys = query_ref[0], key_ref[0]
    mask, carried = twice(mask_ref[0]), twice(carried_ref[0][:, :1])
    totals = state_ref[0, HEADS // 2]
    inv_root = 1.0 / math.sqrt(FEAT)
    for pair, here in pairs_of(step):
        values = value_ref[0, :, here]
        held = jnp.concatenate([values, jnp.ones_like(values)], axis=1)
        own = features_apart(queries, pair)
        slope = dot_nt(own * inv_root, keys) + 1.0
        weight = ((0.5 * slope * slope + 0.5) * mask).astype(low)
        one, two = factors(own, table_ref, base_ref)
        terms = (one * two * base_ref[2:3] * carried).astype(low)
        near = dot_nn(weight, held)
        far = dot_nn(terms, jnp.concatenate([state_ref[0, pair], totals], axis=1))
        picked = far[:, 128:] * at_head(jnp.ones((far.shape[0], 1), jnp.float32), pair)
        den = near[:, 128:] + jnp.sum(picked, axis=1, keepdims=True)
        out_ref[0, :, here] = heads_joined((near[:, :128] + far[:, :128]) / den).astype(low)
        den_ref[0, :, here] = heads_joined(den)


def attend_back_kernel(
    query_ref, key_ref, value_ref, state_ref, mask_ref, carried_ref, table_ref, base_ref, grad_ref, out_ref,
    den_ref, dquery_ref, dkey_ref, dvalue_ref, dstate_ref,
):
    step = pl.program_id(1)
    low, f32 = jnp.bfloat16, jnp.float32
    queries, keys = query_ref[0], key_ref[0]
    mask, carried = twice(mask_ref[0]), twice(carried_ref[0][:, :1])
    totals = state_ref[0, HEADS // 2]
    dquery = jnp.zeros(queries.shape, f32)
    dkey = jnp.zeros(queries.shape, f32)
    keys_small = keys * (1.0 / math.sqrt(FEAT))
    dtotals = dstate_ref[0, HEADS // 2].astype(f32)
    dtotals = jnp.where(step == 0, jnp.zeros_like(dtotals), dtotals)
    inv_root = 1.0 / math.sqrt(FEAT)
    for pair, here in pairs_of(step):
        values = value_ref[0, :, here]
        whole_state = jnp.concatenate([state_ref[0, pair], totals], axis=1)
        dnum = grad_ref[0, :, here] / den_ref[0, :, here]
        dden = -jnp.sum(heads_apart(dnum * out_ref[0, :, here].astype(f32)), axis=1, keepdims=True)
        dnum = heads_apart(dnum).astype(low)
        both = jnp.concatenate([dnum, at_head(dden, pair).astype(low)], axis=1)
        own = features_apart(queries, pair)
        own_small = own * inv_root
        slope = dot_nt(own_small, keys) + 1.0
        weight = ((0.5 * slope * slope + 0.5) * mask).astype(low)
        dscore = ((dot_nt(dnum, values) + dden) * (slope * mask)).astype(low)
        dvalue_ref[0, :, here] = dot_tn(weight, dnum)
        dkey += dot_tn(dscore, own_small)
        one, two = factors(own, table_ref, base_ref)
        scale = base_ref[2:3] * carried
        terms = (one * two * scale).astype(low)
        part = dot_tn(terms, both)[:SENT]
        dstate_ref[0, pair] = part[:, :128].astype(low)
        dtotals += part[:, 128:]
        dterms = dot_nt(both, whole_state) * scale
        through = dot_nt((dterms * two).astype(low), table_ref[0])
        through += dot_nt((dterms * one).astype(low), table_ref[1])
        dquery += features_joined(dot_nn(dscore, keys_small) + through, pair)
    dstate_ref[0, HEADS // 2] = dtotals.astype(low)

    @pl.when(step == 0)
    def _():
        dquery_ref[0] = dquery
        dkey_ref[0] = dkey

    @pl.when(step != 0)
    def _():
        dquery_ref[0] += dquery
        dkey_ref[0] += dkey


def states_back_kernel(
    key_ref, value_ref, last_ref, table_ref, base_ref, dstate_ref, dkey_in, dvalue_in, dkey_ref, dvalue_ref
):
    step = pl.program_id(1)
    low, f32 = jnp.bfloat16, jnp.float32
    keys, last = key_ref[0], last_ref[0]
    last_twice = twice(last[:, :1])
    dtotals = dstate_ref[0, HEADS // 2]
    dkey = jnp.zeros(keys.shape, f32)
    for pair, here in pairs_of(step):
        dstate = dstate_ref[0, pair]
        whole = jnp.concatenate([dstate, dtotals], axis=1)
        one, two = factors(features_apart(keys, pair), table_ref, base_ref)
        terms = (one * two).astype(low)
        dvalue_ref[0, :, here] = dvalue_in[0, :, here] + heads_joined(dot_nn(terms, dstate)) * last
        ones = at_head(jnp.ones((terms.shape[0], 1), f32), pair).astype(low)
        both = jnp.concatenate([heads_apart(value_ref[0, :, here]), ones], axis=1)
        dterms = dot_nt(both, whole) * last_twice
        through = dot_nt((dterms * two).astype(low), table_ref[0])
        through += dot_nt((dterms * one).astype(low), table_ref[1])
        dkey += features_joined(through, pair)

    @pl.when(step == 0)
    def _():
        dkey_ref[0] = dkey_in[0] + dkey

    @pl.when(step != 0)
    def _():
        dkey_ref[0] += dkey


def by_pair(kernel, name, ins, outs):
    def spec(kind, shape):
        if kind == "query":
            return pl.BlockSpec((1, shape[1], HEADS * FEAT), lambda m, p: (m, 0, 0))
        if kind == "key":
            return pl.BlockSpec((1, shape[1], HEADS * FEAT), lambda m, p: (m, 0, 1))
        if kind == "pair":
            return pl.BlockSpec((1, shape[1], PER * 128), lambda m, p: (m, 0, p))
        if kind == "micro":
            return pl.BlockSpec((1,) + shape[1:], lambda m, p: (m,) + (0,) * (len(shape) - 1))
        return pl.BlockSpec(shape, lambda m, p: (0,) * len(shape))

    return pl.pallas_call(
        kernel,
        grid=(ins[0][0].shape[0], HEADS // 2 // PER),
        in_specs=[spec(kind, array.shape) for array, kind in ins],
        out_specs=[spec(kind, shape) for shape, _, kind in outs],
        out_shape=[jax.ShapeDtypeStruct(shape, dtype) for shape, dtype, _ in outs],
        compiler_params=pltpu.CompilerParams(vmem_limit_bytes=48 * 2**20),
        name=name,
    )(*[array for array, _ in ins])


def turn_kernel(places, unit, value_ref, out_ref, turned):
    tokens, rows = value_ref.shape
    for first in range(0, rows, 128):
        turned[first : first + 128] = value_ref[:, first : first + 128].T.astype(jnp.float32)
    pieces, n_dp = out_ref.shape[:2]
    n_ctx, shard = places // n_dp, rows // places
    for place in range(places):
        for piece in range(pieces):
            start, count = piece * unit, min(unit, shard - piece * unit)
            value = turned[place * shard + start : place * shard + start + count]
            if count < unit:
                value = jnp.concatenate([value, jnp.zeros((unit - count, tokens), jnp.float32)], axis=0)
            where = place % n_ctx * unit
            out_ref[piece, place // n_ctx, where : where + unit] = value.astype(jnp.bfloat16)


def turned_pieces(value, places, n_dp, unit):
    tokens, rows = value.shape
    pieces = -(-(rows // places) // unit)
    return pl.pallas_call(
        partial(turn_kernel, places, unit),
        out_shape=jax.ShapeDtypeStruct((pieces, n_dp, places // n_dp * unit, tokens), jnp.bfloat16),
        in_specs=[pl.BlockSpec(memory_space=pltpu.VMEM)],
        out_specs=pl.BlockSpec(memory_space=pltpu.VMEM),
        scratch_shapes=[pltpu.VMEM((rows, tokens), jnp.float32)],
        compiler_params=pltpu.CompilerParams(vmem_limit_bytes=48 * 2**20),
        name="turn",
    )(value)


def chunk_plan(products, unit):
    n_dp = lax.axis_size("dp")
    places = n_dp * lax.axis_size("ctx")
    operands, first_laid, plan, shapes, count, taken = [], {}, [], [], 0, 0
    for number, (operand, gradient) in enumerate(products):
        parts = gradient if isinstance(gradient, tuple) else (gradient,)
        columns = sum(part.shape[1] for part in parts)
        places_of = tuple(range(taken, taken + len(parts)))
        taken += len(parts)
        shard = operand.shape[1] // places
        pieces = -(-shard // unit)
        shapes.append((shard, columns))
        if id(operand) not in first_laid:
            first_laid[id(operand)] = count
            count += pieces
            if pieces > 1:
                operands.append((turned_pieces(operand, places, n_dp, unit), pieces))
            else:
                operands.append((operand, 0))
        for piece in range(pieces):
            first = piece * unit
            plan.append(
                (
                    first_laid[id(operand)] + piece,
                    places_of,
                    number,
                    first,
                    min(unit, shard - first),
                    columns // WIDE,
                )
            )
    return operands, plan, shapes


def as_product(small):
    rows, few = small.shape
    high = small.astype(jnp.bfloat16)
    rest = (small - high.astype(jnp.float32)).astype(jnp.bfloat16)

    def product(tokens):
        both = jnp.zeros((tokens, rows), jnp.bfloat16).at[:few].set(high.T).at[few : 2 * few].set(rest.T)
        pick = np.zeros((tokens, WIDE), np.float32)
        pick[:few, :few] = pick[few : 2 * few, :few] = np.eye(few)
        return both, jnp.asarray(pick, jnp.bfloat16)

    return product


def summed_to_owners(products, cid, unit, carry=0, state=()):
    n_dp, n_ctx = lax.axis_size("dp"), lax.axis_size("ctx")
    laid, plan, shapes = chunk_plan(products, unit)
    gradients = []
    for _, gradient in products:
        gradients += gradient if isinstance(gradient, tuple) else (gradient,)
    return scatter_sums(laid, gradients, shapes, plan, n_dp, n_ctx, cid, carry, state)


def chunks_of(shards):
    out = []
    for place, shard in enumerate(shards):
        rows, columns = shard.shape
        unit = max(128, 1408 * 32 // rows // 128 * 128)
        width = -(-(columns // 128) // -(-columns // unit)) * 128
        for first in range(0, columns, width):
            out.append((place, first, min(width, columns - first)))
    return out


def flat(value):
    return value.reshape(-1, value.shape[-1])


def normed(stream, scale_gain):
    return (
        stream * lax.rsqrt(jnp.mean(stream * stream, axis=-1, keepdims=True) + epsilon) * scale_gain
    )


def matmul(operand, weight):
    return jnp.einsum("mtd,de->mte", operand, weight, preferred_element_type=jnp.float32)


def matmul_back(operand, weight):
    return jnp.einsum("mte,de->mtd", operand, weight, preferred_element_type=jnp.float32)


def weight_grad(operand, gradient):
    return jnp.einsum("mtd,mte->de", operand, gradient, preferred_element_type=jnp.float32)


def layout(seq_lengths, tok_count):
    seq_ends = jnp.cumsum(seq_lengths[:, 0, :], axis=-1, dtype=jnp.int32)
    first_pos = lax.axis_index("ctx") * tok_count

    def segment_of(positions):
        return jnp.sum(
            (positions[None, :, None] >= seq_ends[:, None, :]).astype(jnp.int32),
            axis=-1,
            dtype=jnp.int32,
        )

    own_pos = first_pos + jnp.arange(tok_count, dtype=jnp.int32)
    own_seg = segment_of(own_pos)
    before_seg = segment_of(own_pos - 1)

    def in_lanes(flag):
        return jnp.broadcast_to(flag[:, :, None].astype(jnp.float32), flag.shape + (128,))

    starts = (own_seg != before_seg) | (own_pos == 0)[None, :]
    keep = 1.0 - jnp.max(starts.astype(jnp.float32), axis=1)
    tap_masks = []
    for offset in range(CONV):
        source = own_pos - offset
        tap_masks.append(
            ((segment_of(source) == own_seg) & (source >= 0)[None, :]).astype(jnp.float32)
        )
    key_pos = first_pos - BAND + jnp.arange(tok_count + BAND, dtype=jnp.int32)
    key_seg = jnp.where(key_pos >= 0, segment_of(key_pos), -1)
    window_mask = []
    for first in range(0, tok_count, BAND):
        queries, keys = slice(first, first + BAND), slice(first, first + 2 * BAND)
        ahead = own_pos[queries][:, None] - key_pos[keys][None, :]
        same = own_seg[:, queries][:, :, None] == key_seg[:, keys][:, None, :]
        window_mask.append(((ahead >= 0) & (ahead < WINDOW))[None] & same)
    window_mask = jnp.where(jnp.concatenate(window_mask, axis=1), 0.0, masked_fill)
    causal = (own_pos[:, None] >= own_pos[None, :])[None] & (
        own_seg[:, :, None] == own_seg[:, None, :]
    )
    return {
        "valid": (own_pos[None, :] < seq_ends[:, -1:]).astype(jnp.float32),
        "keep": jnp.broadcast_to(keep[:, None, None], keep.shape + (8, 128)),
        "carried": in_lanes((own_seg == before_seg[:, :1]) & (first_pos > 0)),
        "last": in_lanes(own_seg == own_seg[:, -1:]),
        "causal": causal.astype(jnp.float32),
        "taps": jnp.stack(tap_masks),
        "window": window_mask,
    }


def conv_gate(pre_values, rim_rows, tap_weights, tap_masks):
    tok_count = pre_values.shape[1]
    rim_width = rim_rows.shape[1]
    extended = jnp.concatenate([rim_rows, pre_values], axis=1)
    conv_sum = jnp.zeros_like(pre_values)
    for offset in range(rim_width + 1):
        shifted = extended[:, rim_width - offset : rim_width - offset + tok_count, :]
        conv_sum = conv_sum + tap_weights[:, offset] * shifted * tap_masks[offset][:, :, None]
    return conv_sum * jax.nn.silu(pre_values)


def linear_forward(stream, rim_stream, weights, layout_info, gather_more):
    norm_gain, qk_weight, value_weight, tap_weights = weights
    micro_count, tok_count, model_width = stream.shape
    normed_rows, norm_back = jax.vjp(normed, stream, norm_gain.astype(jnp.float32))
    normed_low = normed_rows.astype(jnp.bfloat16)
    qk_rows = matmul(normed_low, qk_weight).astype(jnp.bfloat16)
    pre_values = matmul(normed_low, value_weight)
    rim_normed = normed(rim_stream.astype(jnp.float32), norm_gain.astype(jnp.float32))
    rim_rows = matmul(rim_normed.astype(jnp.bfloat16), value_weight)
    value_rows, conv_back = jax.vjp(
        partial(conv_gate, tap_masks=layout_info["taps"]),
        pre_values,
        rim_rows,
        tap_weights.astype(jnp.float32),
    )
    values = value_rows.astype(jnp.bfloat16)
    tables, base = feature_tables()
    state_shape = (micro_count, HEADS // 2 + 1, SENT, 128)
    (state,) = by_pair(
        states_kernel,
        "states",
        [(qk_rows, "key"), (values, "pair"), (layout_info["last"], "micro"), (tables, "whole"), (base, "whole")],
        [(state_shape, jnp.bfloat16, "micro")],
    )
    *more, state_in = gather_more((state, layout_info["keep"]))
    out_weight = more[0]
    shared = [
        (qk_rows, "query"),
        (qk_rows, "key"),
        (values, "pair"),
        (state_in, "micro"),
        (layout_info["causal"], "micro"),
        (layout_info["carried"], "micro"),
        (tables, "whole"),
        (base, "whole"),
    ]
    attended_low, den = by_pair(
        attend_kernel,
        "linear_attend",
        shared,
        [(values.shape, jnp.bfloat16, "pair"), (values.shape, jnp.float32, "pair")],
    )
    branch = matmul(attended_low, out_weight)
    return (
        stream + branch,
        (norm_back, normed_low, conv_back, shared, attended_low, den),
        more,
    )


def linear_backward(grad_stream, residuals, weights, layout_info, other_gains, sum_others):
    norm_back, normed_low, conv_back, shared, attended_low, den = residuals
    qk_weight, value_weight, out_weight = (weights[1], weights[2], weights[4])
    micro_count, tok_count, model_width = grad_stream.shape
    grad_branch = grad_stream.astype(jnp.bfloat16)
    grad_out = (flat(attended_low), flat(grad_branch))
    grad_attended = matmul_back(grad_branch, out_weight)
    f32, low = jnp.float32, jnp.bfloat16
    feat_shape = (micro_count, tok_count, HEADS * FEAT)
    state_shape = (micro_count, HEADS // 2 + 1, SENT, 128)
    grad_query, grad_key, grad_value, grad_state = by_pair(
        attend_back_kernel,
        "linear_attend_back",
        shared + [(grad_attended, "pair"), (attended_low, "pair"), (den, "pair")],
        [
            (feat_shape, f32, "micro"),
            (feat_shape, f32, "micro"),
            (grad_stream.shape, f32, "pair"),
            (state_shape, low, "micro"),
        ],
    )
    *sums, later = sum_others(grad_out, (grad_state, layout_info["keep"]))
    grad_key, grad_value = by_pair(
        states_back_kernel,
        "states_back",
        [shared[1], shared[2], (layout_info["last"], "micro"), shared[6], shared[7], (later, "micro")]
        + [(grad_key, "micro"), (grad_value, "pair")],
        [(feat_shape, f32, "micro"), (grad_stream.shape, f32, "pair")],
    )
    grad_qk = jnp.concatenate([grad_query, grad_key], axis=-1).astype(low)
    grad_pre, grad_rim, grad_taps = conv_back(grad_value)
    returned = passed_along(grad_rim, "ctx", -1)
    grad_pre = grad_pre.at[:, tok_count - CONV + 1 :, :].add(returned)
    grad_pre_low = grad_pre.astype(jnp.bfloat16)
    grad_normed = matmul_back(grad_qk, qk_weight) + matmul_back(grad_pre_low, value_weight)
    grad_input, grad_gain = norm_back(grad_normed)
    small = jnp.concatenate([grad_gain[:, None], other_gains, grad_taps], axis=1)
    operand = flat(normed_low)
    own = summed_to_owners(
        [
            as_product(small)(operand.shape[0]),
            (operand, flat(grad_qk)),
            (operand, flat(grad_pre_low)),
        ],
        3,
        model_width // (lax.axis_size("dp") * lax.axis_size("ctx")),
    )
    return (grad_stream + grad_input, own, sums)


BAND = 128
RIM = 64
WIDE_PER = 4


def band_probabilities(queries, keys, bias):
    scores = [dot_nt(q, k) + bias for q, k in zip(queries, keys)]
    tops = [jnp.max(score, axis=1, keepdims=True) for score in scores]
    powers = [jnp.exp(score - top) for score, top in zip(scores, tops)]
    totals = [1.0 / jnp.sum(power, axis=1, keepdims=True) for power in powers]
    return [power * total for power, total in zip(powers, totals)]


def band_attend(queries, keys, values, bias):
    low = jnp.bfloat16
    chances = band_probabilities([heads_apart(q * 0.125) for q in queries], keys, twice(bias))
    outs = [dot_nn(chance.astype(low), v) for chance, v in zip(chances, values)]
    return [heads_joined(out).astype(low) for out in outs]


def band_back(queries, grads, keys, values, bias):
    low = jnp.bfloat16
    queries = [heads_apart(q * 0.125) for q in queries]
    grads = [heads_apart(g) for g in grads]
    dchances = [dot_nt(g, v) for g, v in zip(grads, values)]
    chances = band_probabilities(queries, keys, twice(bias))
    inners = [jnp.sum(d * c, axis=1, keepdims=True) for d, c in zip(dchances, chances)]
    dscores = [(c * (d - inner)).astype(low) for c, d, inner in zip(chances, dchances, inners)]
    dqueries = [dot_nn(d, k) for d, k in zip(dscores, keys)]
    dkeys = [dot_tn(d, q) for d, q in zip(dscores, queries)]
    dvalues = [dot_tn(c.astype(low), g) for c, g in zip(chances, grads)]
    return [(heads_joined(d) * 0.125).astype(low) for d in dqueries], dkeys, dvalues


LANES = [slice(128 * n, 128 * (n + 1)) for n in range(WIDE_PER)]


def by_pairs(ref, rows):
    return [ref[0, rows, here] for here in LANES]


def with_rim(own_ref, rim_ref):
    out = []
    for own, rim in zip(by_pairs(own_ref, slice(None)), by_pairs(rim_ref, slice(None))):
        out.append(jnp.concatenate([jnp.zeros((BAND - RIM, 128), own.dtype), rim, own], axis=0))
    return out


def first_band_kernel(query_ref, key_ref, value_ref, rim_key_ref, rim_value_ref, bias_ref, out_ref):
    keys, values = with_rim(key_ref, rim_key_ref), with_rim(value_ref, rim_value_ref)
    outs = band_attend(by_pairs(query_ref, slice(None)), keys, values, bias_ref[0])
    for here, out in zip(LANES, outs):
        out_ref[0, :, here] = out


def later_bands_kernel(query_ref, key_ref, value_ref, bias_ref, out_ref):
    for first in range(BAND, query_ref.shape[1], BAND):
        rows, near = slice(first, first + BAND), slice(first - BAND, first + BAND)
        outs = band_attend(
            by_pairs(query_ref, rows), by_pairs(key_ref, near), by_pairs(value_ref, near), bias_ref[0, rows]
        )
        for here, out in zip(LANES, outs):
            out_ref[0, first - BAND : first, here] = out


def first_band_back_kernel(
    query_ref, key_ref, value_ref, rim_key_ref, rim_value_ref, bias_ref, grad_ref, dquery_ref, dkey_ref,
    dvalue_ref, drim_key_ref, drim_value_ref,
):
    keys, values = with_rim(key_ref, rim_key_ref), with_rim(value_ref, rim_value_ref)
    whole = slice(None)
    all_back = band_back(by_pairs(query_ref, whole), by_pairs(grad_ref, whole), keys, values, bias_ref[0])
    for here, dquery, dkey, dvalue in zip(LANES, *all_back):
        dquery_ref[0, :, here] = dquery
        dkey_ref[0, :, here] = dkey[BAND:]
        dvalue_ref[0, :, here] = dvalue[BAND:]
        drim_key_ref[0, :, here] = dkey[BAND - RIM : BAND].astype(jnp.bfloat16)
        drim_value_ref[0, :, here] = dvalue[BAND - RIM : BAND].astype(jnp.bfloat16)


def later_bands_back_kernel(
    query_ref, key_ref, value_ref, bias_ref, grad_ref, first_dkey_ref, first_dvalue_ref, dquery_ref, dkey_ref,
    dvalue_ref,
):
    dkey_ref[0, :BAND] = first_dkey_ref[0]
    dvalue_ref[0, :BAND] = first_dvalue_ref[0]
    for first in range(BAND, query_ref.shape[1], BAND):
        rows, before, near = (
            slice(first, first + BAND),
            slice(first - BAND, first),
            slice(first - BAND, first + BAND),
        )
        all_back = band_back(
            by_pairs(query_ref, rows),
            by_pairs(grad_ref, rows),
            by_pairs(key_ref, near),
            by_pairs(value_ref, near),
            bias_ref[0, rows],
        )
        for here, dquery, dkey, dvalue in zip(LANES, *all_back):
            dquery_ref[0, before, here] = dquery
            dkey_ref[0, before, here] += dkey[:BAND]
            dvalue_ref[0, before, here] += dvalue[:BAND]
            dkey_ref[0, rows, here] = dkey[BAND:]
            dvalue_ref[0, rows, here] = dvalue[BAND:]


def by_window(kernel, name, ins, outs):
    micro, steps = ins[0][0].shape[0], HEADS // 2 // WIDE_PER

    def spec(rows, place, width):
        if place is None:
            return pl.BlockSpec((1, rows, width), lambda m, p: (m, 0, 0))
        return pl.BlockSpec((1, rows, WIDE_PER * 128), lambda m, p: (m, 0, p + place * steps))

    return pl.pallas_call(
        kernel,
        grid=(micro, steps),
        in_specs=[spec(rows, place, array.shape[2]) for array, rows, place in ins],
        out_specs=[spec(rows, 0, 0) for rows, _ in outs],
        out_shape=[jax.ShapeDtypeStruct((micro, rows, HEADS * 64), dtype) for rows, dtype in outs],
        compiler_params=pltpu.CompilerParams(vmem_limit_bytes=48 * 2**20),
        name=name,
    )(*[array for array, _, _ in ins])


def window_forward(stream, weights, layout_info):
    norm_gain, qkv_weight, out_weight = weights
    micro_count, tok_count, model_width = stream.shape
    normed_rows, norm_back = jax.vjp(normed, stream, norm_gain.astype(jnp.float32))
    normed_low = normed_rows.astype(jnp.bfloat16)
    qkv_rows = matmul(normed_low, qkv_weight).astype(jnp.bfloat16)
    rim_rows = passed_along(qkv_rows[:, tok_count - RIM :, model_width:], "ctx", 1)
    mask = layout_info["window"]
    parts = []
    if tok_count > BAND:
        parts = by_window(
            later_bands_kernel,
            "window_later",
            [(qkv_rows, tok_count, 0), (qkv_rows, tok_count, 1), (qkv_rows, tok_count, 2), (mask, tok_count, None)],
            [(tok_count - BAND, jnp.bfloat16)],
        )
        rim_rows, parts = lax.optimization_barrier((rim_rows, parts))
    (start,) = by_window(
        first_band_kernel,
        "window_first",
        [(qkv_rows, BAND, 0), (qkv_rows, BAND, 1), (qkv_rows, BAND, 2), (rim_rows, RIM, 0), (rim_rows, RIM, 1)]
        + [(mask, BAND, None)],
        [(BAND, jnp.bfloat16)],
    )
    attended = jnp.concatenate([start] + list(parts), axis=1)
    branch = matmul(attended, out_weight)
    return (stream + branch, (norm_back, normed_low, qkv_rows, rim_rows, attended))


def window_backward(grad_stream, residuals, weights, layout_info):
    norm_back, normed_low, qkv_rows, rim_rows, attended = residuals
    qkv_weight, out_weight = (weights[1], weights[2])
    micro_count, tok_count, model_width = grad_stream.shape
    f32, low = jnp.float32, jnp.bfloat16
    grad_branch = grad_stream.astype(low)
    grad_out = (flat(attended), flat(grad_branch))
    grad_attended = matmul_back(grad_branch, out_weight).astype(low)
    mask = layout_info["window"]
    grad_query, grad_key, grad_value, rim_key, rim_value = by_window(
        first_band_back_kernel,
        "window_first_back",
        [(qkv_rows, BAND, 0), (qkv_rows, BAND, 1), (qkv_rows, BAND, 2), (rim_rows, RIM, 0), (rim_rows, RIM, 1)]
        + [(mask, BAND, None), (grad_attended, BAND, 0)],
        [(BAND, low), (BAND, f32), (BAND, f32), (RIM, low), (RIM, low)],
    )
    returned = passed_along(jnp.concatenate([rim_key, rim_value], axis=-1), "ctx", -1)
    if tok_count > BAND:
        more_query, grad_key, grad_value = by_window(
            later_bands_back_kernel,
            "window_later_back",
            [(qkv_rows, tok_count, 0), (qkv_rows, tok_count, 1), (qkv_rows, tok_count, 2), (mask, tok_count, None)]
            + [(grad_attended, tok_count, 0), (grad_key, BAND, 0), (grad_value, BAND, 0)],
            [(tok_count - BAND, low), (tok_count, f32), (tok_count, f32)],
        )
        grad_query = jnp.concatenate([grad_query, more_query], axis=1)
        returned, grad_key = lax.optimization_barrier((returned, grad_key))
    returned = returned.astype(f32)
    returned = jnp.pad(returned, ((0, 0), (tok_count - RIM, 0), (0, 0)))
    grad_qkv = jnp.concatenate(
        [
            grad_query,
            (grad_key + returned[..., :model_width]).astype(low),
            (grad_value + returned[..., model_width:]).astype(low),
        ],
        axis=-1,
    )
    grad_qkv_weight = (flat(normed_low), flat(grad_qkv))
    grad_input, grad_gain = norm_back(lax.optimization_barrier(matmul_back(grad_qkv, qkv_weight)))
    return (grad_stream + grad_input, (grad_gain, grad_qkv_weight, grad_out))


def ffn_forward(stream, weights):
    norm_gain, gate_up, down_weight = weights
    hidden_width = down_weight.shape[0]
    normed_rows, norm_back = jax.vjp(normed, stream, norm_gain.astype(jnp.float32))
    normed_low = normed_rows.astype(jnp.bfloat16)
    projected = matmul(normed_low, gate_up)
    hidden = (jax.nn.silu(projected[..., :hidden_width]) * projected[..., hidden_width:]).astype(
        jnp.bfloat16
    )
    hidden, projected = lax.optimization_barrier((hidden, projected.astype(jnp.bfloat16)))
    branch = matmul(hidden, down_weight)
    return (stream + branch, (norm_back, normed_low, projected, hidden))


def ffn_backward(grad_stream, residuals, weights):
    norm_back, normed_low, projected, hidden = residuals
    gate_up, down_weight = (weights[1], weights[2])
    hidden_width = down_weight.shape[0]
    grad_branch = grad_stream.astype(jnp.bfloat16)
    grad_down = (flat(hidden), flat(grad_branch))
    grad_hidden = matmul_back(grad_branch, down_weight)
    gate_part = projected[..., :hidden_width].astype(jnp.float32)
    up_part = projected[..., hidden_width:].astype(jnp.float32)
    sigmoid_gate = jax.nn.sigmoid(gate_part)
    grad_gate = grad_hidden * up_part * sigmoid_gate * (1.0 + gate_part * (1.0 - sigmoid_gate))
    grad_up = grad_hidden * gate_part * sigmoid_gate
    grad_projected = jnp.concatenate([grad_gate, grad_up], axis=-1).astype(jnp.bfloat16)
    low = jnp.bfloat16
    grad_gate_up = (flat(normed_low), (flat(grad_gate.astype(low)), flat(grad_up.astype(low))))
    grad_input, grad_gain = norm_back(lax.optimization_barrier(matmul_back(grad_projected, gate_up)))
    return (grad_stream + grad_input, (grad_gain, grad_gate_up, grad_down))


def body(
    tokens_in,
    seq_lengths,
    norm_linear,
    proj_qk,
    proj_values,
    conv_taps,
    out_linear,
    norm_ffn_one,
    gate_up_one,
    down_one,
    norm_window,
    proj_qkv,
    out_window,
    norm_ffn_two,
    gate_up_two,
    down_two,
    cotangent,
):
    tok_count = tokens_in.shape[2]
    layout_info = layout(seq_lengths, tok_count)
    stream = tokens_in[:, 0].astype(jnp.float32)
    small = jnp.concatenate(
        [
            norm_linear[:, None],
            norm_ffn_one[:, None],
            norm_window[:, None],
            norm_ffn_two[:, None],
            conv_taps,
            jnp.zeros((conv_taps.shape[0], 121), jnp.bfloat16),
        ],
        axis=1,
    )
    n_dp, n_ctx = lax.axis_size("dp"), lax.axis_size("ctx")
    first_shards = [small, proj_qk, proj_values]
    rim_stream = passed_along(tokens_in[:, 0, tok_count - CONV + 1 :], "ctx", 1)
    small, w_qk, w_values = gather_all(first_shards, n_dp, n_ctx, chunks_of(first_shards), cid=0)
    small, rim_stream = lax.optimization_barrier((small, rim_stream))

    def gather_more(state):
        shards = [out_linear, gate_up_one, down_one, proj_qkv, out_window, down_two]
        return gather_all(shards, n_dp, n_ctx, chunks_of(shards), cid=2, carry=1, state=state)

    middle, saved_linear, more = linear_forward(
        stream, rim_stream, (small[:, 0], w_qk, w_values, small[:, 4:7]), layout_info, gather_more
    )
    w_out_linear, w_gu_one, w_dn_one, w_qkv, w_out_window, w_dn_two = more
    w_gu_two = lax.all_gather(gate_up_two, ("dp", "ctx"), axis=0, tiled=True)
    layer_one = (small[:, 0], w_qk, w_values, small[:, 4:7], w_out_linear, small[:, 1], w_gu_one, w_dn_one)
    layer_two = (small[:, 2], w_qkv, w_out_window, small[:, 3], w_gu_two, w_dn_two)
    first_out, saved_ffn_one = ffn_forward(middle, layer_one[5:])
    second_mid, saved_window = window_forward(first_out, layer_two[:3], layout_info)
    closing, saved_ffn_two = ffn_forward(second_mid, layer_two[3:])
    valid_rows = layout_info["valid"][:, :, None]
    output = (closing * valid_rows).astype(jnp.bfloat16)[:, None]
    grad_stream = cotangent[:, 0].astype(jnp.float32) * valid_rows
    grad_stream, grads_ffn_two = ffn_backward(grad_stream, saved_ffn_two, layer_two[3:])
    operand, gradient = grads_ffn_two[1]
    gradient = jnp.concatenate(gradient, axis=-1)
    partial_sums = jnp.einsum("tr,te->re", operand, gradient, preferred_element_type=jnp.float32)
    partial_sums = partial_sums.astype(jnp.bfloat16)
    for axis in ("dp", "ctx"):
        partial_sums = lax.psum_scatter(partial_sums, axis, scatter_dimension=0, tiled=True)
    sum_gate_up_two = partial_sums.astype(jnp.float32)
    grad_stream, grads_window = window_backward(
        grad_stream, saved_window, layer_two[:3], layout_info
    )
    grad_stream, grads_ffn_one = ffn_backward(grad_stream, saved_ffn_one, layer_one[5:])
    other_gains = jnp.stack([grads_ffn_one[0], grads_window[0], grads_ffn_two[0]], axis=1)

    def sum_others(of_out, state):
        products = [
            of_out,
            grads_ffn_one[1],
            grads_ffn_one[2],
            grads_window[1],
            grads_window[2],
            grads_ffn_two[2],
        ]
        return summed_to_owners(products, 1, out_linear.shape[0], -1, state)

    grad_stream, own_sums, sums = linear_backward(
        grad_stream, saved_linear, layer_one[:5], layout_info, other_gains, sum_others
    )
    small, grad_qk, grad_values = own_sums
    tokens_grad = grad_stream.astype(jnp.bfloat16)[:, None]
    return (
        output,
        tokens_grad,
        small[:, 0],
        grad_qk,
        grad_values,
        small[:, 4:7],
        sums[0],
        small[:, 1],
        sums[1],
        sums[2],
        small[:, 2],
        sums[3],
        sums[4],
        small[:, 3],
        sum_gate_up_two,
        sums[5],
    )


def solution(mesh):
    placed = (
        P(None, "dp", "ctx", None),
        P(None, "dp", None),
        P(("dp", "ctx")),
        P(("dp", "ctx"), None),
        P(("dp", "ctx"), None),
        P(("dp", "ctx"), None),
        P(("dp", "ctx"), None),
        P(("dp", "ctx")),
        P(("dp", "ctx"), None),
        P(("dp", "ctx"), None),
        P(("dp", "ctx")),
        P(("dp", "ctx"), None),
        P(("dp", "ctx"), None),
        P(("dp", "ctx")),
        P(("dp", "ctx"), None),
        P(("dp", "ctx"), None),
        P(None, "dp", "ctx", None),
    )
    return jax.shard_map(
        body,
        mesh=mesh,
        in_specs=placed,
        out_specs=(
            P(None, "dp", "ctx", None),
            P(None, "dp", "ctx", None),
            P(("dp", "ctx")),
            P(("dp", "ctx"), None),
            P(("dp", "ctx"), None),
            P(("dp", "ctx"), None),
            P(("dp", "ctx"), None),
            P(("dp", "ctx")),
            P(("dp", "ctx"), None),
            P(("dp", "ctx"), None),
            P(("dp", "ctx")),
            P(("dp", "ctx"), None),
            P(("dp", "ctx"), None),
            P(("dp", "ctx")),
            P(("dp", "ctx"), None),
            P(("dp", "ctx"), None),
        ),
        check_vma=False,
    )
```

```python
from functools import partial
import math

import jax
import jax.numpy as jnp
import numpy as np
from jax import lax
from jax.experimental import pallas as pl
from jax.experimental.pallas import tpu as pltpu
from jax.sharding import PartitionSpec as P

HEADS = 16
FEAT = 16
WINDOW = 64
CONV = 3


epsilon = 1e-05
masked_fill = -1e30
highest = lax.Precision.HIGHEST


MESH = pl.DeviceIdType.MESH

def carried(sign, n_ctx, dp, ctx, own, keep, out, came, total, sent, arrived):
    first, last = (0, n_ctx - 1) if sign > 0 else (n_ctx - 1, 0)
    low, f32 = jnp.bfloat16, jnp.float32
    micro, planes, rows = own.shape[:3]

    def copy(m, p):
        return pltpu.make_async_remote_copy(
            src_ref=total.at[m, p],
            dst_ref=came.at[m, p],
            send_sem=sent.at[m, p],
            recv_sem=arrived.at[m, p],
            device_id=(dp, lax.rem(ctx + sign + n_ctx, n_ctx)),
            device_id_type=MESH,
        )

    def act(i):
        m, p = i // planes, i % planes

        @pl.when(ctx != first)
        def _():
            copy(m, p).wait_recv()
            value = came[m, p]
            out[m, p, :rows] = value
            total[m, p] = (own[m, p].astype(f32) + keep[m, 0:1] * value.astype(f32)).astype(low)

        @pl.when(ctx == first)
        def _():
            out[m, p, :rows] = jnp.zeros((rows, 128), low)
            total[m, p] = own[m, p]

        @pl.when(ctx != last)
        def _():
            copy(m, p).start()

    def finish():
        for m in range(micro):
            for p in range(planes):
                out[m, p, rows:] = jnp.zeros((out.shape[2] - rows, 128), low)

        @pl.when(ctx != last)
        def _():
            for m in range(micro):
                for p in range(planes):
                    copy(m, p).wait_send()

    return micro * planes, act, finish


def carry_specs(state):
    whole = pl.BlockSpec(memory_space=pltpu.VMEM)
    shape = state.shape[:2] + (TERMS,) + state.shape[3:]
    held = pltpu.VMEM(state.shape, jnp.bfloat16)
    sems = pltpu.SemaphoreType.DMA(state.shape[:2])
    return [whole, whole], [whole], [jax.ShapeDtypeStruct(shape, jnp.bfloat16)], [held, held, sems, sems]


def gather_kernel(n_dp, n_ctx, chunks, lag, n_w, carry, *refs):
    n_c = 2 if carry else 0
    ins, outs = refs[:n_w], refs[n_w + n_c:2 * n_w + n_c]
    local_sem, send_sem, recv_sem = refs[2 * n_w + 3 * n_c // 2:][:3]
    dp, ctx = lax.axis_index("dp"), lax.axis_index("ctx")
    bits = [1 << i for i in range(n_dp.bit_length() - 1)]
    low_bits, (bit_x, bit_y) = bits[:-2], bits[-2:]
    barrier = pltpu.get_barrier_semaphore()
    greeted = 0
    for bit in bits:
        pl.semaphore_signal(barrier, inc=1, device_id=(dp ^ bit, ctx), device_id_type=MESH)
        greeted += 1
    for hop in range(1, n_ctx):
        pl.semaphore_signal(barrier, inc=1, device_id=(dp, lax.rem(ctx + hop, n_ctx)), device_id_type=MESH)
        greeted += 1
    pl.semaphore_wait(barrier, greeted)
    sends = []

    def piece(c, start, shards):
        w, col, width = chunks[c]
        return outs[w].at[pl.ds(start, shards), :, pl.ds(col, width)]

    def send(c, slot, start, rows, target, src=None):
        where = piece(c, start, rows)
        copy = pltpu.make_async_remote_copy(
            src_ref=where if src is None else src, dst_ref=where,
            send_sem=send_sem.at[c, slot], recv_sem=recv_sem.at[c, slot],
            device_id=target, device_id_type=MESH)
        copy.start()
        sends.append(copy)

    def arrive(c, slot, start, rows):
        where = piece(c, start, rows)
        pltpu.make_async_remote_copy(
            src_ref=where, dst_ref=where, send_sem=send_sem.at[c, slot], recv_sem=recv_sem.at[c, slot],
            device_id=(dp ^ 1, ctx), device_id_type=MESH).wait_recv()

    def stage_ctx(c):
        w, col, width = chunks[c]
        own = ins[w].at[:, :, pl.ds(col, width)]
        start = dp * n_ctx + ctx
        for hop in range(1, n_ctx):
            send(c, hop - 1, start, 1, (dp, lax.rem(ctx + hop, n_ctx)), src=own)
        pltpu.make_async_copy(own, piece(c, start, 1), local_sem.at[c]).start()

    base = n_ctx - 1
    SX, SY, SDX, SDY, SC = base, base + 1, base + 2, base + 3, base + 4

    def stage_sides(c):
        w, col, width = chunks[c]
        for hop in range(1, n_ctx):
            arrive(c, hop - 1, dp * n_ctx + lax.rem(ctx - hop + n_ctx, n_ctx), 1)
        own = ins[w].at[:, :, pl.ds(col, width)]
        pltpu.make_async_copy(own, piece(c, dp * n_ctx + ctx, 1), local_sem.at[c]).wait()
        group = n_ctx
        send(c, SX, dp * group, group, (dp ^ bit_x, ctx))
        send(c, SY, dp * group, group, (dp ^ bit_y, ctx))

    def stage_diag(c):
        group = n_ctx
        a0, an, b0, bn = 0, n_ctx // 2, n_ctx // 2, n_ctx - n_ctx // 2
        arrive(c, SX, (dp ^ bit_x) * group, group)
        send(c, SDY, (dp ^ bit_x) * group + a0, an, (dp ^ bit_y, ctx))
        arrive(c, SY, (dp ^ bit_y) * group, group)
        send(c, SDX, (dp ^ bit_y) * group + b0, bn, (dp ^ bit_x, ctx))

    def low_slot(level, j):
        return SC + 4 * ((1 << level) - 1) + j

    def quads(base_dp, level):
        out = []
        for top in range(4):
            for low in range(1 << level):
                flip = (bit_x if top & 1 else 0) | (bit_y if top & 2 else 0)
                for i in range(level):
                    if low >> i & 1:
                        flip |= low_bits[len(low_bits) - 1 - i]
                out.append(base_dp ^ flip)
        return out

    def stage_low(c, level):
        group = n_ctx
        if level == 0:
            a0, an, b0, bn = 0, n_ctx // 2, n_ctx // 2, n_ctx - n_ctx // 2
            arrive(c, SDY, (dp ^ bit_x ^ bit_y) * group + a0, an)
            arrive(c, SDX, (dp ^ bit_x ^ bit_y) * group + b0, bn)
        else:
            bit = low_bits[len(low_bits) - level]
            for j, block in enumerate(quads(dp ^ bit, level - 1)):
                arrive(c, low_slot(level - 1, j), block * group, group)
        if level < len(low_bits):
            bit = low_bits[len(low_bits) - 1 - level]
            for j, block in enumerate(quads(dp, level)):
                send(c, low_slot(level, j), block * group, group, (dp ^ bit, ctx))

    stages = [stage_ctx, stage_sides, stage_diag] + [partial(stage_low, level=l) for l in range(len(low_bits) + 1)]
    depth = len(stages)
    turns = len(chunks) + (depth - 1) * lag
    due = {}
    if carry:
        own, keep = refs[n_w:n_w + 2]
        n_pieces, act, finish = carried(carry, n_ctx, dp, ctx, own, keep, refs[2 * n_w + 2], *refs[2 * n_w + 6:])
        for place in range(n_ctx):
            for i in range(n_pieces):
                due.setdefault(place + i // 2, []).append((place, i))
        turns = max(turns, max(due) + 1)
    for t in range(turns):
        for place, i in due.get(t, []):
            @pl.when(ctx == (place if carry > 0 else n_ctx - 1 - place))
            def _():
                act(i)
        for s in range(depth):
            c = t - s * lag
            if 0 <= c < len(chunks):
                stages[s](c)
    if carry:
        finish()
    for copy in sends:
        copy.wait_send()

def gather_all(weights, n_dp, n_ctx, chunks, lag=1, cid=0, carry=0, state=()):
    n = len(weights)
    places = n_dp * n_ctx
    slots = n_ctx - 1 + 4 + 4 * (n_dp // 4 - 1)
    more_in, more_out, more_shape, more_scratch = carry_specs(state[0]) if carry else ([], [], [], [])
    full = pl.pallas_call(
        partial(gather_kernel, n_dp, n_ctx, chunks, lag, n, carry),
        out_shape=[jax.ShapeDtypeStruct((places,) + w.shape, w.dtype) for w in weights] + more_shape,
        in_specs=[pl.BlockSpec(memory_space=pltpu.HBM)] * n + more_in,
        out_specs=[pl.BlockSpec(memory_space=pltpu.HBM)] * n + more_out,
        scratch_shapes=[pltpu.SemaphoreType.DMA((len(chunks),)), pltpu.SemaphoreType.DMA((len(chunks), slots)), pltpu.SemaphoreType.DMA((len(chunks), slots))]
        + more_scratch,
        compiler_params=pltpu.CompilerParams(collective_id=cid, has_side_effects=True),
        name="gather_weights")(*[w[None] for w in weights], *state)
    return [f.reshape(places * f.shape[1], f.shape[2]) for f in full[:n]] + list(full[n:])


WIDE = 512
SLOTS_HELD = 8
APART = 4


def scatter_kernel(n_dp, n_ctx, plan, lags, pieces, n_y, n_o, carry, *refs):
    n_x = len(pieces)
    xs, ys, refs = refs[:n_x], refs[n_x : n_x + n_y], refs[n_x + n_y :]
    state, refs = (refs[:2], refs[2:]) if carry else ((), refs)
    outs, refs = refs[:n_o], refs[n_o:]
    state_out, refs = (refs[:1], refs[1:]) if carry else ((), refs)
    bits = [1 << i for i in range(n_dp.bit_length() - 1)]
    low_bits, (bit_x, bit_y) = bits[:-2], bits[-2:]
    n_low = len(low_bits)
    x_all, y_all, natural = refs[0], refs[1], refs[-1]
    low_out, low_in = refs[2 : 2 + n_low], refs[2 + n_low : 2 + 2 * n_low]
    refs = refs[2 + 2 * n_low :]
    cross, cross_y, cross_x, side_x, side_y, came_x, came_y, shards, came_ctx, result = refs[:10]
    x_sem, y_sem, out_sem, sent, arrived, credit = refs[10:16]
    held = y_all.shape[0]
    dp, ctx = lax.axis_index("dp"), lax.axis_index("ctx")
    group = cross.shape[1]
    half = group // 2
    rows = group // n_ctx
    f32, low = jnp.float32, jnp.bfloat16
    A_CY, A_CX, A_X, A_Y, A_Z = n_low, n_low + 1, n_low + 2, n_low + 3, n_low + 4
    C_X, C_Y, C_Z = n_low, n_low + 1, n_low + 2

    def at_ctx(hop):
        return (dp, lax.rem(ctx + hop, n_ctx))

    barrier = pltpu.get_barrier_semaphore()
    for bit in bits:
        pl.semaphore_signal(barrier, inc=1, device_id=(dp ^ bit, ctx), device_id_type=MESH)
    for hop in range(1, n_ctx):
        pl.semaphore_signal(barrier, inc=1, device_id=at_ctx(hop), device_id_type=MESH)
    pl.semaphore_wait(barrier, len(bits) + n_ctx - 1)

    bounds, count = [], 0
    for segment in plan:
        bounds.append((count, count + segment[5]))
        count += segment[5]
    laid_at = [sum(max(1, n) for n in pieces[:i]) for i in range(n_x)]
    x_first = {}
    for segment, (first, _) in zip(plan, bounds):
        x_first.setdefault(segment[0], first)

    def x_copy(i):
        if pieces[i]:
            return pltpu.make_async_copy(xs[i], x_all.at[pl.ds(laid_at[i], pieces[i])], x_sem.at[i])
        return pltpu.make_async_copy(xs[i], natural.at[pieces[:i].count(0)], x_sem.at[i])

    def x_ready(i):
        x_copy(i).wait()
        if not pieces[i]:
            for place in range(n_dp):
                value = natural[pieces[:i].count(0), :, place * group : (place + 1) * group]
                x_all[laid_at[i], place] = value.T

    for i in range(n_x):
        x_copy(i).start()

    def y_part(slot, number, where, to, width):
        pltpu.make_async_copy(
            ys[number].at[:, pl.ds(where, width)], y_all.at[slot, :, pl.ds(to, width)], y_sem.at[slot]
        ).start()

    def y_fetch(k, slot, numbers):
        if len(numbers) == 1:
            y_part(slot, numbers[0], pl.multiple_of(k * WIDE, WIDE), 0, WIDE)
            return
        width = ys[numbers[0]].shape[1]
        whole, left = width // WIDE, width % WIDE

        @pl.when(k < whole)
        def _():
            y_part(slot, numbers[0], pl.multiple_of(k * WIDE, WIDE), 0, WIDE)

        if left:

            @pl.when(k == whole)
            def _():
                y_part(slot, numbers[0], whole * WIDE, 0, left)
                y_part(slot, numbers[1], 0, left, WIDE - left)

        @pl.when(k >= whole + (1 if left else 0))
        def _():
            y_part(slot, numbers[1], pl.multiple_of(k * WIDE - width, 128), 0, WIDE)

    def y_start(c):
        slot = lax.rem(c, held)
        for segment, (first, last) in zip(plan, bounds):

            @pl.when((c >= first) & (c < last))
            def _():
                y_fetch(c - first, slot, segment[1])

    def x_place(c):
        return sum((c >= first).astype(jnp.int32) for first in sorted(x_first.values())[1:])

    def partial_sum(c, flip):
        return jnp.dot(
            x_all[x_place(c), dp ^ flip], y_all[lax.rem(c, held)], preferred_element_type=f32
        )

    def rest(level):
        free = low_bits[level + 1 :] + [bit_x, bit_y]
        return [sum(b for i, b in enumerate(free) if n >> i & 1) for n in range(1 << len(free))]

    def summed(c, flip, levels):
        total = partial_sum(c, flip)
        for level in range(levels):
            total = total + low_in[level][lax.rem(c, held), rest(level).index(flip)].astype(f32)
        return total

    def remote(src, dst, slot, kind, target):
        return pltpu.make_async_remote_copy(
            src_ref=src,
            dst_ref=dst,
            send_sem=sent.at[slot, kind],
            recv_sem=arrived.at[slot, kind],
            device_id=target,
            device_id_type=MESH,
        )

    def copy_of(slot, kind):
        over_x, over_y = (dp ^ bit_x, ctx), (dp ^ bit_y, ctx)
        if kind < n_low:
            return remote(
                low_out[kind].at[slot], low_in[kind].at[slot], slot, kind, (dp ^ low_bits[kind], ctx)
            )
        if kind == A_CY:
            return remote(cross.at[slot, pl.ds(0, half)], cross_y.at[slot], slot, kind, over_y)
        if kind == A_CX:
            return remote(cross.at[slot, pl.ds(half, half)], cross_x.at[slot], slot, kind, over_x)
        if kind == A_X:
            return remote(side_x.at[slot], came_x.at[slot], slot, kind, over_x)
        if kind == A_Y:
            return remote(side_y.at[slot], came_y.at[slot], slot, kind, over_y)
        hop = kind - A_Z + 1
        there = lax.rem(ctx + hop, n_ctx)
        return remote(shards.at[slot, there], came_ctx.at[slot, hop - 1], slot, kind, (dp, there))

    def need_credit(c, kind):
        @pl.when(c >= held)
        def _():
            pl.semaphore_wait(credit.at[kind], 1)

    def step_low(level, c):
        slot = lax.rem(c, held)
        if level == 0:
            for i in range(n_x):

                @pl.when(c == x_first[laid_at[i]])
                def _():
                    x_ready(i)

            pltpu.make_async_copy(y_all.at[slot], y_all.at[slot], y_sem.at[slot]).wait()
        else:
            copy_of(slot, level - 1).wait_recv()
        need_credit(c, level)
        for j, flip in enumerate(rest(level)):
            low_out[level][slot, j] = summed(c, flip | low_bits[level], level).astype(low)
        copy_of(slot, level).start()

    def step_cross(c):
        slot = lax.rem(c, held)
        if n_low:
            copy_of(slot, n_low - 1).wait_recv()
        need_credit(c, C_X)
        need_credit(c, C_Y)
        cross[slot] = summed(c, bit_x | bit_y, n_low).astype(low)
        copy_of(slot, A_CY).start()
        copy_of(slot, A_CX).start()

    def step_sides(c):
        slot = lax.rem(c, held)
        over_x = summed(c, bit_x, n_low)
        over_y = summed(c, bit_y, n_low)
        copy_of(slot, A_CY).wait_recv()
        side_x[slot, :half] = (over_x[:half] + cross_y[slot].astype(f32)).astype(low)
        side_x[slot, half:] = over_x[half:].astype(low)
        copy_of(slot, A_X).start()
        copy_of(slot, A_CX).wait_recv()
        side_y[slot, :half] = over_y[:half].astype(low)
        side_y[slot, half:] = (over_y[half:] + cross_x[slot].astype(f32)).astype(low)
        copy_of(slot, A_Y).start()

    def step_own(c):
        slot = lax.rem(c, held)
        total = summed(c, 0, n_low)
        copy_of(slot, A_X).wait_recv()
        copy_of(slot, A_Y).wait_recv()
        total = total + came_x[slot].astype(f32) + came_y[slot].astype(f32)
        for j in range(n_ctx):
            shards[slot, j] = total[j * rows : (j + 1) * rows].astype(low)
        for hop in range(1, n_ctx):
            need_credit(c, C_Z + hop - 1)
            copy_of(slot, A_Z + hop - 1).start()

    def out_copy(c, slot, segment, first):
        where = pl.multiple_of((c - first) * WIDE, WIDE)
        _, _, o, row, n_rows, _ = segment
        return pltpu.make_async_copy(
            result.at[slot, pl.ds(0, n_rows)],
            outs[o].at[pl.ds(row, n_rows), pl.ds(where, WIDE)],
            out_sem.at[slot],
        )

    def each_segment(c, act):
        for segment, (first, last) in zip(plan, bounds):

            @pl.when((c >= first) & (c < last))
            def _():
                act(segment, first)

    def out_wait(c):
        slot = lax.rem(c, held)
        each_segment(c, lambda segment, first: out_copy(c, slot, segment, first).wait())

    def step_end(c):
        slot = lax.rem(c, held)

        @pl.when(c >= held)
        def _():
            out_wait(c - held)

        total = shards[slot, ctx].astype(f32)
        for hop in range(1, n_ctx):
            copy_of(slot, A_Z + hop - 1).wait_recv()
            total = total + came_ctx[slot, hop - 1].astype(f32)
        result[slot] = total
        each_segment(c, lambda segment, first: out_copy(c, slot, segment, first).start())
        for kind in range(A_Z + n_ctx - 1):
            copy_of(slot, kind).wait_send()

        @pl.when(c + held < count)
        def _():
            for level, bit in enumerate(low_bits):
                pl.semaphore_signal(credit.at[level], inc=1, device_id=(dp ^ bit, ctx), device_id_type=MESH)
            pl.semaphore_signal(credit.at[C_X], inc=1, device_id=(dp ^ bit_x, ctx), device_id_type=MESH)
            pl.semaphore_signal(credit.at[C_Y], inc=1, device_id=(dp ^ bit_y, ctx), device_id_type=MESH)
            for hop in range(1, n_ctx):
                pl.semaphore_signal(
                    credit.at[C_Z + hop - 1], inc=1, device_id=at_ctx(n_ctx - hop), device_id_type=MESH
                )

    steps = [partial(step_low, level) for level in range(n_low)] + [step_cross, step_sides, step_own, step_end]
    ahead = 2
    for c in range(ahead):
        y_start(jnp.int32(c))

    turns = count + lags[-1]
    if carry:
        n_pieces, act, finish = carried(carry, n_ctx, dp, ctx, *state, *state_out, *refs[16:-1])
        place = ctx if carry > 0 else n_ctx - 1 - ctx
        turns = max(turns, n_pieces + APART * (n_ctx - 1))

    def turn(t, none):
        if carry:
            i = t - APART * place

            @pl.when((i >= 0) & (i < n_pieces))
            def _():
                act(i)

        @pl.when(t + ahead < count)
        def _():
            y_start(t + ahead)

        for step, lag in zip(steps, lags):
            c = t - lag

            @pl.when((c >= 0) & (c < count))
            def _():
                step(c)

        return none

    lax.fori_loop(0, turns, turn, 0)
    if carry:
        finish()
    for c in range(max(0, count - held), count):
        out_wait(jnp.int32(c))


def scatter_sums(xs, ys, out_shapes, plan, n_dp, n_ctx, cid=1, carry=0, state=(), lags=None, held=SLOTS_HELD):
    pieces = [n for _, n in xs]
    tokens = ys[0].shape[0]
    group = [x.shape[1] // n_dp for x, n in xs if not n][0]
    n_low = n_dp.bit_length() - 3
    rows = group // n_ctx
    low, f32 = jnp.bfloat16, jnp.float32
    lags = lags or list(range(n_low + 4))
    low_shapes = [
        pltpu.VMEM((held, n_dp >> (level + 1), group, WIDE), low) for level in range(n_low)
    ]
    half = group // 2
    kinds = n_low + 4 + n_ctx - 1
    more_in, more_out, more_shape, more_scratch = carry_specs(state[0]) if carry else ([], [], [], [])
    return pl.pallas_call(
        partial(scatter_kernel, n_dp, n_ctx, plan, lags, pieces, len(ys), len(out_shapes), carry),
        out_shape=[jax.ShapeDtypeStruct(shape, f32) for shape in out_shapes] + more_shape,
        in_specs=[pl.BlockSpec(memory_space=pl.ANY)] * (len(xs) + len(ys)) + more_in,
        out_specs=[pl.BlockSpec(memory_space=pltpu.HBM)] * len(out_shapes) + more_out,
        scratch_shapes=[
            pltpu.VMEM((sum(max(1, n) for n in pieces), n_dp, group, tokens), low),
            pltpu.VMEM((held, tokens, WIDE), low),
            *low_shapes,
            *low_shapes,
            pltpu.VMEM((held, group, WIDE), low),
            pltpu.VMEM((held, half, WIDE), low),
            pltpu.VMEM((held, half, WIDE), low),
            pltpu.VMEM((held, group, WIDE), low),
            pltpu.VMEM((held, group, WIDE), low),
            pltpu.VMEM((held, group, WIDE), low),
            pltpu.VMEM((held, group, WIDE), low),
            pltpu.VMEM((held, n_ctx, rows, WIDE), low),
            pltpu.VMEM((held, n_ctx - 1, rows, WIDE), low),
            pltpu.VMEM((held, rows, WIDE), f32),
            pltpu.SemaphoreType.DMA((len(xs),)),
            pltpu.SemaphoreType.DMA((held,)),
            pltpu.SemaphoreType.DMA((held,)),
            pltpu.SemaphoreType.DMA((held, kinds)),
            pltpu.SemaphoreType.DMA((held, kinds)),
            pltpu.SemaphoreType.REGULAR((n_low + 2 + n_ctx - 1,)),
            *more_scratch,
            pltpu.VMEM((pieces.count(0), tokens, n_dp * group), low),
        ],
        compiler_params=pltpu.CompilerParams(
            collective_id=cid, has_side_effects=True, vmem_limit_bytes=56 * 2**20
        ),
        name="scatter_sums",
    )(*[x for x, _ in xs], *ys, *state)


def passed_along(value, axis, steps):
    count = lax.axis_size(axis)
    leading, last = (max(0, -steps), min(count, count - steps))
    return lax.ppermute(value, axis, [(source, source + steps) for source in range(leading, last)])


TERMS = 256
SENT = 160
PER = 4


def feature_tables():
    first = np.zeros((FEAT, TERMS), np.float32)
    second = np.zeros((FEAT, TERMS), np.float32)
    base = np.zeros((8, TERMS), np.float32)
    base[0, 0] = base[1, 0] = base[2, 0] = 1.0
    column = 1
    for f in range(FEAT):
        first[f, column] = base[1, column] = 1.0
        base[2, column] = 1.0 / math.sqrt(FEAT)
        column += 1
    for f in range(FEAT):
        for g in range(f, FEAT):
            first[f, column] = second[g, column] = 1.0
            base[2, column] = (0.5 if f == g else 1.0) / FEAT
            column += 1
    tile = np.stack([np.tile(first, (HEADS, 1)), np.tile(second, (HEADS, 1))])
    return jnp.asarray(tile, jnp.bfloat16), jnp.asarray(base)


def dot_nn(a, b):
    return jnp.dot(a, b, preferred_element_type=jnp.float32)


def dot_nt(a, b):
    return lax.dot_general(a, b, (((1,), (1,)), ((), ())), preferred_element_type=jnp.float32)


def dot_tn(a, b):
    return lax.dot_general(a, b, (((0,), (0,)), ((), ())), preferred_element_type=jnp.float32)


def lanes_of(shape, size):
    return lax.broadcasted_iota(jnp.int32, shape, len(shape) - 1) // size


def only(mask, value):
    return jnp.where(mask, value, jnp.zeros_like(value))


def pairs_of(step):
    return [(step * PER + n, slice(128 * n, 128 * (n + 1))) for n in range(PER)]


def twice(value):
    return jnp.concatenate([value, value], axis=0)


def features_apart(value, pair):
    head = lanes_of(value.shape, FEAT)
    return jnp.concatenate([only(head == 2 * pair, value), only(head == 2 * pair + 1, value)], axis=0)


def features_joined(value, pair):
    rows = value.shape[0] // 2
    head = lanes_of((rows, value.shape[1]), FEAT)
    return only(head == 2 * pair, value[:rows]) + only(head == 2 * pair + 1, value[rows:])


def heads_apart(value):
    lane = lanes_of(value.shape, 64)
    return jnp.concatenate([only(lane == 0, value), only(lane == 1, value)], axis=0)


def heads_joined(value):
    rows = value.shape[0] // 2
    return jnp.where(lanes_of((rows, value.shape[1]), 64) == 0, value[:rows], value[rows:])


def at_head(value, pair):
    rows = value.shape[0] // 2
    lane = lanes_of((rows, 128), 1)
    return jnp.concatenate(
        [
            only(lane == 2 * pair, jnp.broadcast_to(value[:rows], (rows, 128))),
            only(lane == 2 * pair + 1, jnp.broadcast_to(value[rows:], (rows, 128))),
        ],
        axis=0,
    )


def factors(all_rows, tables, base):
    one = [dot_nn(rows, tables[0]) + base[0:1] for rows in all_rows]
    two = [dot_nn(rows, tables[1]) + base[1:2] for rows in all_rows]
    return one, two


def states_kernel(key_ref, value_ref, last_ref, table_ref, base_ref, state_ref):
    step = pl.program_id(1)
    low, f32 = jnp.bfloat16, jnp.float32
    keys, last = key_ref[0], last_ref[0]
    rows = keys.shape[0]
    lane = lanes_of((SENT, 128), 1)
    totals = state_ref[0, HEADS // 2]
    totals = jnp.where(step == 0, jnp.zeros_like(totals), totals)
    pairs = pairs_of(step)
    held = [
        jnp.concatenate([(value_ref[0, :, here].astype(f32) * last).astype(low), last.astype(low)], axis=1)
        for _, here in pairs
    ]
    ones, twos = factors([features_apart(keys, pair) for pair, _ in pairs], table_ref, base_ref)
    terms = [(one * two).astype(low) for one, two in zip(ones, twos)]
    first = [dot_tn(t[:rows], h)[:SENT] for t, h in zip(terms, held)]
    second = [dot_tn(t[rows:], h)[:SENT] for t, h in zip(terms, held)]
    for (pair, _), one, two in zip(pairs, first, second):
        state_ref[0, pair] = jnp.where(lane < 64, one[:, :128], two[:, :128]).astype(low)
        totals = jnp.where(lane == 2 * pair, one[:, 128:].astype(low), totals)
        totals = jnp.where(lane == 2 * pair + 1, two[:, 128:].astype(low), totals)
    state_ref[0, HEADS // 2] = totals


def attend_kernel(
    query_ref, key_ref, value_ref, state_ref, mask_ref, carried_ref, table_ref, base_ref, out_ref, den_ref
):
    step = pl.program_id(1)
    low, f32 = jnp.bfloat16, jnp.float32
    queries, keys = query_ref[0], key_ref[0]
    mask, carried = twice(mask_ref[0]), twice(carried_ref[0][:, :1])
    scale = base_ref[2:3] * carried
    totals = state_ref[0, HEADS // 2]
    inv_root = 1.0 / math.sqrt(FEAT)
    pairs = pairs_of(step)
    values = [value_ref[0, :, here] for _, here in pairs]
    held = [jnp.concatenate([v, jnp.ones_like(v)], axis=1) for v in values]
    states = [jnp.concatenate([state_ref[0, pair], totals], axis=1) for pair, _ in pairs]
    own = [features_apart(queries, pair) for pair, _ in pairs]
    slopes = [dot_nt(o * inv_root, keys) + 1.0 for o in own]
    ones, twos = factors(own, table_ref, base_ref)
    weights = [((0.5 * slope * slope + 0.5) * mask).astype(low) for slope in slopes]
    terms = [(one * two * scale).astype(low) for one, two in zip(ones, twos)]
    near = [dot_nn(w, h) for w, h in zip(weights, held)]
    far = [dot_nn(t, s) for t, s in zip(terms, states)]
    picks = [at_head(jnp.ones((2 * queries.shape[0], 1), f32), pair) for pair, _ in pairs]
    dens = [
        n[:, 128:] + jnp.sum(f[:, 128:] * pick, axis=1, keepdims=True) for n, f, pick in zip(near, far, picks)
    ]
    for (_, here), n, f, den in zip(pairs, near, far, dens):
        out_ref[0, :, here] = heads_joined((n[:, :128] + f[:, :128]) / den).astype(low)
        den_ref[0, :, here] = heads_joined(den)


def attend_back_kernel(
    query_ref, key_ref, value_ref, state_ref, mask_ref, carried_ref, table_ref, base_ref, grad_ref, out_ref,
    den_ref, dquery_ref, dkey_ref, dvalue_ref, dstate_ref,
):
    step = pl.program_id(1)
    low, f32 = jnp.bfloat16, jnp.float32
    queries, keys = query_ref[0], key_ref[0]
    mask, carried = twice(mask_ref[0]), twice(carried_ref[0][:, :1])
    scale = base_ref[2:3] * carried
    totals = state_ref[0, HEADS // 2]
    inv_root = 1.0 / math.sqrt(FEAT)
    keys_small = keys * inv_root
    dtotals = dstate_ref[0, HEADS // 2].astype(f32)
    dtotals = jnp.where(step == 0, jnp.zeros_like(dtotals), dtotals)
    pairs = pairs_of(step)
    values = [value_ref[0, :, here] for _, here in pairs]
    states = [jnp.concatenate([state_ref[0, pair], totals], axis=1) for pair, _ in pairs]
    dnums = [grad_ref[0, :, here] / den_ref[0, :, here] for _, here in pairs]
    inners = [d * out_ref[0, :, here].astype(f32) for d, (_, here) in zip(dnums, pairs)]
    ddens = [-jnp.sum(heads_apart(inner), axis=1, keepdims=True) for inner in inners]
    dnums = [heads_apart(d).astype(low) for d in dnums]
    both = [
        jnp.concatenate([dnum, at_head(dden, pair).astype(low)], axis=1)
        for dnum, dden, (pair, _) in zip(dnums, ddens, pairs)
    ]
    own = [features_apart(queries, pair) for pair, _ in pairs]
    own_small = [o * inv_root for o in own]
    slopes = [dot_nt(o, keys) + 1.0 for o in own_small]
    dtaylors = [dot_nt(dnum, v) + dden for dnum, v, dden in zip(dnums, values, ddens)]
    ones, twos = factors(own, table_ref, base_ref)
    dterms = [dot_nt(b, s) * scale for b, s in zip(both, states)]
    weights = [((0.5 * slope * slope + 0.5) * mask).astype(low) for slope in slopes]
    dscores = [(d * (slope * mask)).astype(low) for d, slope in zip(dtaylors, slopes)]
    terms = [(one * two * scale).astype(low) for one, two in zip(ones, twos)]
    by_one = [(d * two).astype(low) for d, two in zip(dterms, twos)]
    by_two = [(d * one).astype(low) for d, one in zip(dterms, ones)]
    dvalues = [dot_tn(w, dnum) for w, dnum in zip(weights, dnums)]
    dkeys = [dot_tn(d, o) for d, o in zip(dscores, own_small)]
    parts = [dot_tn(t, b)[:SENT] for t, b in zip(terms, both)]
    through = [
        dot_nn(d, keys_small) + dot_nt(a, table_ref[0]) + dot_nt(b, table_ref[1])
        for d, a, b in zip(dscores, by_one, by_two)
    ]
    for (pair, here), dvalue, part in zip(pairs, dvalues, parts):
        dvalue_ref[0, :, here] = dvalue
        dstate_ref[0, pair] = part[:, :128].astype(low)
    dtotals += sum(part[:, 128:] for part in parts)
    dquery = sum(features_joined(value, pair) for value, (pair, _) in zip(through, pairs))
    dkey = sum(dkeys)
    dstate_ref[0, HEADS // 2] = dtotals.astype(low)

    @pl.when(step == 0)
    def _():
        dquery_ref[0] = dquery
        dkey_ref[0] = dkey

    @pl.when(step != 0)
    def _():
        dquery_ref[0] += dquery
        dkey_ref[0] += dkey


def states_back_kernel(
    key_ref, value_ref, last_ref, table_ref, base_ref, dstate_ref, dkey_in, dvalue_in, dkey_ref, dvalue_ref
):
    step = pl.program_id(1)
    low, f32 = jnp.bfloat16, jnp.float32
    keys, last = key_ref[0], last_ref[0]
    last_twice = twice(last[:, :1])
    dtotals = dstate_ref[0, HEADS // 2]
    pairs = pairs_of(step)
    dstates = [dstate_ref[0, pair] for pair, _ in pairs]
    whole = [jnp.concatenate([dstate, dtotals], axis=1) for dstate in dstates]
    marks = [at_head(jnp.ones((2 * keys.shape[0], 1), f32), pair).astype(low) for pair, _ in pairs]
    both = [
        jnp.concatenate([heads_apart(value_ref[0, :, here]), mark], axis=1)
        for (_, here), mark in zip(pairs, marks)
    ]
    ones, twos = factors([features_apart(keys, pair) for pair, _ in pairs], table_ref, base_ref)
    dterms = [dot_nt(b, w) * last_twice for b, w in zip(both, whole)]
    terms = [(one * two).astype(low) for one, two in zip(ones, twos)]
    by_one = [(d * two).astype(low) for d, two in zip(dterms, twos)]
    by_two = [(d * one).astype(low) for d, one in zip(dterms, ones)]
    dvalues = [dot_nn(t, d) for t, d in zip(terms, dstates)]
    through = [dot_nt(a, table_ref[0]) + dot_nt(b, table_ref[1]) for a, b in zip(by_one, by_two)]
    for (_, here), dvalue in zip(pairs, dvalues):
        dvalue_ref[0, :, here] = dvalue_in[0, :, here] + heads_joined(dvalue) * last
    dkey = sum(features_joined(value, pair) for value, (pair, _) in zip(through, pairs))

    @pl.when(step == 0)
    def _():
        dkey_ref[0] = dkey_in[0] + dkey

    @pl.when(step != 0)
    def _():
        dkey_ref[0] += dkey


def by_pair(kernel, name, ins, outs):
    def spec(kind, shape):
        if kind == "query":
            return pl.BlockSpec((1, shape[1], HEADS * FEAT), lambda m, p: (m, 0, 0))
        if kind == "key":
            return pl.BlockSpec((1, shape[1], HEADS * FEAT), lambda m, p: (m, 0, 1))
        if kind == "pair":
            return pl.BlockSpec((1, shape[1], PER * 128), lambda m, p: (m, 0, p))
        if kind == "micro":
            return pl.BlockSpec((1,) + shape[1:], lambda m, p: (m,) + (0,) * (len(shape) - 1))
        return pl.BlockSpec(shape, lambda m, p: (0,) * len(shape))

    return pl.pallas_call(
        kernel,
        grid=(ins[0][0].shape[0], HEADS // 2 // PER),
        in_specs=[spec(kind, array.shape) for array, kind in ins],
        out_specs=[spec(kind, shape) for shape, _, kind in outs],
        out_shape=[jax.ShapeDtypeStruct(shape, dtype) for shape, dtype, _ in outs],
        compiler_params=pltpu.CompilerParams(vmem_limit_bytes=48 * 2**20),
        name=name,
    )(*[array for array, _ in ins])


def turn_kernel(places, unit, value_ref, out_ref, turned):
    tokens, rows = value_ref.shape
    for first in range(0, rows, 128):
        turned[first : first + 128] = value_ref[:, first : first + 128].T.astype(jnp.float32)
    pieces, n_dp = out_ref.shape[:2]
    n_ctx, shard = places // n_dp, rows // places
    for place in range(places):
        for piece in range(pieces):
            start, count = piece * unit, min(unit, shard - piece * unit)
            value = turned[place * shard + start : place * shard + start + count]
            if count < unit:
                value = jnp.concatenate([value, jnp.zeros((unit - count, tokens), jnp.float32)], axis=0)
            where = place % n_ctx * unit
            out_ref[piece, place // n_ctx, where : where + unit] = value.astype(jnp.bfloat16)


def turned_pieces(value, places, n_dp, unit):
    tokens, rows = value.shape
    pieces = -(-(rows // places) // unit)
    return pl.pallas_call(
        partial(turn_kernel, places, unit),
        out_shape=jax.ShapeDtypeStruct((pieces, n_dp, places // n_dp * unit, tokens), jnp.bfloat16),
        in_specs=[pl.BlockSpec(memory_space=pltpu.VMEM)],
        out_specs=pl.BlockSpec(memory_space=pltpu.VMEM),
        scratch_shapes=[pltpu.VMEM((rows, tokens), jnp.float32)],
        compiler_params=pltpu.CompilerParams(vmem_limit_bytes=48 * 2**20),
        name="turn",
    )(value)


def chunk_plan(products, unit):
    n_dp = lax.axis_size("dp")
    places = n_dp * lax.axis_size("ctx")
    operands, first_laid, plan, shapes, count, taken = [], {}, [], [], 0, 0
    for number, (operand, gradient) in enumerate(products):
        parts = gradient if isinstance(gradient, tuple) else (gradient,)
        columns = sum(part.shape[1] for part in parts)
        places_of = tuple(range(taken, taken + len(parts)))
        taken += len(parts)
        shard = operand.shape[1] // places
        pieces = -(-shard // unit)
        shapes.append((shard, columns))
        if id(operand) not in first_laid:
            first_laid[id(operand)] = count
            count += pieces
            if pieces > 1:
                operands.append((turned_pieces(operand, places, n_dp, unit), pieces))
            else:
                operands.append((operand, 0))
        for piece in range(pieces):
            first = piece * unit
            plan.append(
                (
                    first_laid[id(operand)] + piece,
                    places_of,
                    number,
                    first,
                    min(unit, shard - first),
                    columns // WIDE,
                )
            )
    return operands, plan, shapes


def as_product(small):
    rows, few = small.shape
    high = small.astype(jnp.bfloat16)
    rest = (small - high.astype(jnp.float32)).astype(jnp.bfloat16)

    def product(tokens):
        both = jnp.zeros((tokens, rows), jnp.bfloat16).at[:few].set(high.T).at[few : 2 * few].set(rest.T)
        pick = np.zeros((tokens, WIDE), np.float32)
        pick[:few, :few] = pick[few : 2 * few, :few] = np.eye(few)
        return both, jnp.asarray(pick, jnp.bfloat16)

    return product


def summed_to_owners(products, cid, unit, carry=0, state=()):
    n_dp, n_ctx = lax.axis_size("dp"), lax.axis_size("ctx")
    laid, plan, shapes = chunk_plan(products, unit)
    gradients = []
    for _, gradient in products:
        gradients += gradient if isinstance(gradient, tuple) else (gradient,)
    return scatter_sums(laid, gradients, shapes, plan, n_dp, n_ctx, cid, carry, state)


def chunks_of(shards):
    out = []
    for place, shard in enumerate(shards):
        rows, columns = shard.shape
        unit = max(128, 1408 * 32 // rows // 128 * 128)
        width = -(-(columns // 128) // -(-columns // unit)) * 128
        for first in range(0, columns, width):
            out.append((place, first, min(width, columns - first)))
    return out


def flat(value):
    return value.reshape(-1, value.shape[-1])


def normed(stream, scale_gain):
    return (
        stream * lax.rsqrt(jnp.mean(stream * stream, axis=-1, keepdims=True) + epsilon) * scale_gain
    )


def matmul(operand, weight):
    return jnp.einsum("mtd,de->mte", operand, weight, preferred_element_type=jnp.float32)


def matmul_back(operand, weight):
    return jnp.einsum("mte,de->mtd", operand, weight, preferred_element_type=jnp.float32)


def weight_grad(operand, gradient):
    return jnp.einsum("mtd,mte->de", operand, gradient, preferred_element_type=jnp.float32)


def layout(seq_lengths, tok_count):
    seq_ends = jnp.cumsum(seq_lengths[:, 0, :], axis=-1, dtype=jnp.int32)
    first_pos = lax.axis_index("ctx") * tok_count

    def segment_of(positions):
        return jnp.sum(
            (positions[None, :, None] >= seq_ends[:, None, :]).astype(jnp.int32),
            axis=-1,
            dtype=jnp.int32,
        )

    own_pos = first_pos + jnp.arange(tok_count, dtype=jnp.int32)
    own_seg = segment_of(own_pos)
    before_seg = segment_of(own_pos - 1)

    def in_lanes(flag):
        return jnp.broadcast_to(flag[:, :, None].astype(jnp.float32), flag.shape + (128,))

    starts = (own_seg != before_seg) | (own_pos == 0)[None, :]
    keep = 1.0 - jnp.max(starts.astype(jnp.float32), axis=1)
    tap_masks = []
    for offset in range(CONV):
        source = own_pos - offset
        tap_masks.append(
            ((segment_of(source) == own_seg) & (source >= 0)[None, :]).astype(jnp.float32)
        )
    key_pos = first_pos - BAND + jnp.arange(tok_count + BAND, dtype=jnp.int32)
    key_seg = jnp.where(key_pos >= 0, segment_of(key_pos), -1)
    window_mask = []
    for first in range(0, tok_count, BAND):
        queries, keys = slice(first, first + BAND), slice(first, first + 2 * BAND)
        ahead = own_pos[queries][:, None] - key_pos[keys][None, :]
        same = own_seg[:, queries][:, :, None] == key_seg[:, keys][:, None, :]
        window_mask.append(((ahead >= 0) & (ahead < WINDOW))[None] & same)
    window_mask = jnp.where(jnp.concatenate(window_mask, axis=1), 0.0, masked_fill)
    causal = (own_pos[:, None] >= own_pos[None, :])[None] & (
        own_seg[:, :, None] == own_seg[:, None, :]
    )
    return {
        "valid": (own_pos[None, :] < seq_ends[:, -1:]).astype(jnp.float32),
        "keep": jnp.broadcast_to(keep[:, None, None], keep.shape + (8, 128)),
        "carried": in_lanes((own_seg == before_seg[:, :1]) & (first_pos > 0)),
        "last": in_lanes(own_seg == own_seg[:, -1:]),
        "causal": causal.astype(jnp.float32),
        "taps": jnp.stack(tap_masks),
        "window": window_mask,
    }


def conv_gate(pre_values, rim_rows, tap_weights, tap_masks):
    tok_count = pre_values.shape[1]
    rim_width = rim_rows.shape[1]
    extended = jnp.concatenate([rim_rows, pre_values], axis=1)
    conv_sum = jnp.zeros_like(pre_values)
    for offset in range(rim_width + 1):
        shifted = extended[:, rim_width - offset : rim_width - offset + tok_count, :]
        conv_sum = conv_sum + tap_weights[:, offset] * shifted * tap_masks[offset][:, :, None]
    return conv_sum * jax.nn.silu(pre_values)


def linear_forward(stream, rim_stream, weights, layout_info, gather_more):
    norm_gain, qk_weight, value_weight, tap_weights = weights
    micro_count, tok_count, model_width = stream.shape
    normed_rows, norm_back = jax.vjp(normed, stream, norm_gain.astype(jnp.float32))
    normed_low = normed_rows.astype(jnp.bfloat16)
    qk_rows = matmul(normed_low, qk_weight).astype(jnp.bfloat16)
    pre_values = matmul(normed_low, value_weight)
    rim_normed = normed(rim_stream.astype(jnp.float32), norm_gain.astype(jnp.float32))
    rim_rows = matmul(rim_normed.astype(jnp.bfloat16), value_weight)
    value_rows, conv_back = jax.vjp(
        partial(conv_gate, tap_masks=layout_info["taps"]),
        pre_values,
        rim_rows,
        tap_weights.astype(jnp.float32),
    )
    values = value_rows.astype(jnp.bfloat16)
    tables, base = feature_tables()
    state_shape = (micro_count, HEADS // 2 + 1, SENT, 128)
    (state,) = by_pair(
        states_kernel,
        "states",
        [(qk_rows, "key"), (values, "pair"), (layout_info["last"], "micro"), (tables, "whole"), (base, "whole")],
        [(state_shape, jnp.bfloat16, "micro")],
    )
    *more, state_in = gather_more((state, layout_info["keep"]))
    out_weight = more[0]
    shared = [
        (qk_rows, "query"),
        (qk_rows, "key"),
        (values, "pair"),
        (state_in, "micro"),
        (layout_info["causal"], "micro"),
        (layout_info["carried"], "micro"),
        (tables, "whole"),
        (base, "whole"),
    ]
    attended_low, den = by_pair(
        attend_kernel,
        "linear_attend",
        shared,
        [(values.shape, jnp.bfloat16, "pair"), (values.shape, jnp.float32, "pair")],
    )
    branch = matmul(attended_low, out_weight)
    return (
        stream + branch,
        (norm_back, normed_low, conv_back, shared, attended_low, den),
        more,
    )


def linear_backward(grad_stream, residuals, weights, layout_info, other_gains, sum_others):
    norm_back, normed_low, conv_back, shared, attended_low, den = residuals
    qk_weight, value_weight, out_weight = (weights[1], weights[2], weights[4])
    micro_count, tok_count, model_width = grad_stream.shape
    grad_branch = grad_stream.astype(jnp.bfloat16)
    grad_out = (flat(attended_low), flat(grad_branch))
    grad_attended = matmul_back(grad_branch, out_weight)
    f32, low = jnp.float32, jnp.bfloat16
    feat_shape = (micro_count, tok_count, HEADS * FEAT)
    state_shape = (micro_count, HEADS // 2 + 1, SENT, 128)
    grad_query, grad_key, grad_value, grad_state = by_pair(
        attend_back_kernel,
        "linear_attend_back",
        shared + [(grad_attended, "pair"), (attended_low, "pair"), (den, "pair")],
        [
            (feat_shape, f32, "micro"),
            (feat_shape, f32, "micro"),
            (grad_stream.shape, f32, "pair"),
            (state_shape, low, "micro"),
        ],
    )
    *sums, later = sum_others(grad_out, (grad_state, layout_info["keep"]))
    grad_key, grad_value = by_pair(
        states_back_kernel,
        "states_back",
        [shared[1], shared[2], (layout_info["last"], "micro"), shared[6], shared[7], (later, "micro")]
        + [(grad_key, "micro"), (grad_value, "pair")],
        [(feat_shape, f32, "micro"), (grad_stream.shape, f32, "pair")],
    )
    grad_qk = jnp.concatenate([grad_query, grad_key], axis=-1).astype(low)
    grad_pre, grad_rim, grad_taps = conv_back(grad_value)
    returned = passed_along(grad_rim, "ctx", -1)
    grad_pre = grad_pre.at[:, tok_count - CONV + 1 :, :].add(returned)
    grad_pre_low = grad_pre.astype(jnp.bfloat16)
    grad_normed = matmul_back(grad_qk, qk_weight) + matmul_back(grad_pre_low, value_weight)
    grad_input, grad_gain = norm_back(grad_normed)
    small = jnp.concatenate([grad_gain[:, None], other_gains, grad_taps], axis=1)
    operand = flat(normed_low)
    own = summed_to_owners(
        [
            as_product(small)(operand.shape[0]),
            (operand, flat(grad_qk)),
            (operand, flat(grad_pre_low)),
        ],
        3,
        model_width // (lax.axis_size("dp") * lax.axis_size("ctx")),
    )
    return (grad_stream + grad_input, own, sums)


BAND = 128
RIM = 64
WIDE_PER = 8


def band_probabilities(queries, keys, bias):
    scores = [dot_nt(q, k) + bias for q, k in zip(queries, keys)]
    tops = [jnp.max(score, axis=1, keepdims=True) for score in scores]
    powers = [jnp.exp(score - top) for score, top in zip(scores, tops)]
    totals = [1.0 / jnp.sum(power, axis=1, keepdims=True) for power in powers]
    return [power * total for power, total in zip(powers, totals)]


def band_attend(queries, keys, values, bias):
    low = jnp.bfloat16
    chances = band_probabilities([heads_apart(q * 0.125) for q in queries], keys, twice(bias))
    outs = [dot_nn(chance.astype(low), v) for chance, v in zip(chances, values)]
    return [heads_joined(out).astype(low) for out in outs]


def band_back(queries, grads, keys, values, bias):
    low = jnp.bfloat16
    queries = [heads_apart(q * 0.125) for q in queries]
    grads = [heads_apart(g) for g in grads]
    dchances = [dot_nt(g, v) for g, v in zip(grads, values)]
    chances = band_probabilities(queries, keys, twice(bias))
    inners = [jnp.sum(d * c, axis=1, keepdims=True) for d, c in zip(dchances, chances)]
    dscores = [(c * (d - inner)).astype(low) for c, d, inner in zip(chances, dchances, inners)]
    dqueries = [dot_nn(d, k) for d, k in zip(dscores, keys)]
    dkeys = [dot_tn(d, q) for d, q in zip(dscores, queries)]
    dvalues = [dot_tn(c.astype(low), g) for c, g in zip(chances, grads)]
    return [(heads_joined(d) * 0.125).astype(low) for d in dqueries], dkeys, dvalues


LANES = [slice(128 * n, 128 * (n + 1)) for n in range(WIDE_PER)]


def by_pairs(ref, rows):
    return [ref[0, rows, here] for here in LANES]


def with_rim(own_ref, rim_ref):
    out = []
    for own, rim in zip(by_pairs(own_ref, slice(None)), by_pairs(rim_ref, slice(None))):
        out.append(jnp.concatenate([jnp.zeros((BAND - RIM, 128), own.dtype), rim, own], axis=0))
    return out


def first_band_kernel(query_ref, key_ref, value_ref, rim_key_ref, rim_value_ref, bias_ref, out_ref):
    keys, values = with_rim(key_ref, rim_key_ref), with_rim(value_ref, rim_value_ref)
    outs = band_attend(by_pairs(query_ref, slice(None)), keys, values, bias_ref[0])
    for here, out in zip(LANES, outs):
        out_ref[0, :, here] = out


def later_bands_kernel(query_ref, key_ref, value_ref, bias_ref, out_ref):
    for first in range(BAND, query_ref.shape[1], BAND):
        rows, near = slice(first, first + BAND), slice(first - BAND, first + BAND)
        outs = band_attend(
            by_pairs(query_ref, rows), by_pairs(key_ref, near), by_pairs(value_ref, near), bias_ref[0, rows]
        )
        for here, out in zip(LANES, outs):
            out_ref[0, first - BAND : first, here] = out


def first_band_back_kernel(
    query_ref, key_ref, value_ref, rim_key_ref, rim_value_ref, bias_ref, grad_ref, dquery_ref, dkey_ref,
    dvalue_ref, drim_key_ref, drim_value_ref,
):
    keys, values = with_rim(key_ref, rim_key_ref), with_rim(value_ref, rim_value_ref)
    whole = slice(None)
    all_back = band_back(by_pairs(query_ref, whole), by_pairs(grad_ref, whole), keys, values, bias_ref[0])
    for here, dquery, dkey, dvalue in zip(LANES, *all_back):
        dquery_ref[0, :, here] = dquery
        dkey_ref[0, :, here] = dkey[BAND:]
        dvalue_ref[0, :, here] = dvalue[BAND:]
        drim_key_ref[0, :, here] = dkey[BAND - RIM : BAND].astype(jnp.bfloat16)
        drim_value_ref[0, :, here] = dvalue[BAND - RIM : BAND].astype(jnp.bfloat16)


def later_bands_back_kernel(
    query_ref, key_ref, value_ref, bias_ref, grad_ref, first_dkey_ref, first_dvalue_ref, dquery_ref, dkey_ref,
    dvalue_ref,
):
    dkey_ref[0, :BAND] = first_dkey_ref[0]
    dvalue_ref[0, :BAND] = first_dvalue_ref[0]
    for first in range(BAND, query_ref.shape[1], BAND):
        rows, before, near = (
            slice(first, first + BAND),
            slice(first - BAND, first),
            slice(first - BAND, first + BAND),
        )
        all_back = band_back(
            by_pairs(query_ref, rows),
            by_pairs(grad_ref, rows),
            by_pairs(key_ref, near),
            by_pairs(value_ref, near),
            bias_ref[0, rows],
        )
        for here, dquery, dkey, dvalue in zip(LANES, *all_back):
            dquery_ref[0, before, here] = dquery
            dkey_ref[0, before, here] += dkey[:BAND]
            dvalue_ref[0, before, here] += dvalue[:BAND]
            dkey_ref[0, rows, here] = dkey[BAND:]
            dvalue_ref[0, rows, here] = dvalue[BAND:]


def by_window(kernel, name, ins, outs):
    micro, steps = ins[0][0].shape[0], HEADS // 2 // WIDE_PER

    def spec(rows, place, width):
        if place is None:
            return pl.BlockSpec((1, rows, width), lambda m, p: (m, 0, 0))
        return pl.BlockSpec((1, rows, WIDE_PER * 128), lambda m, p: (m, 0, p + place * steps))

    return pl.pallas_call(
        kernel,
        grid=(micro, steps),
        in_specs=[spec(rows, place, array.shape[2]) for array, rows, place in ins],
        out_specs=[spec(rows, 0, 0) for rows, _ in outs],
        out_shape=[jax.ShapeDtypeStruct((micro, rows, HEADS * 64), dtype) for rows, dtype in outs],
        compiler_params=pltpu.CompilerParams(vmem_limit_bytes=48 * 2**20),
        name=name,
    )(*[array for array, _, _ in ins])


def window_forward(stream, weights, layout_info):
    norm_gain, qkv_weight, out_weight = weights
    micro_count, tok_count, model_width = stream.shape
    normed_rows, norm_back = jax.vjp(normed, stream, norm_gain.astype(jnp.float32))
    normed_low = normed_rows.astype(jnp.bfloat16)
    qkv_rows = matmul(normed_low, qkv_weight).astype(jnp.bfloat16)
    rim_rows = passed_along(qkv_rows[:, tok_count - RIM :, model_width:], "ctx", 1)
    mask = layout_info["window"]
    parts = []
    if tok_count > BAND:
        parts = by_window(
            later_bands_kernel,
            "window_later",
            [(qkv_rows, tok_count, 0), (qkv_rows, tok_count, 1), (qkv_rows, tok_count, 2), (mask, tok_count, None)],
            [(tok_count - BAND, jnp.bfloat16)],
        )
        rim_rows, parts = lax.optimization_barrier((rim_rows, parts))
    (start,) = by_window(
        first_band_kernel,
        "window_first",
        [(qkv_rows, BAND, 0), (qkv_rows, BAND, 1), (qkv_rows, BAND, 2), (rim_rows, RIM, 0), (rim_rows, RIM, 1)]
        + [(mask, BAND, None)],
        [(BAND, jnp.bfloat16)],
    )
    attended = jnp.concatenate([start] + list(parts), axis=1)
    branch = matmul(attended, out_weight)
    return (stream + branch, (norm_back, normed_low, qkv_rows, rim_rows, attended))


def window_backward(grad_stream, residuals, weights, layout_info):
    norm_back, normed_low, qkv_rows, rim_rows, attended = residuals
    qkv_weight, out_weight = (weights[1], weights[2])
    micro_count, tok_count, model_width = grad_stream.shape
    f32, low = jnp.float32, jnp.bfloat16
    grad_branch = grad_stream.astype(low)
    grad_out = (flat(attended), flat(grad_branch))
    grad_attended = matmul_back(grad_branch, out_weight).astype(low)
    mask = layout_info["window"]
    grad_query, grad_key, grad_value, rim_key, rim_value = by_window(
        first_band_back_kernel,
        "window_first_back",
        [(qkv_rows, BAND, 0), (qkv_rows, BAND, 1), (qkv_rows, BAND, 2), (rim_rows, RIM, 0), (rim_rows, RIM, 1)]
        + [(mask, BAND, None), (grad_attended, BAND, 0)],
        [(BAND, low), (BAND, f32), (BAND, f32), (RIM, low), (RIM, low)],
    )
    returned = passed_along(jnp.concatenate([rim_key, rim_value], axis=-1), "ctx", -1)
    if tok_count > BAND:
        more_query, grad_key, grad_value = by_window(
            later_bands_back_kernel,
            "window_later_back",
            [(qkv_rows, tok_count, 0), (qkv_rows, tok_count, 1), (qkv_rows, tok_count, 2), (mask, tok_count, None)]
            + [(grad_attended, tok_count, 0), (grad_key, BAND, 0), (grad_value, BAND, 0)],
            [(tok_count - BAND, low), (tok_count, f32), (tok_count, f32)],
        )
        grad_query = jnp.concatenate([grad_query, more_query], axis=1)
        returned, grad_key = lax.optimization_barrier((returned, grad_key))
    returned = returned.astype(f32)
    returned = jnp.pad(returned, ((0, 0), (tok_count - RIM, 0), (0, 0)))
    grad_qkv = jnp.concatenate(
        [
            grad_query,
            (grad_key + returned[..., :model_width]).astype(low),
            (grad_value + returned[..., model_width:]).astype(low),
        ],
        axis=-1,
    )
    grad_qkv_weight = (flat(normed_low), flat(grad_qkv))
    grad_input, grad_gain = norm_back(lax.optimization_barrier(matmul_back(grad_qkv, qkv_weight)))
    return (grad_stream + grad_input, (grad_gain, grad_qkv_weight, grad_out))


def ffn_forward(stream, weights):
    norm_gain, gate_up, down_weight = weights
    hidden_width = down_weight.shape[0]
    normed_rows, norm_back = jax.vjp(normed, stream, norm_gain.astype(jnp.float32))
    normed_low = normed_rows.astype(jnp.bfloat16)
    projected = matmul(normed_low, gate_up)
    hidden = (jax.nn.silu(projected[..., :hidden_width]) * projected[..., hidden_width:]).astype(
        jnp.bfloat16
    )
    hidden, projected = lax.optimization_barrier((hidden, projected.astype(jnp.bfloat16)))
    branch = matmul(hidden, down_weight)
    return (stream + branch, (norm_back, normed_low, projected, hidden))


def ffn_backward(grad_stream, residuals, weights):
    norm_back, normed_low, projected, hidden = residuals
    gate_up, down_weight = (weights[1], weights[2])
    hidden_width = down_weight.shape[0]
    grad_branch = grad_stream.astype(jnp.bfloat16)
    grad_down = (flat(hidden), flat(grad_branch))
    grad_hidden = matmul_back(grad_branch, down_weight)
    gate_part = projected[..., :hidden_width].astype(jnp.float32)
    up_part = projected[..., hidden_width:].astype(jnp.float32)
    sigmoid_gate = jax.nn.sigmoid(gate_part)
    grad_gate = grad_hidden * up_part * sigmoid_gate * (1.0 + gate_part * (1.0 - sigmoid_gate))
    grad_up = grad_hidden * gate_part * sigmoid_gate
    grad_projected = jnp.concatenate([grad_gate, grad_up], axis=-1).astype(jnp.bfloat16)
    low = jnp.bfloat16
    grad_gate_up = (flat(normed_low), (flat(grad_gate.astype(low)), flat(grad_up.astype(low))))
    grad_input, grad_gain = norm_back(lax.optimization_barrier(matmul_back(grad_projected, gate_up)))
    return (grad_stream + grad_input, (grad_gain, grad_gate_up, grad_down))


def body(
    tokens_in,
    seq_lengths,
    norm_linear,
    proj_qk,
    proj_values,
    conv_taps,
    out_linear,
    norm_ffn_one,
    gate_up_one,
    down_one,
    norm_window,
    proj_qkv,
    out_window,
    norm_ffn_two,
    gate_up_two,
    down_two,
    cotangent,
):
    tok_count = tokens_in.shape[2]
    layout_info = layout(seq_lengths, tok_count)
    stream = tokens_in[:, 0].astype(jnp.float32)
    small = jnp.concatenate(
        [
            norm_linear[:, None],
            norm_ffn_one[:, None],
            norm_window[:, None],
            norm_ffn_two[:, None],
            conv_taps,
            jnp.zeros((conv_taps.shape[0], 121), jnp.bfloat16),
        ],
        axis=1,
    )
    n_dp, n_ctx = lax.axis_size("dp"), lax.axis_size("ctx")
    first_shards = [small, proj_qk, proj_values]
    rim_stream = passed_along(tokens_in[:, 0, tok_count - CONV + 1 :], "ctx", 1)
    small, w_qk, w_values = gather_all(first_shards, n_dp, n_ctx, chunks_of(first_shards), cid=0)
    small, rim_stream = lax.optimization_barrier((small, rim_stream))

    def gather_more(state):
        shards = [out_linear, gate_up_one, down_one, proj_qkv, out_window, down_two]
        return gather_all(shards, n_dp, n_ctx, chunks_of(shards), cid=2, carry=1, state=state)

    middle, saved_linear, more = linear_forward(
        stream, rim_stream, (small[:, 0], w_qk, w_values, small[:, 4:7]), layout_info, gather_more
    )
    w_out_linear, w_gu_one, w_dn_one, w_qkv, w_out_window, w_dn_two = more
    w_gu_two = lax.all_gather(gate_up_two, ("dp", "ctx"), axis=0, tiled=True)
    layer_one = (small[:, 0], w_qk, w_values, small[:, 4:7], w_out_linear, small[:, 1], w_gu_one, w_dn_one)
    layer_two = (small[:, 2], w_qkv, w_out_window, small[:, 3], w_gu_two, w_dn_two)
    first_out, saved_ffn_one = ffn_forward(middle, layer_one[5:])
    second_mid, saved_window = window_forward(first_out, layer_two[:3], layout_info)
    closing, saved_ffn_two = ffn_forward(second_mid, layer_two[3:])
    valid_rows = layout_info["valid"][:, :, None]
    output = (closing * valid_rows).astype(jnp.bfloat16)[:, None]
    grad_stream = cotangent[:, 0].astype(jnp.float32) * valid_rows
    grad_stream, grads_ffn_two = ffn_backward(grad_stream, saved_ffn_two, layer_two[3:])
    operand, gradient = grads_ffn_two[1]
    gradient = jnp.concatenate(gradient, axis=-1)
    partial_sums = jnp.einsum("tr,te->re", operand, gradient, preferred_element_type=jnp.float32)
    partial_sums = partial_sums.astype(jnp.bfloat16)
    for axis in ("dp", "ctx"):
        partial_sums = lax.psum_scatter(partial_sums, axis, scatter_dimension=0, tiled=True)
    sum_gate_up_two = partial_sums.astype(jnp.float32)
    grad_stream, grads_window = window_backward(
        grad_stream, saved_window, layer_two[:3], layout_info
    )
    grad_stream, grads_ffn_one = ffn_backward(grad_stream, saved_ffn_one, layer_one[5:])
    other_gains = jnp.stack([grads_ffn_one[0], grads_window[0], grads_ffn_two[0]], axis=1)

    def sum_others(of_out, state):
        products = [
            of_out,
            grads_ffn_one[1],
            grads_ffn_one[2],
            grads_window[1],
            grads_window[2],
            grads_ffn_two[2],
        ]
        return summed_to_owners(products, 1, out_linear.shape[0], -1, state)

    grad_stream, own_sums, sums = linear_backward(
        grad_stream, saved_linear, layer_one[:5], layout_info, other_gains, sum_others
    )
    small, grad_qk, grad_values = own_sums
    tokens_grad = grad_stream.astype(jnp.bfloat16)[:, None]
    return (
        output,
        tokens_grad,
        small[:, 0],
        grad_qk,
        grad_values,
        small[:, 4:7],
        sums[0],
        small[:, 1],
        sums[1],
        sums[2],
        small[:, 2],
        sums[3],
        sums[4],
        small[:, 3],
        sum_gate_up_two,
        sums[5],
    )


def solution(mesh):
    placed = (
        P(None, "dp", "ctx", None),
        P(None, "dp", None),
        P(("dp", "ctx")),
        P(("dp", "ctx"), None),
        P(("dp", "ctx"), None),
        P(("dp", "ctx"), None),
        P(("dp", "ctx"), None),
        P(("dp", "ctx")),
        P(("dp", "ctx"), None),
        P(("dp", "ctx"), None),
        P(("dp", "ctx")),
        P(("dp", "ctx"), None),
        P(("dp", "ctx"), None),
        P(("dp", "ctx")),
        P(("dp", "ctx"), None),
        P(("dp", "ctx"), None),
        P(None, "dp", "ctx", None),
    )
    return jax.shard_map(
        body,
        mesh=mesh,
        in_specs=placed,
        out_specs=(
            P(None, "dp", "ctx", None),
            P(None, "dp", "ctx", None),
            P(("dp", "ctx")),
            P(("dp", "ctx"), None),
            P(("dp", "ctx"), None),
            P(("dp", "ctx"), None),
            P(("dp", "ctx"), None),
            P(("dp", "ctx")),
            P(("dp", "ctx"), None),
            P(("dp", "ctx"), None),
            P(("dp", "ctx")),
            P(("dp", "ctx"), None),
            P(("dp", "ctx"), None),
            P(("dp", "ctx")),
            P(("dp", "ctx"), None),
            P(("dp", "ctx"), None),
        ),
        check_vma=False,
    )
```
